256 devices in a mesh: seq: 32 (over z, x), head: 8 (over y, core).
Axes of the slice: x: 4, y: 4, z: 8, core: 2. Of those that a mesh axis runs over, the one named last changes fastest.
Arguments:
- queries: bfloat16 [6144, 8192], P('seq', 'head'), may hold values from -20 to 20
- image_kv: bfloat16 [64, 256, 2, 1024], P('seq', 'head'), may hold values from -6 to 6
- gate_logit: float32 [64], P('head'), may hold values from 0.3 to 1.5
- d_gated: bfloat16 [6144, 8192], P('seq', 'head'), may hold values from -6 to 6
- media_list: int32 [32, 16], replicated, may hold values from 0 to 63, as said below
- media_count: int32 [32], replicated, may hold values from 12 to 16, as said below
- image_slot: int32 [64], replicated, may hold values from 0 to 63, as said below
Outputs:
- gated: bfloat16 [6144, 8192], P('seq', 'head')
- d_queries: bfloat16 [6144, 8192], P('seq', 'head')
- d_image_kv: bfloat16 [64, 256, 2, 1024], P('seq', 'head')
The draws below stay inside these ranges and needn't reach their ends.
Inputs may be any that keep to these rules, and one draw needn't show every extreme that they name: `media_list`: the 16 images of one segment's list lie in slots of 16 different owners (image_slot // 2 differ); ids in a row are distinct. `media_count`: the last segment attends its whole list. `image_slot`: A permutation of the slots.
All inputs are finite; a program needn't handle non-finite values.
Results may differ from the reference program's by a relative error of at most 0.022.
Values may be sent and summed in bfloat16 or wider, within the bound.
A program may use at most 128 MiB of HBM per device.

```python
import jax
import jax.numpy as jnp
from jax import lax

HD = 128
GROUP = 8
VT = 256
IMG_DEV = 2
TOK_DEV = 192
HEADS_KV = 8
MEDIA = 16
SEGMENTS = 32
TOKENS = 6144
IMAGES = 64


def shared_slots(key):
    slot_key = jax.random.fold_in(key, 102)
    return jax.random.permutation(slot_key, IMAGES).astype(jnp.int32)


def draw_queries(key, part):
    key = jax.random.fold_in(key, 11)
    width = HEADS_KV * GROUP * HD
    values = jnp.clip(2.5 * jax.random.normal(key, (TOKENS, width), jnp.float32), -20.0, 20.0)
    return values.astype(jnp.bfloat16)


def draw_image_kv(key, part):
    key = jax.random.fold_in(key, 12)
    shape = (IMAGES, VT, 2, HEADS_KV * HD)
    values = jnp.clip(jax.random.normal(key, shape, jnp.float32), -6.0, 6.0)
    return values.astype(jnp.bfloat16)


def draw_image_slot(key, part):
    slots = shared_slots(key)
    return slots


def draw_media_list(key, part):
    slots = shared_slots(key)
    key = jax.random.fold_in(key, 14)
    inverse = jnp.zeros((IMAGES,), jnp.int32).at[slots].set(jnp.arange(IMAGES, dtype=jnp.int32))
    owner_total = IMAGES // IMG_DEV
    row_keys = jax.random.split(key, SEGMENTS)
    owners = jax.vmap(lambda row_key: jax.random.permutation(row_key, owner_total)[:MEDIA])(row_keys).astype(jnp.int32)
    picks = jax.random.randint(jax.random.fold_in(key, 1), (SEGMENTS, MEDIA), 0, IMG_DEV).astype(jnp.int32)
    return jnp.take(inverse, owners * IMG_DEV + picks).astype(jnp.int32)


def draw_media_count(key, part):
    key = jax.random.fold_in(key, 15)
    lowest = MEDIA - MEDIA // 4
    counts = jax.random.randint(key, (SEGMENTS,), lowest, MEDIA + 1).astype(jnp.int32)
    return counts.at[SEGMENTS - 1].set(MEDIA)


def level_of(key, shape, shards, least, high):
    level = 1.0
    for dim, shards_of in shards:
        steps = jax.random.uniform(jax.random.fold_in(jax.random.fold_in(key, 6), dim), (shards_of,), jnp.float32, least / len(shards), high / len(shards))
        level = level * jnp.repeat(jnp.exp(steps), shape[dim] // shards_of).reshape((-1,) + (1,) * (len(shape) - 1 - dim))
    return level


def normal_values(own_key, shape, scale, most, shards=(), kind=jnp.bfloat16):
    gain = level_of(own_key, shape, shards, -0.22, 0.18) if shards else 1.0
    result = jax.random.normal(own_key, shape, jnp.float32) * scale * gain
    return jnp.minimum(jnp.maximum(result, -most), most).astype(kind)


def setup_inputs(seed: int = 0) -> dict:
    seeds = jax.random.split(jax.random.key(seed), 8)
    return {
        "queries": draw_queries(jax.random.fold_in(seeds[7], 71), 0),
        "image_kv": draw_image_kv(jax.random.fold_in(seeds[7], 71), 0),
        "gate_logit": jnp.clip(0.3 + 1.2 * jax.random.uniform(seeds[2], (HEADS_KV * GROUP,), jnp.float32) ** level_of(seeds[2], (HEADS_KV * GROUP,), ((0, 8),), -0.2, 0.2), 0.3, 1.5),
        "d_gated": normal_values(seeds[3], (TOKENS, HEADS_KV * GROUP * HD), 1.0, 6.0, ((0, 32), (1, 8))),
        "media_list": draw_media_list(jax.random.fold_in(seeds[7], 71), 0),
        "media_count": draw_media_count(jax.random.fold_in(seeds[7], 71), 0),
        "image_slot": draw_image_slot(jax.random.fold_in(seeds[7], 71), 0),
    }


def one_head(operands):
    query_rows, grad_rows, kv_rows, gate_tanh, live_keys = operands
    inv_root = HD ** -0.5
    key_rows = kv_rows[:, 0, :].astype(jnp.float32)
    value_rows = kv_rows[:, 1, :].astype(jnp.float32)
    query_wide = query_rows.astype(jnp.float32)
    scores = jnp.einsum('tgd,kd->tgk', query_wide, key_rows) * inv_root
    masked = jnp.where(live_keys[None, None, :], scores, -jnp.inf)
    row_top = jnp.max(masked, axis=-1)
    weights = jnp.where(live_keys[None, None, :], jnp.exp(scores - row_top[..., None]), 0.0)
    row_total = jnp.sum(weights, axis=-1)
    probs = weights / row_total[..., None]
    probs_low = probs.astype(jnp.bfloat16)
    attended = jnp.einsum('tgk,kd->tgd', probs_low.astype(jnp.float32), value_rows)
    gate_wide = gate_tanh[None, :, None]
    gated = (gate_wide * attended).astype(jnp.bfloat16)
    d_attended = (gate_wide * grad_rows.astype(jnp.float32)).astype(jnp.bfloat16)
    d_wide = d_attended.astype(jnp.float32)
    row_delta = jnp.sum(d_wide * attended, axis=-1)
    d_probs = jnp.einsum('tgd,kd->tgk', d_wide, value_rows)
    d_scores = (probs * (d_probs - row_delta[..., None])).astype(jnp.bfloat16)
    d_scores_wide = d_scores.astype(jnp.float32)
    d_query = (jnp.einsum('tgk,kd->tgd', d_scores_wide, key_rows) * inv_root).astype(jnp.bfloat16)
    d_keys = jnp.einsum('tgk,tgd->kd', d_scores_wide, query_wide) * inv_root
    d_values = jnp.einsum('tgk,tgd->kd', probs_low.astype(jnp.float32), d_wide)
    segment_grad = jnp.stack([d_keys, d_values], axis=1).astype(jnp.bfloat16)
    return gated, d_query, segment_grad


def reference(queries, image_kv, gate_logit, d_gated, media_list, media_count, image_slot):
    gate_all = jnp.tanh(gate_logit).reshape(HEADS_KV, GROUP)

    def one_segment(grad_total, segment):
        first_row = (segment * TOK_DEV).astype(jnp.int32)
        query_block = lax.dynamic_slice_in_dim(queries, first_row, TOK_DEV, 0).reshape(TOK_DEV, HEADS_KV, GROUP, HD)
        grad_block = lax.dynamic_slice_in_dim(d_gated, first_row, TOK_DEV, 0).reshape(TOK_DEV, HEADS_KV, GROUP, HD)
        slots = jnp.take(image_slot, media_list[segment]).astype(jnp.int32)
        kv_block = jnp.take(image_kv, slots, axis=0)
        live_keys = jnp.repeat(jnp.arange(MEDIA) < media_count[segment], VT)
        kv_heads = kv_block.reshape(MEDIA * VT, 2, HEADS_KV, HD).transpose(2, 0, 1, 3)
        live_heads = jnp.broadcast_to(live_keys[None, :], (HEADS_KV, MEDIA * VT))
        gated_h, d_query_h, grad_h = lax.map(one_head, (query_block.transpose(1, 0, 2, 3), grad_block.transpose(1, 0, 2, 3), kv_heads, gate_all, live_heads))
        gated_seg = gated_h.transpose(1, 0, 2, 3).reshape(TOK_DEV, HEADS_KV * GROUP * HD)
        d_query_seg = d_query_h.transpose(1, 0, 2, 3).reshape(TOK_DEV, HEADS_KV * GROUP * HD)
        grad_seg = grad_h.transpose(1, 2, 0, 3).reshape(MEDIA, VT, 2, HEADS_KV * HD)
        grad_total = grad_total.at[slots].add(grad_seg.astype(jnp.float32))
        return grad_total, (gated_seg, d_query_seg)

    grad_start = jnp.zeros((IMAGES, VT, 2, HEADS_KV * HD), jnp.float32)
    grad_total, (gated_all, d_query_all) = lax.scan(one_segment, grad_start, jnp.arange(SEGMENTS, dtype=jnp.int32))
    gated = gated_all.reshape(TOKENS, HEADS_KV * GROUP * HD)
    d_queries = d_query_all.reshape(TOKENS, HEADS_KV * GROUP * HD)
    return gated, d_queries, grad_total.astype(jnp.bfloat16)
```

```python
import functools

import jax
import jax.numpy as jnp
from jax import lax
from jax.experimental import pallas as pl
from jax.experimental.pallas import tpu as pltpu
from jax.sharding import PartitionSpec as P

MESH = pl.DeviceIdType.MESH
HD = 128
XN = 4
ZN = 8
HN = 8
MEDIA = 16
LOWEST = 12
TOK = 192
ROWS = 1536
HALF = 768
RB = 256
KEYS = 1024
PART = 64
SLOTS = 64
LOG2E = 1.4426950408889634
INV_ROOT = HD ** (-0.5)
F32 = jnp.float32
BF16 = jnp.bfloat16


def mod(value, n):
    return lax.rem(value + n, n)


def nt_dot(a, b):
    return lax.dot_general(a, b, (((1,), (1,)), ((), ())), preferred_element_type=F32)


def nn_dot(a, b):
    return jnp.dot(a, b, preferred_element_type=F32)


def kernel(
    slots_ref, counts_ref, inv_ref, gate_ref, q_ref, dg_ref, kv_ref,
    gated_ref, dq_ref, dkv_ref,
    kall, vall, qall, daall, dat, dap, pmat, kc, kt, vc, vt, sbuf, dsbuf, ot,
    stat, statin, fac, dlt, xo, xin, gk, gv, rout, rin, fin, dkvin,
    a2a_s, a2a_r, ag_s, ag_r, xg_s, xg_r, st_s, st_r, xr_s, xr_r, rs_s, rs_r, fa_s, fa_r,
):
    seq = lax.axis_index("seq")
    h = lax.axis_index("head")
    z = seq // XN
    x = lax.rem(seq, XN)
    hq = h // 2
    hp = lax.rem(h, 2)
    kv_all = (kall, vall)
    xg_all = (qall, daall)
    grads = (gk, gv)
    pending = []

    def dev(zz, xx, hh):
        return (zz * XN + xx, hh)

    def send(src, dst, ssem, rsem, device):
        copy = pltpu.make_async_remote_copy(
            src_ref=src, dst_ref=dst, send_sem=ssem, recv_sem=rsem, device_id=device, device_id_type=MESH
        )
        copy.start()
        pending.append(copy)

    def arrived(ref, sem):
        pltpu.make_async_copy(ref, ref, sem).wait()

    z_to = (mod(z + 1, ZN), mod(z - 1, ZN))
    x_to = (mod(x + 1, XN), mod(x - 1, XN))
    x_opp = mod(x + 2, XN)
    self_in = x == hq

    barrier = pltpu.get_barrier_semaphore()

    def greet(device):
        pl.semaphore_signal(barrier, inc=1, device_id=device, device_id_type=MESH)

    for k in range(1, HN):
        greet(dev(z, hq, mod(h + k, HN)))
    for k in range(1, XN):
        greet(dev(z, mod(x + k, XN), 2 * x + hp))
        greet(dev(z, mod(x + k, XN), 2 * x + 1 - hp))
        greet(dev(z, mod(x + k, XN), h))
    greet(dev(z, x, 2 * x + 1 - hp))

    @pl.when(jnp.logical_not(self_in))
    def _():
        greet(dev(z, hq, h))
        greet(dev(z, x, 2 * x + hp))

    for d in range(2):
        greet(dev(z_to[d], x, h))
    pl.semaphore_wait(barrier, jnp.where(self_in, 19, 21))

    def a2a_copy(t, k):
        target = mod(h + k, HN)
        mine = kall if t == 0 else vall
        dst = mine.at[pl.ds(2 * seq, 2), hp]
        return pltpu.make_async_remote_copy(
            src_ref=kv_ref.at[t, target], dst_ref=dst, send_sem=a2a_s.at[t, k],
            recv_sem=a2a_r.at[t, 2 * x + hp], device_id=dev(z, hq, target), device_id_type=MESH,
        )

    for t in range(2):
        for k in range(1, HN):
            a2a_copy(t, k).start()

        @pl.when(jnp.logical_not(self_in))
        def _():
            a2a_copy(t, 0).start()

        @pl.when(self_in)
        def _():
            pltpu.make_async_copy(
                kv_ref.at[t, h], kv_all[t].at[pl.ds(2 * seq, 2), hp], a2a_r.at[t, 2 * x + hp]
            ).start()

    def a2a_wait(t):
        for xx in range(XN):
            for jj in range(2):
                arrived(kv_all[t].at[pl.ds(2 * (z * XN + xx), 2), jj], a2a_r.at[t, 2 * xx + jj])

    def xg_ref(t, c, half):
        return xg_all[t].at[c, half]

    def xg_first(t):
        for pos in range(2):
            for d in range(2):
                half = d if pos == 0 else 1 - d
                ref = xg_ref(t, x, half)
                send(ref, ref, xg_s.at[t, d, pos], xg_r.at[t, d, pos], dev(z, x_to[d], h))

    def xg_wait(t, d, pos):
        c = x_opp if pos == 2 else x_to[1 - d]
        half = 1 - d if pos == 1 else d
        arrived(xg_ref(t, c, half), xg_r.at[t, d, pos])

    def xg_forward(t):
        for d in range(2):
            xg_wait(t, d, 0)
            ref = xg_ref(t, x_to[1 - d], d)
            send(ref, ref, xg_s.at[t, d, 2], xg_r.at[t, d, 2], dev(z, x_to[d], h))

    def ag_ref(t, zz, d, pos):
        sub = d if pos == 0 else 1 - d
        return kv_all[t].at[pl.ds(zz * 8 + 4 * sub, 4)]

    def ag_send(t, k, pos):
        for d in range(2):
            zz = mod(z - (k - 1), ZN) if d == 0 else mod(z + (k - 1), ZN)
            ref = ag_ref(t, zz, d, pos)
            i = 2 * (k - 1) + pos
            send(ref, ref, ag_s.at[t, d, i], ag_r.at[t, d, i], dev(z_to[d], x, h))

    def ag_wait(t, k, pos):
        for d in range(2):
            zz = mod(z - k, ZN) if d == 0 else mod(z + k, ZN)
            arrived(ag_ref(t, zz, d, pos), ag_r.at[t, d, 2 * (k - 1) + pos])

    def ag_step(t, k):
        for pos in range(1 if k == 4 else 2):
            if k > 1:
                ag_wait(t, k - 1, pos)
            ag_send(t, k, pos)

    def ag_end(t):
        ag_wait(t, 3, 1)
        ag_wait(t, 4, 0)

    for g in range(8):
        rows = q_ref[:, g * HD : (g + 1) * HD]
        qall[x, g // 4, (g % 4) * TOK : (g % 4 + 1) * TOK, :] = rows
    xg_first(0)
    for g in range(8):
        rows = dg_ref[:, g * HD : (g + 1) * HD].astype(F32) * gate_ref[g]
        daall[x, g // 4, (g % 4) * TOK : (g % 4 + 1) * TOK, :] = rows.astype(BF16)
    stat[...] = jnp.ones_like(stat)

    a2a_wait(0)
    ag_step(0, 1)
    xg_forward(0)
    xg_first(1)
    ag_step(0, 2)
    a2a_wait(1)
    ag_step(0, 3)
    ag_step(0, 4)
    ag_step(1, 1)
    ag_end(0)

    def pick(src, dst, dst_t, c):
        segment = z * XN + c

        def one(j, carry):
            slot = slots_ref[segment, j]
            dst[c, pl.ds(pl.multiple_of(j * PART, PART), PART), :] = src[slot].reshape(PART, HD)
            return carry

        lax.fori_loop(0, MEDIA, one, 0)
        for ch in range(KEYS // 256):
            block = dst[c, ch * 256 : (ch + 1) * 256, :]
            dst_t[c, :, ch * 256 : (ch + 1) * 256] = block.T

    def lanes(rb):
        return pl.ds(pl.multiple_of(rb * RB, RB), RB)

    def probs_of(c):
        pick(kall, kc, kt, c)
        live = (counts_ref[z * XN + c] - LOWEST) * PART

        def block(rb, carry):
            half = rb // 3
            q_rows = qall[c, half, pl.ds(pl.multiple_of(lax.rem(rb, 3) * RB, RB), RB), :]
            top = None
            for ch in range(4):
                s = nt_dot(kc[c, ch * 256 : (ch + 1) * 256, :], q_rows)
                if ch == 3:
                    row_ids = lax.broadcasted_iota(jnp.int32, (256, RB), 0)
                    s = jnp.where(row_ids < live, s, -1e30)
                sbuf[ch * 256 : (ch + 1) * 256, :] = s
                here = jnp.max(s, axis=0, keepdims=True)
                top = here if top is None else jnp.maximum(top, here)
            total = jnp.zeros((1, RB), F32)
            for ch in range(4):
                p = jnp.exp2((sbuf[ch * 256 : (ch + 1) * 256, :] - top) * (LOG2E * INV_ROOT))
                total = total + jnp.sum(p, axis=0, keepdims=True)
                pmat[c, ch * 256 : (ch + 1) * 256, lanes(rb)] = p.astype(BF16)
            stat[c, 0, pl.ds(rb, 1), :] = top
            stat[c, 1, pl.ds(rb, 1), :] = total
            return carry

        lax.fori_loop(0, 6, block, 0)

    def outs_of(c):
        pick(vall, vc, vt, c)

        def block(rb, carry):
            half = rb // 3
            rows = daall[c, half, pl.ds(pl.multiple_of(lax.rem(rb, 3) * RB, RB), RB), :]
            da_t = rows.T
            dat[c, :, lanes(rb)] = da_t
            o = nn_dot(vt[c], pmat[c, :, lanes(rb)])
            ot[c, :, lanes(rb)] = o
            stat[c, 2, pl.ds(rb, 1), :] = jnp.sum(da_t.astype(F32) * o, axis=0, keepdims=True)
            return carry

        lax.fori_loop(0, 6, block, 0)

    def stat_send(c, i):
        for k in range(1, XN):
            send(
                stat.at[c], statin.at[k - 1, c], st_s.at[i, k - 1], st_r.at[i, k - 1],
                dev(z, mod(x + k, XN), h),
            )

    c_right, c_left = x_to
    probs_of(x)
    ag_step(1, 2)
    xg_wait(0, 0, 1)
    probs_of(c_left)
    xg_forward(1)
    ag_step(1, 3)
    xg_wait(0, 1, 1)
    probs_of(c_right)
    ag_step(1, 4)
    for d in range(2):
        xg_wait(0, d, 2)
    probs_of(x_opp)
    ag_end(1)

    outs_of(x)
    stat_send(x, 0)
    xg_wait(1, 0, 1)
    outs_of(c_left)
    stat_send(c_left, 1)
    xg_wait(1, 1, 1)
    outs_of(c_right)
    stat_send(c_right, 2)
    for d in range(2):
        xg_wait(1, d, 2)
    outs_of(x_opp)
    stat_send(x_opp, 3)
    for i, off in enumerate((0, -1, 1, 2)):
        for k in range(1, XN):
            arrived(statin.at[k - 1, mod(x - k + off + XN, XN)], st_r.at[i, k - 1])

    def combine(c):
        tops = [stat[c, 0]] + [statin[k, c, 0] for k in range(XN - 1)]
        totals = [stat[c, 1]] + [statin[k, c, 1] for k in range(XN - 1)]
        dots = [stat[c, 2]] + [statin[k, c, 2] for k in range(XN - 1)]
        top = functools.reduce(jnp.maximum, tops)
        scales = [jnp.exp2((one - top) * (LOG2E * INV_ROOT)) for one in tops]
        total = sum(a * b for a, b in zip(scales, totals))
        delta = sum(a * b for a, b in zip(scales, dots)) / total
        own = scales[0] / total
        fac[c] = own
        dlt[c] = delta * own

        def block(rb, carry):
            half = rb // 3
            f = fac[c, pl.ds(rb, 1), :]
            cols = pl.ds(pl.multiple_of(lax.rem(rb, 3) * RB, RB), RB)
            xo[0, c, half, :, cols] = (ot[c, :, lanes(rb)] * f).astype(BF16)
            scaled = (dat[c, :, lanes(rb)].astype(F32) * f).astype(BF16)
            dat[c, :, lanes(rb)] = scaled
            dap[c, pl.ds(pl.multiple_of(rb * RB, RB), RB), :] = scaled.T
            return carry

        lax.fori_loop(0, 6, block, 0)

    def xr_opp(t):
        for d in range(2):
            send(xo.at[t, x_opp, d], xin.at[t, d, 0], xr_s.at[t, d, 0], xr_r.at[t, d, 0], dev(z, x_to[d], h))

    def xr_near(t, d):
        send(
            xo.at[t, x_to[d], 1 - d], xin.at[t, d, 1], xr_s.at[t, d, 1], xr_r.at[t, d, 1], dev(z, x_to[d], h)
        )

    def xr_add(t):
        for d in range(2):
            arrived(xin.at[t, d, 0], xr_r.at[t, d, 0])
            both = xo[t, x_to[d], d].astype(F32) + xin[t, d, 0].astype(F32)
            xo[t, x_to[d], d] = both.astype(BF16)
            send(
                xo.at[t, x_to[d], d], xin.at[t, d, 2], xr_s.at[t, d, 2], xr_r.at[t, d, 2], dev(z, x_to[d], h)
            )

    def xr_end(t):
        for d in range(2):
            for i in (1, 2):
                arrived(xin.at[t, d, i], xr_r.at[t, d, i])

    def xr_rows(t, half):
        both = xo[t, x, half].astype(F32) + xin[t, half, 2].astype(F32) + xin[t, 1 - half, 1].astype(F32)
        return both.T

    combine(x_opp)
    xr_opp(0)
    combine(c_right)
    xr_near(0, 0)
    combine(c_left)
    xr_near(0, 1)
    combine(x)

    def value_grads(c):
        for ch in range(2):
            part = nn_dot(pmat[c, ch * 512 : (ch + 1) * 512, :], dap[c])
            gv[c, ch * 8 : (ch + 1) * 8] = part.astype(BF16).reshape(8, PART, HD)

    def over_segments(f):
        def one(c, carry):
            f(c)
            return carry

        lax.fori_loop(0, XN, one, 0)

    over_segments(value_grads)
    xr_add(0)

    def own_part(t, slot):
        out = None
        for c in range(XN):
            entry = inv_ref[z * XN + c, slot]
            block = grads[t][c, jnp.maximum(entry, 0)].astype(F32)
            block = jnp.where(entry >= 0, block, 0.0)
            out = block if out is None else out + block
        return out

    def rs_step(t, i):
        k = (i + 3) // 2
        for d in range(2):
            away = 5 - k
            zt = mod(z + away, ZN) if d == 0 else mod(z - away, ZN)
            sub = d if i % 2 == 0 else 1 - d
            if i >= 2:
                arrived(rin.at[t, d, i - 2], rs_r.at[t, d, i - 2])

            def one(sl, carry):
                part = own_part(t, zt * 8 + 4 * sub + sl)
                if i >= 2:
                    part = part + rin[t, d, i - 2, sl].astype(F32)
                rout[t, d, i, sl] = part.astype(BF16)
                return carry

            lax.fori_loop(0, 4, one, 0)
            send(rout.at[t, d, i], rin.at[t, d, i], rs_s.at[t, d, i], rs_r.at[t, d, i], dev(z_to[d], x, h))

    def rs_end(t):
        for i in (5, 6):
            for d in range(2):
                arrived(rin.at[t, d, i], rs_r.at[t, d, i])
        for sub in range(2):

            def one(sl, carry):
                part = own_part(t, z * 8 + 4 * sub + sl)
                for d in range(2):
                    part = part + rin[t, d, 6 if sub == d else 5, sl].astype(F32)
                fin[t, 4 * sub + sl] = part.astype(BF16).reshape(2, 32, HD)
                return carry

            lax.fori_loop(0, 4, one, 0)

    def fa_copy(t, k, jj):
        target = mod(x + k, XN)
        return pltpu.make_async_remote_copy(
            src_ref=fin.at[t, pl.ds(2 * target, 2), jj], dst_ref=dkvin.at[t, h], send_sem=fa_s.at[t, 2 * k + jj],
            recv_sem=fa_r.at[t, h], device_id=dev(z, target, 2 * x + jj), device_id_type=MESH,
        )

    def fa_start(t):
        for k in range(XN):
            for jj in range(2):
                if k:
                    fa_copy(t, k, jj).start()
                    continue
                own = h == 2 * x + jj

                @pl.when(jnp.logical_not(own))
                def _():
                    fa_copy(t, k, jj).start()

                @pl.when(own)
                def _():
                    pltpu.make_async_copy(fin.at[t, pl.ds(2 * x, 2), jj], dkvin.at[t, h], fa_r.at[t, h]).start()

    def fa_end(t):
        for hh in range(HN):
            arrived(dkvin.at[t, hh], fa_r.at[t, hh])

    def key_grads(c):
        def block(rb, carry):
            da_t = dat[c, :, lanes(rb)]
            d_row = dlt[c, pl.ds(rb, 1), :]
            for ch in range(4):
                rows = slice(ch * 256, (ch + 1) * 256)
                dp = nn_dot(vc[c, rows, :], da_t)
                ds = pmat[c, rows, lanes(rb)].astype(F32) * (dp - d_row)
                dsbuf[rows, lanes(rb)] = ds.astype(BF16)
            cols = pl.ds(pl.multiple_of(lax.rem(rb, 3) * RB, RB), RB)
            part = nn_dot(kt[c], dsbuf[:, lanes(rb)]) * INV_ROOT
            xo[1, c, rb // 3, :, cols] = part.astype(BF16)
            return carry

        lax.fori_loop(0, 6, block, 0)
        for ch in range(2):
            part = nn_dot(dsbuf[ch * 512 : (ch + 1) * 512, :], qall[c].reshape(ROWS, HD)) * INV_ROOT
            gk[c, ch * 8 : (ch + 1) * 8] = part.astype(BF16).reshape(8, PART, HD)

    rs_step(1, 0)
    rs_step(1, 1)
    key_grads(x_opp)
    xr_opp(1)
    rs_step(1, 2)
    rs_step(1, 3)
    key_grads(c_right)
    xr_near(1, 0)
    rs_step(1, 4)
    rs_step(1, 5)
    key_grads(c_left)
    xr_near(1, 1)
    rs_step(1, 6)
    xr_add(1)
    key_grads(x)
    rs_step(0, 0)
    rs_step(0, 1)
    rs_end(1)
    fa_start(1)
    rs_step(0, 2)
    rs_step(0, 3)

    xr_end(0)
    for half in range(2):
        rows = xr_rows(0, half)
        for gg in range(4):
            g = half * 4 + gg
            gated_ref[:, g * HD : (g + 1) * HD] = (rows[gg * TOK : (gg + 1) * TOK, :] * gate_ref[g]).astype(BF16)
    rs_step(0, 4)
    rs_step(0, 5)
    xr_end(1)
    for half in range(2):
        rows = xr_rows(1, half)
        for gg in range(4):
            g = half * 4 + gg
            dq_ref[:, g * HD : (g + 1) * HD] = rows[gg * TOK : (gg + 1) * TOK, :].astype(BF16)
    rs_step(0, 6)
    rs_end(0)
    fa_start(0)
    fa_end(1)
    dkv_ref[1] = dkvin[1]
    fa_end(0)
    dkv_ref[0] = dkvin[0]

    for copy in pending:
        copy.wait_send()
    for t in range(2):
        for k in range(1, HN):
            a2a_copy(t, k).wait_send()

        @pl.when(jnp.logical_not(self_in))
        def _():
            a2a_copy(t, 0).wait_send()

        for k in range(XN):
            for jj in range(2):
                if k:
                    fa_copy(t, k, jj).wait_send()
                    continue

                @pl.when(h != 2 * x + jj)
                def _():
                    fa_copy(t, k, jj).wait_send()


def on_device(queries, image_kv, gate_logit, d_gated, media_list, media_count, image_slot):
    ids = jnp.arange(SLOTS, dtype=jnp.int32)
    slots = jnp.sum(jnp.where(media_list[:, :, None] == ids, image_slot, 0), axis=-1)
    entry = jnp.arange(MEDIA, dtype=jnp.int32)
    live = entry[None, :] < media_count[:, None]
    here = (slots[:, :, None] == ids) & live[:, :, None]
    inv = jnp.sum(jnp.where(here, entry[None, :, None] + 1, 0), axis=1) - 1
    kv = image_kv.reshape(2, 32, 2, HN, HD).transpose(2, 3, 0, 1, 4)
    smem = pl.BlockSpec(memory_space=pltpu.SMEM)
    vmem = pl.BlockSpec(memory_space=pltpu.VMEM)
    dma = pltpu.SemaphoreType.DMA
    gated, d_queries, d_kv = pl.pallas_call(
        kernel,
        out_shape=(
            jax.ShapeDtypeStruct((TOK, HN * HD), BF16),
            jax.ShapeDtypeStruct((TOK, HN * HD), BF16),
            jax.ShapeDtypeStruct((2, HN, 2, 32, HD), BF16),
        ),
        in_specs=[smem] * 4 + [vmem] * 3,
        out_specs=(vmem,) * 3,
        scratch_shapes=[
            pltpu.VMEM((SLOTS, 2, 32, HD), BF16),
            pltpu.VMEM((SLOTS, 2, 32, HD), BF16),
            pltpu.VMEM((XN, 2, HALF, HD), BF16),
            pltpu.VMEM((XN, 2, HALF, HD), BF16),
            pltpu.VMEM((XN, HD, ROWS), BF16),
            pltpu.VMEM((XN, ROWS, HD), BF16),
            pltpu.VMEM((XN, KEYS, ROWS), BF16),
            pltpu.VMEM((XN, KEYS, HD), BF16),
            pltpu.VMEM((XN, HD, KEYS), BF16),
            pltpu.VMEM((XN, KEYS, HD), BF16),
            pltpu.VMEM((XN, HD, KEYS), BF16),
            pltpu.VMEM((KEYS, RB), F32),
            pltpu.VMEM((KEYS, ROWS), BF16),
            pltpu.VMEM((XN, HD, ROWS), F32),
            pltpu.VMEM((XN, 3, 8, RB), F32),
            pltpu.VMEM((XN - 1, XN, 3, 8, RB), F32),
            pltpu.VMEM((XN, 8, RB), F32),
            pltpu.VMEM((XN, 8, RB), F32),
            pltpu.VMEM((2, XN, 2, HD, HALF), BF16),
            pltpu.VMEM((2, 2, 3, HD, HALF), BF16),
            pltpu.VMEM((XN, MEDIA, PART, HD), BF16),
            pltpu.VMEM((XN, MEDIA, PART, HD), BF16),
            pltpu.VMEM((2, 2, 7, 4, PART, HD), BF16),
            pltpu.VMEM((2, 2, 7, 4, PART, HD), BF16),
            pltpu.VMEM((2, 8, 2, 32, HD), BF16),
            pltpu.VMEM((2, HN, 2, 32, HD), BF16),
            dma((2, 8)), dma((2, 8)),
            dma((2, 2, 7)), dma((2, 2, 7)),
            dma((2, 2, 3)), dma((2, 2, 3)),
            dma((4, 3)), dma((4, 3)),
            dma((2, 2, 3)), dma((2, 2, 3)),
            dma((2, 2, 7)), dma((2, 2, 7)),
            dma((2, 8)), dma((2, 8)),
        ],
        compiler_params=pltpu.CompilerParams(
            collective_id=0, has_side_effects=True, vmem_limit_bytes=60 * 1024 * 1024
        ),
        name="attend",
    )(slots, media_count, inv, jnp.tanh(gate_logit), queries, d_gated, kv)
    d_image_kv = d_kv.transpose(2, 3, 0, 1, 4).reshape(2, 32, 2, HN * HD)
    return gated, d_queries, d_image_kv


def solution(mesh):
    return jax.shard_map(
        on_device,
        mesh=mesh,
        in_specs=(
            P("seq", "head"),
            P("seq", "head", None, None),
            P("head"),
            P("seq", "head"),
            P(),
            P(),
            P(),
        ),
        out_specs=(P("seq", "head"), P("seq", "head"), P("seq", "head", None, None)),
        check_vma=False,
    )
```

```python
import functools

import jax
import jax.numpy as jnp
from jax import lax
from jax.experimental import pallas as pl
from jax.experimental.pallas import tpu as pltpu
from jax.sharding import PartitionSpec as P

MESH = pl.DeviceIdType.MESH
HD = 128
XN = 4
ZN = 8
HN = 8
MEDIA = 16
LOWEST = 12
TOK = 192
ROWS = 1536
HALF = 768
RB = 256
KEYS = 1024
PART = 64
SLOTS = 64
LOG2E = 1.4426950408889634
INV_ROOT = HD ** (-0.5)
F32 = jnp.float32
BF16 = jnp.bfloat16


def mod(value, n):
    return lax.rem(value + n, n)


def nt_dot(a, b):
    return lax.dot_general(a, b, (((1,), (1,)), ((), ())), preferred_element_type=F32)


def nn_dot(a, b):
    return jnp.dot(a, b, preferred_element_type=F32)


def kernel(
    media_ref, counts_ref, place_ref, gate_ref, q_ref, dg_ref, kv_ref,
    gated_ref, dq_ref, dkv_ref,
    kall, vall, qall, daall, dat, dap, pmat, kc, kt, vc, vt, sbuf, dsbuf, ot,
    stat, statin, fac, dlt, xo, xin, gk, gv, rout, rin, fin, dkvin, inv_v, inv_ref, inv_sem,
    a2a_s, a2a_r, ag_s, ag_r, xg_s, xg_r, st_s, st_r, xr_s, xr_r, rs_s, rs_r, fa_s, fa_r,
):
    seq = lax.axis_index("seq")
    h = lax.axis_index("head")
    z = seq // XN
    x = lax.rem(seq, XN)
    hq = h // 2
    hp = lax.rem(h, 2)
    kv_all = (kall, vall)
    xg_all = (qall, daall)
    grads = (gk, gv)
    pending = []

    def dev(zz, xx, hh):
        return (zz * XN + xx, hh)

    def send(src, dst, ssem, rsem, device):
        copy = pltpu.make_async_remote_copy(
            src_ref=src, dst_ref=dst, send_sem=ssem, recv_sem=rsem, device_id=device, device_id_type=MESH
        )
        copy.start()
        pending.append(copy)

    def arrived(ref, sem):
        pltpu.make_async_copy(ref, ref, sem).wait()

    z_to = (mod(z + 1, ZN), mod(z - 1, ZN))
    x_to = (mod(x + 1, XN), mod(x - 1, XN))
    x_opp = mod(x + 2, XN)
    x_part = lax.rem(x + hq + 2 * hp, XN)
    self_in = x_part == x

    def holder(k, jj):
        return 2 * ((2 * XN - k - 2 * jj) % XN) + jj

    barrier = pltpu.get_barrier_semaphore()

    def greet(device):
        pl.semaphore_signal(barrier, inc=1, device_id=device, device_id_type=MESH)

    for k in range(1, HN):
        greet(dev(z, x_part, mod(h + k, HN)))
    for k in range(1, XN):
        greet(dev(z, mod(x + k, XN), h))
        for jj in range(2):
            greet(dev(z, mod(x + k, XN), holder(k, jj)))
    for jj in range(2):

        @pl.when(h != holder(0, jj))
        def _():
            greet(dev(z, x, holder(0, jj)))

    @pl.when(jnp.logical_not(self_in))
    def _():
        greet(dev(z, x_part, h))

    for d in range(2):
        greet(dev(z_to[d], x, h))
    pl.semaphore_wait(barrier, jnp.where(self_in, 19, 21))

    def kv_lanes(t, head):
        return kv_ref.at[:, :, pl.ds(pl.multiple_of((t * HN + head) * HD, HD), HD)]

    def a2a_copy(t, k):
        target = mod(h + k, HN)
        mine = kall if t == 0 else vall
        dst = mine.at[pl.ds(2 * seq, 2), hp]
        return pltpu.make_async_remote_copy(
            src_ref=kv_lanes(t, target), dst_ref=dst, send_sem=a2a_s.at[t, k],
            recv_sem=a2a_r.at[t, 2 * x + hp], device_id=dev(z, x_part, target), device_id_type=MESH,
        )

    for t in range(2):
        for k in range(1, HN):
            a2a_copy(t, k).start()

        @pl.when(jnp.logical_not(self_in))
        def _():
            a2a_copy(t, 0).start()

        @pl.when(self_in)
        def _():
            pltpu.make_async_copy(
                kv_lanes(t, h), kv_all[t].at[pl.ds(2 * seq, 2), hp], a2a_r.at[t, 2 * x + hp]
            ).start()

    def a2a_wait(t):
        for xx in range(XN):
            for jj in range(2):
                arrived(kv_all[t].at[pl.ds(2 * (z * XN + xx), 2), jj], a2a_r.at[t, 2 * xx + jj])

    def xg_ref(t, c, half):
        return xg_all[t].at[c, half]

    def xg_first(t):
        for pos in range(2):
            for d in range(2):
                half = d if pos == 0 else 1 - d
                ref = xg_ref(t, x, half)
                send(ref, ref, xg_s.at[t, d, pos], xg_r.at[t, d, pos], dev(z, x_to[d], h))

    def xg_wait(t, d, pos):
        c = x_opp if pos == 2 else x_to[1 - d]
        half = 1 - d if pos == 1 else d
        arrived(xg_ref(t, c, half), xg_r.at[t, d, pos])

    def xg_forward(t):
        for d in range(2):
            xg_wait(t, d, 0)
            ref = xg_ref(t, x_to[1 - d], d)
            send(ref, ref, xg_s.at[t, d, 2], xg_r.at[t, d, 2], dev(z, x_to[d], h))

    def ag_ref(t, zz, d, pos):
        sub = d if pos == 0 else 1 - d
        return kv_all[t].at[pl.ds(zz * 8 + 4 * sub, 4)]

    def ag_send(t, k, pos):
        for d in range(2):
            zz = mod(z - (k - 1), ZN) if d == 0 else mod(z + (k - 1), ZN)
            ref = ag_ref(t, zz, d, pos)
            i = 2 * (k - 1) + pos
            send(ref, ref, ag_s.at[t, d, i], ag_r.at[t, d, i], dev(z_to[d], x, h))

    def ag_wait(t, k, pos):
        for d in range(2):
            zz = mod(z - k, ZN) if d == 0 else mod(z + k, ZN)
            arrived(ag_ref(t, zz, d, pos), ag_r.at[t, d, 2 * (k - 1) + pos])

    def ag_pass(t, k, pos):
        ag_wait(t, k - 1, pos)
        ag_send(t, k, pos)

    def ag_step(t, k):
        for pos in range(1 if k == 4 else 2):
            ag_pass(t, k, pos)

    def ag_end(t):
        ag_wait(t, 3, 1)
        ag_wait(t, 4, 0)

    for g in range(8):
        rows = q_ref[:, g * HD : (g + 1) * HD]
        qall[x, g // 4, (g % 4) * TOK : (g % 4 + 1) * TOK, :] = rows
    xg_first(0)

    def gate_row(g):
        return jnp.tanh(jnp.full((1, HD), gate_ref[g], F32))

    for g in range(8):
        rows = dg_ref[:, g * HD : (g + 1) * HD].astype(F32) * gate_row(g)
        daall[x, g // 4, (g % 4) * TOK : (g % 4 + 1) * TOK, :] = rows.astype(BF16)
    stat[...] = jnp.ones_like(stat)

    lane = lax.broadcasted_iota(jnp.int32, (1, HD), 1)
    inv_v[...] = jnp.full((8, HD), -1, jnp.int32)
    for c in range(XN):
        found = jnp.full((1, HD), -1, jnp.int32)
        for j in range(MEDIA):
            slot = place_ref[media_ref[j, z * XN + c]]
            slot = jnp.where(j < counts_ref[z * XN + c], slot, -1)
            found = jnp.where(lane == slot, j, found)
        inv_v[c : c + 1, :] = found
    inv_copy = pltpu.make_async_copy(inv_v, inv_ref, inv_sem)
    inv_copy.start()

    a2a_wait(0)
    ag_send(0, 1, 0)
    ag_send(0, 1, 1)
    a2a_wait(1)
    ag_send(1, 1, 0)
    xg_forward(0)
    xg_first(1)
    ag_step(0, 2)
    ag_send(1, 1, 1)
    ag_step(0, 3)
    ag_pass(1, 2, 0)
    ag_step(0, 4)
    ag_pass(1, 2, 1)
    inv_copy.wait()
    ag_end(0)

    def pick(src, dst, dst_t, c):
        segment = z * XN + c

        def one(j, carry):
            slot = place_ref[media_ref[j, segment]]
            dst[c, pl.ds(pl.multiple_of(j * PART, PART), PART), :] = src[slot].reshape(PART, HD)
            return carry

        lax.fori_loop(0, MEDIA, one, 0)
        for ch in range(KEYS // 256):
            block = dst[c, ch * 256 : (ch + 1) * 256, :]
            dst_t[c, :, ch * 256 : (ch + 1) * 256] = block.T

    def lanes(rb):
        return pl.ds(pl.multiple_of(rb * RB, RB), RB)

    def probs_of(c):
        pick(kall, kc, kt, c)
        live = (counts_ref[z * XN + c] - LOWEST) * PART

        def block(rb, carry):
            half = rb // 3
            q_rows = qall[c, half, pl.ds(pl.multiple_of(lax.rem(rb, 3) * RB, RB), RB), :]
            top = None
            for ch in range(4):
                s = nt_dot(kc[c, ch * 256 : (ch + 1) * 256, :], q_rows)
                if ch == 3:
                    row_ids = lax.broadcasted_iota(jnp.int32, (256, RB), 0)
                    s = jnp.where(row_ids < live, s, -1e30)
                sbuf[ch * 256 : (ch + 1) * 256, :] = s
                here = jnp.max(s, axis=0, keepdims=True)
                top = here if top is None else jnp.maximum(top, here)
            total = jnp.zeros((1, RB), F32)
            for ch in range(4):
                p = jnp.exp2((sbuf[ch * 256 : (ch + 1) * 256, :] - top) * (LOG2E * INV_ROOT))
                total = total + jnp.sum(p, axis=0, keepdims=True)
                pmat[c, ch * 256 : (ch + 1) * 256, lanes(rb)] = p.astype(BF16)
            stat[c, 0, pl.ds(rb, 1), :] = top
            stat[c, 1, pl.ds(rb, 1), :] = total
            return carry

        lax.fori_loop(0, 6, block, 0)

    def outs_of(c):
        pick(vall, vc, vt, c)

        def block(rb, carry):
            half = rb // 3
            rows = daall[c, half, pl.ds(pl.multiple_of(lax.rem(rb, 3) * RB, RB), RB), :]
            da_t = rows.T
            dat[c, :, lanes(rb)] = da_t
            o = nn_dot(vt[c], pmat[c, :, lanes(rb)])
            ot[c, :, lanes(rb)] = o
            stat[c, 2, pl.ds(rb, 1), :] = jnp.sum(da_t.astype(F32) * o, axis=0, keepdims=True)
            return carry

        lax.fori_loop(0, 6, block, 0)

    def stat_send(c, i):
        for k in range(1, XN):
            send(
                stat.at[c], statin.at[k - 1, c], st_s.at[i, k - 1], st_r.at[i, k - 1],
                dev(z, mod(x + k, XN), h),
            )

    c_right, c_left = x_to
    probs_of(x)
    ag_step(1, 3)
    xg_wait(0, 0, 1)
    probs_of(c_left)
    xg_forward(1)
    ag_step(1, 4)
    xg_wait(0, 1, 1)
    probs_of(c_right)
    for d in range(2):
        xg_wait(0, d, 2)
    probs_of(x_opp)
    ag_end(1)

    outs_of(x)
    stat_send(x, 0)
    xg_wait(1, 0, 1)
    outs_of(c_left)
    stat_send(c_left, 1)
    xg_wait(1, 1, 1)
    outs_of(c_right)
    stat_send(c_right, 2)
    for d in range(2):
        xg_wait(1, d, 2)
    outs_of(x_opp)
    stat_send(x_opp, 3)
    for i, off in enumerate((0, -1, 1, 2)):
        for k in range(1, XN):
            arrived(statin.at[k - 1, mod(x - k + off + XN, XN)], st_r.at[i, k - 1])

    def combine(c):
        tops = [stat[c, 0]] + [statin[k, c, 0] for k in range(XN - 1)]
        totals = [stat[c, 1]] + [statin[k, c, 1] for k in range(XN - 1)]
        dots = [stat[c, 2]] + [statin[k, c, 2] for k in range(XN - 1)]
        top = functools.reduce(jnp.maximum, tops)
        scales = [jnp.exp2((one - top) * (LOG2E * INV_ROOT)) for one in tops]
        total = sum(a * b for a, b in zip(scales, totals))
        delta = sum(a * b for a, b in zip(scales, dots)) / total
        own = scales[0] / total
        fac[c] = own
        dlt[c] = delta * own

        def block(rb, carry):
            half = rb // 3
            f = fac[c, pl.ds(rb, 1), :]
            cols = pl.ds(pl.multiple_of(lax.rem(rb, 3) * RB, RB), RB)
            xo[0, c, half, :, cols] = (ot[c, :, lanes(rb)] * f).astype(BF16)
            scaled = (dat[c, :, lanes(rb)].astype(F32) * f).astype(BF16)
            dat[c, :, lanes(rb)] = scaled
            dap[c, pl.ds(pl.multiple_of(rb * RB, RB), RB), :] = scaled.T
            return carry

        lax.fori_loop(0, 6, block, 0)

    def xr_opp(t):
        for d in range(2):
            send(xo.at[t, x_opp, d], xin.at[t, d, 0], xr_s.at[t, d, 0], xr_r.at[t, d, 0], dev(z, x_to[d], h))

    def xr_near(t, d):
        send(
            xo.at[t, x_to[d], 1 - d], xin.at[t, d, 1], xr_s.at[t, d, 1], xr_r.at[t, d, 1], dev(z, x_to[d], h)
        )

    def xr_add(t):
        for d in range(2):
            arrived(xin.at[t, d, 0], xr_r.at[t, d, 0])
            both = xo[t, x_to[d], d].astype(F32) + xin[t, d, 0].astype(F32)
            xo[t, x_to[d], d] = both.astype(BF16)
            send(
                xo.at[t, x_to[d], d], xin.at[t, d, 2], xr_s.at[t, d, 2], xr_r.at[t, d, 2], dev(z, x_to[d], h)
            )

    def xr_end(t):
        for d in range(2):
            for i in (1, 2):
                arrived(xin.at[t, d, i], xr_r.at[t, d, i])

    def xr_rows(t, half):
        both = xo[t, x, half].astype(F32) + xin[t, half, 2].astype(F32) + xin[t, 1 - half, 1].astype(F32)
        return both.T

    combine(x_opp)
    xr_opp(0)
    combine(c_right)
    xr_near(0, 0)
    combine(c_left)
    xr_near(0, 1)
    combine(x)

    def value_grads(c):
        for ch in range(2):
            part = nn_dot(pmat[c, ch * 512 : (ch + 1) * 512, :], dap[c])
            gv[c, ch * 8 : (ch + 1) * 8] = part.astype(BF16).reshape(8, PART, HD)

    def over_segments(f):
        def one(c, carry):
            f(c)
            return carry

        lax.fori_loop(0, XN, one, 0)

    over_segments(value_grads)

    def own_part(t, slot):
        out = None
        for c in range(XN):
            entry = inv_ref[c, slot]
            block = grads[t][c, jnp.maximum(entry, 0)].astype(F32)
            block = jnp.where(entry >= 0, block, 0.0)
            out = block if out is None else out + block
        return out

    def rs_step(t, i):
        k = (i + 3) // 2
        for d in range(2):
            away = 5 - k
            zt = mod(z + away, ZN) if d == 0 else mod(z - away, ZN)
            sub = d if i % 2 == 0 else 1 - d
            if i >= 2:
                arrived(rin.at[t, d, i - 2], rs_r.at[t, d, i - 2])

            def one(sl, carry):
                part = own_part(t, zt * 8 + 4 * sub + sl)
                if i >= 2:
                    part = part + rin[t, d, i - 2, sl].astype(F32)
                rout[t, d, i, sl] = part.astype(BF16)
                return carry

            lax.fori_loop(0, 4, one, 0)
            send(rout.at[t, d, i], rin.at[t, d, i], rs_s.at[t, d, i], rs_r.at[t, d, i], dev(z_to[d], x, h))

    def rs_end(t):
        for i in (5, 6):
            for d in range(2):
                arrived(rin.at[t, d, i], rs_r.at[t, d, i])
        for sub in range(2):

            def one(sl, carry):
                part = own_part(t, z * 8 + 4 * sub + sl)
                for d in range(2):
                    part = part + rin[t, d, 6 if sub == d else 5, sl].astype(F32)
                fin[t, 4 * sub + sl] = part.astype(BF16).reshape(2, 32, HD)
                return carry

            lax.fori_loop(0, 4, one, 0)

    def fa_copy(t, k, jj):
        target = mod(x + k, XN)
        return pltpu.make_async_remote_copy(
            src_ref=fin.at[t, pl.ds(2 * target, 2), jj], dst_ref=dkvin.at[t, h], send_sem=fa_s.at[t, 2 * k + jj],
            recv_sem=fa_r.at[t, h], device_id=dev(z, target, holder(k, jj)), device_id_type=MESH,
        )

    def fa_start(t):
        for k in range(XN):
            for jj in range(2):
                if k:
                    fa_copy(t, k, jj).start()
                    continue
                own = h == holder(0, jj)

                @pl.when(jnp.logical_not(own))
                def _():
                    fa_copy(t, k, jj).start()

                @pl.when(own)
                def _():
                    pltpu.make_async_copy(fin.at[t, pl.ds(2 * x, 2), jj], dkvin.at[t, h], fa_r.at[t, h]).start()

    def fa_end(t):
        for hh in range(HN):
            arrived(dkvin.at[t, hh], fa_r.at[t, hh])

    def key_grads(c):
        def block(rb, carry):
            da_t = dat[c, :, lanes(rb)]
            d_row = dlt[c, pl.ds(rb, 1), :]
            for ch in range(4):
                rows = slice(ch * 256, (ch + 1) * 256)
                dp = nn_dot(vc[c, rows, :], da_t)
                ds = pmat[c, rows, lanes(rb)].astype(F32) * (dp - d_row)
                dsbuf[rows, lanes(rb)] = ds.astype(BF16)
            cols = pl.ds(pl.multiple_of(lax.rem(rb, 3) * RB, RB), RB)
            part = nn_dot(kt[c], dsbuf[:, lanes(rb)]) * INV_ROOT
            xo[1, c, rb // 3, :, cols] = part.astype(BF16)
            return carry

        lax.fori_loop(0, 6, block, 0)
        for ch in range(2):
            part = nn_dot(dsbuf[ch * 512 : (ch + 1) * 512, :], qall[c].reshape(ROWS, HD)) * INV_ROOT
            gk[c, ch * 8 : (ch + 1) * 8] = part.astype(BF16).reshape(8, PART, HD)

    rs_step(1, 0)
    rs_step(1, 1)
    xr_add(0)
    key_grads(x_opp)
    xr_opp(1)
    rs_step(1, 2)
    rs_step(1, 3)
    key_grads(c_right)
    xr_near(1, 0)
    rs_step(1, 4)
    rs_step(1, 5)
    key_grads(c_left)
    xr_near(1, 1)
    rs_step(1, 6)
    xr_add(1)
    key_grads(x)
    rs_step(0, 0)
    rs_step(0, 1)
    rs_end(1)
    fa_start(1)
    rs_step(0, 2)
    rs_step(0, 3)

    xr_end(0)
    for half in range(2):
        rows = xr_rows(0, half)
        for gg in range(4):
            g = half * 4 + gg
            gated_ref[:, g * HD : (g + 1) * HD] = (rows[gg * TOK : (gg + 1) * TOK, :] * gate_row(g)).astype(BF16)
    rs_step(0, 4)
    rs_step(0, 5)
    xr_end(1)
    for half in range(2):
        rows = xr_rows(1, half)
        for gg in range(4):
            g = half * 4 + gg
            dq_ref[:, g * HD : (g + 1) * HD] = rows[gg * TOK : (gg + 1) * TOK, :].astype(BF16)
    rs_step(0, 6)
    rs_end(0)
    fa_start(0)
    for t in (1, 0):
        fa_end(t)
        for hh in range(HN):
            dkv_ref[:, :, (t * HN + hh) * HD : (t * HN + hh + 1) * HD] = dkvin[t, hh]

    for copy in pending:
        copy.wait_send()
    for t in range(2):
        for k in range(1, HN):
            a2a_copy(t, k).wait_send()

        @pl.when(jnp.logical_not(self_in))
        def _():
            a2a_copy(t, 0).wait_send()

        for k in range(XN):
            for jj in range(2):
                if k:
                    fa_copy(t, k, jj).wait_send()
                    continue

                @pl.when(h != holder(0, jj))
                def _():
                    fa_copy(t, k, jj).wait_send()


def on_device(queries, image_kv, gate_logit, d_gated, media_list, media_count, image_slot):
    kv = image_kv.reshape(2, 32, 2 * HN * HD)
    smem = pl.BlockSpec(memory_space=pltpu.SMEM)
    vmem = pl.BlockSpec(memory_space=pltpu.VMEM)
    dma = pltpu.SemaphoreType.DMA
    gated, d_queries, d_kv = pl.pallas_call(
        kernel,
        out_shape=(
            jax.ShapeDtypeStruct((TOK, HN * HD), BF16),
            jax.ShapeDtypeStruct((TOK, HN * HD), BF16),
            jax.ShapeDtypeStruct((2, 32, 2 * HN * HD), BF16),
        ),
        in_specs=[smem] * 4 + [vmem] * 3,
        out_specs=(vmem,) * 3,
        scratch_shapes=[
            pltpu.VMEM((SLOTS, 2, 32, HD), BF16),
            pltpu.VMEM((SLOTS, 2, 32, HD), BF16),
            pltpu.VMEM((XN, 2, HALF, HD), BF16),
            pltpu.VMEM((XN, 2, HALF, HD), BF16),
            pltpu.VMEM((XN, HD, ROWS), BF16),
            pltpu.VMEM((XN, ROWS, HD), BF16),
            pltpu.VMEM((XN, KEYS, ROWS), BF16),
            pltpu.VMEM((XN, KEYS, HD), BF16),
            pltpu.VMEM((XN, HD, KEYS), BF16),
            pltpu.VMEM((XN, KEYS, HD), BF16),
            pltpu.VMEM((XN, HD, KEYS), BF16),
            pltpu.VMEM((KEYS, RB), F32),
            pltpu.VMEM((KEYS, ROWS), BF16),
            pltpu.VMEM((XN, HD, ROWS), F32),
            pltpu.VMEM((XN, 3, 8, RB), F32),
            pltpu.VMEM((XN - 1, XN, 3, 8, RB), F32),
            pltpu.VMEM((XN, 8, RB), F32),
            pltpu.VMEM((XN, 8, RB), F32),
            pltpu.VMEM((2, XN, 2, HD, HALF), BF16),
            pltpu.VMEM((2, 2, 3, HD, HALF), BF16),
            pltpu.VMEM((XN, MEDIA, PART, HD), BF16),
            pltpu.VMEM((XN, MEDIA, PART, HD), BF16),
            pltpu.VMEM((2, 2, 7, 4, PART, HD), BF16),
            pltpu.VMEM((2, 2, 7, 4, PART, HD), BF16),
            pltpu.VMEM((2, 8, 2, 32, HD), BF16),
            pltpu.VMEM((2, HN, 2, 32, HD), BF16),
            pltpu.VMEM((8, HD), jnp.int32),
            pltpu.SMEM((8, HD), jnp.int32),
            dma,
            dma((2, 8)), dma((2, 8)),
            dma((2, 2, 7)), dma((2, 2, 7)),
            dma((2, 2, 3)), dma((2, 2, 3)),
            dma((4, 3)), dma((4, 3)),
            dma((2, 2, 3)), dma((2, 2, 3)),
            dma((2, 2, 7)), dma((2, 2, 7)),
            dma((2, 8)), dma((2, 8)),
        ],
        compiler_params=pltpu.CompilerParams(
            collective_id=0, has_side_effects=True, vmem_limit_bytes=60 * 1024 * 1024
        ),
        name="attend",
    )(media_list.T, media_count, image_slot, gate_logit, queries, d_gated, kv)
    d_image_kv = d_kv.reshape(2, 32, 2, HN * HD)
    return gated, d_queries, d_image_kv


def solution(mesh):
    return jax.shard_map(
        on_device,
        mesh=mesh,
        in_specs=(
            P("seq", "head"),
            P("seq", "head", None, None),
            P("head"),
            P("seq", "head"),
            P(),
            P(),
            P(),
        ),
        out_specs=(P("seq", "head"), P("seq", "head"), P("seq", "head", None, None)),
        check_vma=False,
    )
```

```python
import functools

import jax
import jax.numpy as jnp
from jax import lax
from jax.experimental import pallas as pl
from jax.experimental.pallas import tpu as pltpu
from jax.sharding import PartitionSpec as P

MESH = pl.DeviceIdType.MESH
HD = 128
XN = 4
ZN = 8
HN = 8
MEDIA = 16
LOWEST = 12
TOK = 192
ROWS = 1536
HALF = 768
RB = 256
KEYS = 1024
PART = 64
SLOTS = 64
MS = 256
UNROLL = 6
LOG2E = 1.4426950408889634
INV_ROOT = HD ** (-0.5)
F32 = jnp.float32
BF16 = jnp.bfloat16


def mod(value, n):
    return lax.rem(value + n, n)


def nt_dot(a, b):
    return lax.dot_general(a, b, (((1,), (1,)), ((), ())), preferred_element_type=F32)


def nn_dot(a, b):
    return jnp.dot(a, b, preferred_element_type=F32)


def kernel(
    media_ref, counts_ref, place_ref, gate_ref, q_ref, dg_ref, kv_ref,
    gated_ref, dq_ref, dkv_ref,
    kall, vall, qall, daall, dat, dap, pmat, kc, kt, vc, vt, sbuf, ot,
    stat, statin, fac, dlt, xo, xin, gk, gv, rout, rin, fin, dkvin, inv_v, inv_ref, inv_sem,
    a2a_s, a2a_r, ag_s, ag_r, xg_s, xg_r, st_s, st_r, xr_s, xr_r, rs_s, rs_r, fa_s, fa_r,
):
    seq = lax.axis_index("seq")
    h = lax.axis_index("head")
    z = seq // XN
    x = lax.rem(seq, XN)
    hq = h // 2
    hp = lax.rem(h, 2)
    kv_all = (kall, vall)
    xg_all = (qall, daall)
    grads = (gk, gv)
    pending = []

    def dev(zz, xx, hh):
        return (zz * XN + xx, hh)

    def send(src, dst, ssem, rsem, device):
        copy = pltpu.make_async_remote_copy(
            src_ref=src, dst_ref=dst, send_sem=ssem, recv_sem=rsem, device_id=device, device_id_type=MESH
        )
        copy.start()
        pending.append(copy)

    def arrived(ref, sem):
        pltpu.make_async_copy(ref, ref, sem).wait()

    z_to = (mod(z + 1, ZN), mod(z - 1, ZN))
    x_to = (mod(x + 1, XN), mod(x - 1, XN))
    x_opp = mod(x + 2, XN)
    x_part = lax.rem(x + hq + 2 * hp, XN)
    self_in = x_part == x

    def holder(k, jj):
        return 2 * ((2 * XN - k - 2 * jj) % XN) + jj

    barrier = pltpu.get_barrier_semaphore()

    def greet(device):
        pl.semaphore_signal(barrier, inc=1, device_id=device, device_id_type=MESH)

    for k in range(1, HN):
        greet(dev(z, x_part, mod(h + k, HN)))
    for k in range(1, XN):
        greet(dev(z, mod(x + k, XN), h))
        for jj in range(2):
            greet(dev(z, mod(x + k, XN), holder(k, jj)))
    for jj in range(2):

        @pl.when(h != holder(0, jj))
        def _():
            greet(dev(z, x, holder(0, jj)))

    @pl.when(jnp.logical_not(self_in))
    def _():
        greet(dev(z, x_part, h))

    for d in range(2):
        greet(dev(z_to[d], x, h))
    pl.semaphore_wait(barrier, jnp.where(self_in, 19, 21))

    def kv_lanes(t, head):
        return kv_ref.at[:, :, pl.ds(pl.multiple_of((t * HN + head) * HD, HD), HD)]

    def a2a_copy(t, k):
        target = mod(h + k, HN)
        mine = kall if t == 0 else vall
        dst = mine.at[pl.ds(2 * seq, 2), hp]
        return pltpu.make_async_remote_copy(
            src_ref=kv_lanes(t, target), dst_ref=dst, send_sem=a2a_s.at[t, k],
            recv_sem=a2a_r.at[t, 2 * x + hp], device_id=dev(z, x_part, target), device_id_type=MESH,
        )

    for t in range(2):
        for k in range(1, HN):
            a2a_copy(t, k).start()

        @pl.when(jnp.logical_not(self_in))
        def _():
            a2a_copy(t, 0).start()

        @pl.when(self_in)
        def _():
            pltpu.make_async_copy(
                kv_lanes(t, h), kv_all[t].at[pl.ds(2 * seq, 2), hp], a2a_r.at[t, 2 * x + hp]
            ).start()

    def a2a_wait(t):
        for xx in range(XN):
            for jj in range(2):
                arrived(kv_all[t].at[pl.ds(2 * (z * XN + xx), 2), jj], a2a_r.at[t, 2 * xx + jj])

    def xg_ref(t, c, half):
        return xg_all[t].at[c, half]

    def xg_first(t):
        for pos in range(2):
            for d in range(2):
                half = d if pos == 0 else 1 - d
                ref = xg_ref(t, x, half)
                send(ref, ref, xg_s.at[t, d, pos], xg_r.at[t, d, pos], dev(z, x_to[d], h))

    def xg_wait(t, d, pos):
        c = x_opp if pos == 2 else x_to[1 - d]
        half = 1 - d if pos == 1 else d
        arrived(xg_ref(t, c, half), xg_r.at[t, d, pos])

    def xg_forward(t):
        for d in range(2):
            xg_wait(t, d, 0)
            ref = xg_ref(t, x_to[1 - d], d)
            send(ref, ref, xg_s.at[t, d, 2], xg_r.at[t, d, 2], dev(z, x_to[d], h))

    def ag_ref(t, zz, d, pos):
        sub = d if pos == 0 else 1 - d
        return kv_all[t].at[pl.ds(zz * 8 + 4 * sub, 4)]

    def ag_send(t, k, pos):
        for d in range(2):
            zz = mod(z - (k - 1), ZN) if d == 0 else mod(z + (k - 1), ZN)
            ref = ag_ref(t, zz, d, pos)
            i = 2 * (k - 1) + pos
            send(ref, ref, ag_s.at[t, d, i], ag_r.at[t, d, i], dev(z_to[d], x, h))

    def ag_wait(t, k, pos):
        for d in range(2):
            zz = mod(z - k, ZN) if d == 0 else mod(z + k, ZN)
            arrived(ag_ref(t, zz, d, pos), ag_r.at[t, d, 2 * (k - 1) + pos])

    def ag_pass(t, k, pos):
        ag_wait(t, k - 1, pos)
        ag_send(t, k, pos)

    def ag_step(t, k):
        for pos in range(1 if k == 4 else 2):
            ag_pass(t, k, pos)

    def ag_end(t):
        ag_wait(t, 3, 1)
        ag_wait(t, 4, 0)

    for g in range(8):
        rows = q_ref[:, g * HD : (g + 1) * HD]
        qall[x, g // 4, (g % 4) * TOK : (g % 4 + 1) * TOK, :] = rows
    xg_first(0)

    def gate_row(g):
        return jnp.tanh(jnp.full((1, HD), gate_ref[g], F32))

    for g in range(8):
        rows = dg_ref[:, g * HD : (g + 1) * HD].astype(F32) * gate_row(g)
        daall[x, g // 4, (g % 4) * TOK : (g % 4 + 1) * TOK, :] = rows.astype(BF16)
    stat[...] = jnp.ones_like(stat)

    lane = lax.broadcasted_iota(jnp.int32, (1, HD), 1)
    inv_v[...] = jnp.full((8, HD), -1, jnp.int32)
    for c in range(XN):
        found = jnp.full((1, HD), -1, jnp.int32)
        for j in range(MEDIA):
            slot = place_ref[media_ref[j, z * XN + c]]
            slot = jnp.where(j < counts_ref[z * XN + c], slot, -1)
            found = jnp.where(lane == slot, j, found)
        inv_v[c : c + 1, :] = found
    inv_copy = pltpu.make_async_copy(inv_v, inv_ref, inv_sem)
    inv_copy.start()

    a2a_wait(0)
    ag_send(0, 1, 0)
    ag_send(0, 1, 1)
    a2a_wait(1)
    ag_send(1, 1, 0)
    xg_forward(0)
    xg_first(1)
    ag_step(0, 2)
    ag_send(1, 1, 1)
    ag_step(0, 3)
    ag_pass(1, 2, 0)
    ag_step(0, 4)
    ag_pass(1, 2, 1)
    inv_copy.wait()
    ag_end(0)

    def pick(src, dst, dst_t, c):
        segment = z * XN + c

        for j in range(MEDIA):
            slot = place_ref[media_ref[j, segment]]
            dst[c, j * PART : (j + 1) * PART, :] = src[slot].reshape(PART, HD)
        for ch in range(KEYS // 256):
            block = dst[c, ch * 256 : (ch + 1) * 256, :]
            dst_t[c, :, ch * 256 : (ch + 1) * 256] = block.T

    def lanes(rb):
        return pl.ds(pl.multiple_of(rb * RB, RB), RB)

    def probs_of(c):
        pick(kall, kc, kt, c)
        live = (counts_ref[z * XN + c] - LOWEST) * PART

        def block(i, carry):
            for r in range(UNROLL):
                rb = i * UNROLL + r
                q_rows = qall[c, rb // 3, pl.ds(pl.multiple_of(lax.rem(rb, 3) * RB, RB), RB), :]
                top = None
                for m in range(KEYS // MS):
                    rows = slice(m * MS, (m + 1) * MS)
                    s = nt_dot(kc[c, rows, :], q_rows)
                    if m == KEYS // MS - 1:
                        first = LOWEST * PART - m * MS
                        row_ids = lax.broadcasted_iota(jnp.int32, (KEYS - LOWEST * PART, RB), 0)
                        last = jnp.where(row_ids < live, s[first:], -1e30)
                        s = jnp.concatenate([s[:first], last], axis=0) if first else last
                    sbuf[r, rows, :] = s
                    here = jnp.max(s, axis=0, keepdims=True)
                    top = here if top is None else jnp.maximum(top, here)
                total = jnp.zeros((1, RB), F32)
                for ch in range(4):
                    rows = slice(ch * 256, (ch + 1) * 256)
                    p = jnp.exp2((sbuf[r, rows, :] - top) * (LOG2E * INV_ROOT))
                    total = total + jnp.sum(p, axis=0, keepdims=True)
                    pmat[c, rows, lanes(rb)] = p.astype(BF16)
                stat[c, 0, pl.ds(rb, 1), :] = top
                stat[c, 1, pl.ds(rb, 1), :] = total
            return carry

        lax.fori_loop(0, 6 // UNROLL, block, 0)

    def outs_of(c):
        pick(vall, vc, vt, c)

        def block(i, carry):
            for r in range(UNROLL):
                rb = i * UNROLL + r
                rows = daall[c, rb // 3, pl.ds(pl.multiple_of(lax.rem(rb, 3) * RB, RB), RB), :]
                da_t = rows.T
                dat[c, :, lanes(rb)] = da_t
                o = nn_dot(vt[c], pmat[c, :, lanes(rb)])
                ot[c, :, lanes(rb)] = o
                stat[c, 2, pl.ds(rb, 1), :] = jnp.sum(da_t.astype(F32) * o, axis=0, keepdims=True)
            return carry

        lax.fori_loop(0, 6 // UNROLL, block, 0)

    def stat_send(c, i):
        for k in range(1, XN):
            send(
                stat.at[c], statin.at[k - 1, c], st_s.at[i, k - 1], st_r.at[i, k - 1],
                dev(z, mod(x + k, XN), h),
            )

    c_right, c_left = x_to
    probs_of(x)
    ag_step(1, 3)
    xg_wait(0, 0, 1)
    probs_of(c_left)
    xg_forward(1)
    ag_step(1, 4)
    xg_wait(0, 1, 1)
    probs_of(c_right)
    for d in range(2):
        xg_wait(0, d, 2)
    probs_of(x_opp)
    ag_end(1)

    outs_of(x)
    stat_send(x, 0)
    xg_wait(1, 0, 1)
    outs_of(c_left)
    stat_send(c_left, 1)
    xg_wait(1, 1, 1)
    outs_of(c_right)
    stat_send(c_right, 2)
    for d in range(2):
        xg_wait(1, d, 2)
    outs_of(x_opp)
    stat_send(x_opp, 3)
    for i, off in enumerate((0, -1, 1, 2)):
        for k in range(1, XN):
            arrived(statin.at[k - 1, mod(x - k + off + XN, XN)], st_r.at[i, k - 1])

    def combine(c):
        tops = [stat[c, 0]] + [statin[k, c, 0] for k in range(XN - 1)]
        totals = [stat[c, 1]] + [statin[k, c, 1] for k in range(XN - 1)]
        dots = [stat[c, 2]] + [statin[k, c, 2] for k in range(XN - 1)]
        top = functools.reduce(jnp.maximum, tops)
        scales = [jnp.exp2((one - top) * (LOG2E * INV_ROOT)) for one in tops]
        total = sum(a * b for a, b in zip(scales, totals))
        delta = sum(a * b for a, b in zip(scales, dots)) / total
        own = scales[0] / total
        fac[c] = own
        dlt[c] = delta * own

        def block(rb, carry):
            half = rb // 3
            f = fac[c, pl.ds(rb, 1), :]
            cols = pl.ds(pl.multiple_of(lax.rem(rb, 3) * RB, RB), RB)
            xo[0, c, half, :, cols] = (ot[c, :, lanes(rb)] * f).astype(BF16)
            scaled = (dat[c, :, lanes(rb)].astype(F32) * f).astype(BF16)
            dat[c, :, lanes(rb)] = scaled
            dap[c, pl.ds(pl.multiple_of(rb * RB, RB), RB), :] = scaled.T
            return carry

        lax.fori_loop(0, 6, block, 0, unroll=True)

    def xr_opp(t):
        for d in range(2):
            send(xo.at[t, x_opp, d], xin.at[t, d, 0], xr_s.at[t, d, 0], xr_r.at[t, d, 0], dev(z, x_to[d], h))

    def xr_near(t, d):
        send(
            xo.at[t, x_to[d], 1 - d], xin.at[t, d, 1], xr_s.at[t, d, 1], xr_r.at[t, d, 1], dev(z, x_to[d], h)
        )

    def xr_add(t):
        for d in range(2):
            arrived(xin.at[t, d, 0], xr_r.at[t, d, 0])
            both = xo[t, x_to[d], d].astype(F32) + xin[t, d, 0].astype(F32)
            xo[t, x_to[d], d] = both.astype(BF16)
            send(
                xo.at[t, x_to[d], d], xin.at[t, d, 2], xr_s.at[t, d, 2], xr_r.at[t, d, 2], dev(z, x_to[d], h)
            )

    def xr_end(t):
        for d in range(2):
            for i in (1, 2):
                arrived(xin.at[t, d, i], xr_r.at[t, d, i])

    def xr_rows(t, half):
        both = xo[t, x, half].astype(F32) + xin[t, half, 2].astype(F32) + xin[t, 1 - half, 1].astype(F32)
        return both.T

    combine(x_opp)
    xr_opp(0)
    combine(c_right)
    xr_near(0, 0)
    combine(c_left)
    xr_near(0, 1)
    combine(x)

    def value_grads(c):
        for m in range(KEYS // MS):
            part = nn_dot(pmat[c, m * MS : (m + 1) * MS, :], dap[c])
            gv[c, m * MS // PART : (m + 1) * MS // PART] = part.astype(BF16).reshape(MS // PART, PART, HD)

    def over_segments(f):
        def one(c, carry):
            f(c)
            return carry

        lax.fori_loop(0, XN, one, 0)

    over_segments(value_grads)

    def own_part(t, slot):
        out = None
        for c in range(XN):
            entry = inv_ref[c, slot]
            block = grads[t][c, jnp.maximum(entry, 0)].astype(F32)
            block = jnp.where(entry >= 0, block, 0.0)
            out = block if out is None else out + block
        return out

    def rs_step(t, i):
        k = (i + 3) // 2
        for d in range(2):
            away = 5 - k
            zt = mod(z + away, ZN) if d == 0 else mod(z - away, ZN)
            sub = d if i % 2 == 0 else 1 - d
            if i >= 2:
                arrived(rin.at[t, d, i - 2], rs_r.at[t, d, i - 2])

            def one(sl, carry):
                part = own_part(t, zt * 8 + 4 * sub + sl)
                if i >= 2:
                    part = part + rin[t, d, i - 2, sl].astype(F32)
                rout[t, d, i, sl] = part.astype(BF16)
                return carry

            lax.fori_loop(0, 4, one, 0)
            send(rout.at[t, d, i], rin.at[t, d, i], rs_s.at[t, d, i], rs_r.at[t, d, i], dev(z_to[d], x, h))

    def rs_end(t):
        for i in (5, 6):
            for d in range(2):
                arrived(rin.at[t, d, i], rs_r.at[t, d, i])
        for sub in range(2):

            def one(sl, carry):
                part = own_part(t, z * 8 + 4 * sub + sl)
                for d in range(2):
                    part = part + rin[t, d, 6 if sub == d else 5, sl].astype(F32)
                fin[t, 4 * sub + sl] = part.astype(BF16).reshape(2, 32, HD)
                return carry

            lax.fori_loop(0, 4, one, 0)

    def fa_copy(t, k, jj):
        target = mod(x + k, XN)
        return pltpu.make_async_remote_copy(
            src_ref=fin.at[t, pl.ds(2 * target, 2), jj], dst_ref=dkvin.at[t, h], send_sem=fa_s.at[t, 2 * k + jj],
            recv_sem=fa_r.at[t, h], device_id=dev(z, target, holder(k, jj)), device_id_type=MESH,
        )

    def fa_start(t):
        for k in range(XN):
            for jj in range(2):
                if k:
                    fa_copy(t, k, jj).start()
                    continue
                own = h == holder(0, jj)

                @pl.when(jnp.logical_not(own))
                def _():
                    fa_copy(t, k, jj).start()

                @pl.when(own)
                def _():
                    pltpu.make_async_copy(fin.at[t, pl.ds(2 * x, 2), jj], dkvin.at[t, h], fa_r.at[t, h]).start()

    def fa_end(t):
        for hh in range(HN):
            arrived(dkvin.at[t, hh], fa_r.at[t, hh])

    def key_grads(c):
        def block(i, carry):
            for r in range(UNROLL):
                rb = i * UNROLL + r
                da_t = dat[c, :, lanes(rb)]
                d_row = dlt[c, pl.ds(rb, 1), :]
                for m in range(KEYS // MS):
                    rows = slice(m * MS, (m + 1) * MS)
                    dp = nn_dot(vc[c, rows, :], da_t) - d_row
                    ds = pmat[c, rows, lanes(rb)].astype(F32) * dp
                    pmat[c, rows, lanes(rb)] = ds.astype(BF16)
            return carry

        lax.fori_loop(0, 6 // UNROLL, block, 0)
        for m in range(KEYS // MS):
            part = nn_dot(pmat[c, m * MS : (m + 1) * MS, :], qall[c].reshape(ROWS, HD)) * INV_ROOT
            gk[c, m * MS // PART : (m + 1) * MS // PART] = part.astype(BF16).reshape(MS // PART, PART, HD)

    def query_grads(c):
        def block(i, carry):
            for r in range(UNROLL):
                rb = i * UNROLL + r
                part = nn_dot(kt[c], pmat[c, :, lanes(rb)]) * INV_ROOT
                cols = pl.ds(pl.multiple_of(lax.rem(rb, 3) * RB, RB), RB)
                xo[1, c, rb // 3, :, cols] = part.astype(BF16)
            return carry

        lax.fori_loop(0, 6 // UNROLL, block, 0)

    rs_step(1, 0)
    rs_step(1, 1)
    xr_add(0)
    key_grads(x_opp)
    rs_step(1, 2)
    rs_step(1, 3)
    key_grads(c_right)
    rs_step(1, 4)
    key_grads(c_left)
    rs_step(1, 5)
    key_grads(x)
    rs_step(0, 0)
    rs_step(0, 1)
    rs_step(1, 6)
    query_grads(x_opp)
    xr_opp(1)
    query_grads(c_right)
    xr_near(1, 0)
    query_grads(c_left)
    xr_near(1, 1)
    rs_step(0, 2)
    rs_step(0, 3)
    query_grads(x)
    rs_end(1)
    fa_start(1)
    rs_step(0, 4)
    xr_add(1)
    rs_step(0, 5)
    xr_end(0)
    for half in range(2):
        rows = xr_rows(0, half)
        for gg in range(4):
            g = half * 4 + gg
            gated_ref[:, g * HD : (g + 1) * HD] = (rows[gg * TOK : (gg + 1) * TOK, :] * gate_row(g)).astype(BF16)
    rs_step(0, 6)
    rs_end(0)
    fa_start(0)
    xr_end(1)
    for half in range(2):
        rows = xr_rows(1, half)
        for gg in range(4):
            g = half * 4 + gg
            dq_ref[:, g * HD : (g + 1) * HD] = rows[gg * TOK : (gg + 1) * TOK, :].astype(BF16)
    for t in (1, 0):
        fa_end(t)
        for hh in range(HN):
            dkv_ref[:, :, (t * HN + hh) * HD : (t * HN + hh + 1) * HD] = dkvin[t, hh]

    for copy in pending:
        copy.wait_send()
    for t in range(2):
        for k in range(1, HN):
            a2a_copy(t, k).wait_send()

        @pl.when(jnp.logical_not(self_in))
        def _():
            a2a_copy(t, 0).wait_send()

        for k in range(XN):
            for jj in range(2):
                if k:
                    fa_copy(t, k, jj).wait_send()
                    continue

                @pl.when(h != holder(0, jj))
                def _():
                    fa_copy(t, k, jj).wait_send()


def on_device(queries, image_kv, gate_logit, d_gated, media_list, media_count, image_slot):
    kv = image_kv.reshape(2, 32, 2 * HN * HD)
    smem = pl.BlockSpec(memory_space=pltpu.SMEM)
    vmem = pl.BlockSpec(memory_space=pltpu.VMEM)
    dma = pltpu.SemaphoreType.DMA
    gated, d_queries, d_kv = pl.pallas_call(
        kernel,
        out_shape=(
            jax.ShapeDtypeStruct((TOK, HN * HD), BF16),
            jax.ShapeDtypeStruct((TOK, HN * HD), BF16),
            jax.ShapeDtypeStruct((2, 32, 2 * HN * HD), BF16),
        ),
        in_specs=[smem] * 4 + [vmem] * 3,
        out_specs=(vmem,) * 3,
        scratch_shapes=[
            pltpu.VMEM((SLOTS, 2, 32, HD), BF16),
            pltpu.VMEM((SLOTS, 2, 32, HD), BF16),
            pltpu.VMEM((XN, 2, HALF, HD), BF16),
            pltpu.VMEM((XN, 2, HALF, HD), BF16),
            pltpu.VMEM((XN, HD, ROWS), BF16),
            pltpu.VMEM((XN, ROWS, HD), BF16),
            pltpu.VMEM((XN, KEYS, ROWS), BF16),
            pltpu.VMEM((XN, KEYS, HD), BF16),
            pltpu.VMEM((XN, HD, KEYS), BF16),
            pltpu.VMEM((XN, KEYS, HD), BF16),
            pltpu.VMEM((XN, HD, KEYS), BF16),
            pltpu.VMEM((UNROLL, KEYS, RB), F32),
            pltpu.VMEM((XN, HD, ROWS), F32),
            pltpu.VMEM((XN, 3, 8, RB), F32),
            pltpu.VMEM((XN - 1, XN, 3, 8, RB), F32),
            pltpu.VMEM((XN, 8, RB), F32),
            pltpu.VMEM((XN, 8, RB), F32),
            pltpu.VMEM((2, XN, 2, HD, HALF), BF16),
            pltpu.VMEM((2, 2, 3, HD, HALF), BF16),
            pltpu.VMEM((XN, MEDIA, PART, HD), BF16),
            pltpu.VMEM((XN, MEDIA, PART, HD), BF16),
            pltpu.VMEM((2, 2, 7, 4, PART, HD), BF16),
            pltpu.VMEM((2, 2, 7, 4, PART, HD), BF16),
            pltpu.VMEM((2, 8, 2, 32, HD), BF16),
            pltpu.VMEM((2, HN, 2, 32, HD), BF16),
            pltpu.VMEM((8, HD), jnp.int32),
            pltpu.SMEM((8, HD), jnp.int32),
            dma,
            dma((2, 8)), dma((2, 8)),
            dma((2, 2, 7)), dma((2, 2, 7)),
            dma((2, 2, 3)), dma((2, 2, 3)),
            dma((4, 3)), dma((4, 3)),
            dma((2, 2, 3)), dma((2, 2, 3)),
            dma((2, 2, 7)), dma((2, 2, 7)),
            dma((2, 8)), dma((2, 8)),
        ],
        compiler_params=pltpu.CompilerParams(
            collective_id=0, has_side_effects=True, vmem_limit_bytes=60 * 1024 * 1024
        ),
        name="attend",
    )(media_list.T, media_count, image_slot, gate_logit, queries, d_gated, kv)
    d_image_kv = d_kv.reshape(2, 32, 2, HN * HD)
    return gated, d_queries, d_image_kv


def solution(mesh):
    return jax.shard_map(
        on_device,
        mesh=mesh,
        in_specs=(
            P("seq", "head"),
            P("seq", "head", None, None),
            P("head"),
            P("seq", "head"),
            P(),
            P(),
            P(),
        ),
        out_specs=(P("seq", "head"), P("seq", "head"), P("seq", "head", None, None)),
        check_vma=False,
    )
```

```python
import functools

import jax
import jax.numpy as jnp
from jax import lax
from jax.experimental import pallas as pl
from jax.experimental.pallas import tpu as pltpu
from jax.sharding import PartitionSpec as P

MESH = pl.DeviceIdType.MESH
HD = 128
XN = 4
ZN = 8
HN = 8
MEDIA = 16
LOWEST = 12
TOK = 192
ROWS = 1536
HALF = 768
RB = 256
KEYS = 1024
PART = 64
SLOTS = 64
MS = 256
UNROLL = 6
LOG2E = 1.4426950408889634
INV_ROOT = HD ** (-0.5)
F32 = jnp.float32
BF16 = jnp.bfloat16


def mod(value, n):
    return lax.rem(value + n, n)


def nt_dot(a, b):
    return lax.dot_general(a, b, (((1,), (1,)), ((), ())), preferred_element_type=F32)


def nn_dot(a, b):
    return jnp.dot(a, b, preferred_element_type=F32)


def kernel(
    media_ref, counts_ref, place_ref, gate_ref, q_ref, dg_ref, kv_ref,
    gated_ref, dq_ref, dkv_ref,
    kall, vall, qall, daall, dat, dap, pmat, kc, kt, vc, vt, sbuf, ot,
    stat, statin, fac, dlt, xo, xin, gk, gv, rout, rin, fin, dkvin, inv_v, inv_ref, inv_sem,
    a2a_s, a2a_r, ag_s, ag_r, xg_s, xg_r, st_s, st_r, xr_s, xr_r, rs_s, rs_r, fa_s, fa_r,
):
    seq = lax.axis_index("seq")
    h = lax.axis_index("head")
    z = seq // XN
    x = lax.rem(seq, XN)
    hq = h // 2
    hp = lax.rem(h, 2)
    kv_all = (kall, vall)
    xg_all = (qall, daall)
    grads = (gk, gv)
    pending = []

    def dev(zz, xx, hh):
        return (zz * XN + xx, hh)

    def send(src, dst, ssem, rsem, device):
        copy = pltpu.make_async_remote_copy(
            src_ref=src, dst_ref=dst, send_sem=ssem, recv_sem=rsem, device_id=device, device_id_type=MESH
        )
        copy.start()
        pending.append(copy)

    def arrived(ref, sem):
        pltpu.make_async_copy(ref, ref, sem).wait()

    z_to = (mod(z + 1, ZN), mod(z - 1, ZN))
    x_to = (mod(x + 1, XN), mod(x - 1, XN))
    x_opp = mod(x + 2, XN)
    x_part = lax.rem(x + hq + 2 * hp, XN)
    self_in = x_part == x

    def holder(k, jj):
        return 2 * ((2 * XN - k - 2 * jj) % XN) + jj

    barrier = pltpu.get_barrier_semaphore()

    def greet(device):
        pl.semaphore_signal(barrier, inc=1, device_id=device, device_id_type=MESH)

    for k in range(1, HN):
        greet(dev(z, x_part, mod(h + k, HN)))
    for k in range(1, XN):
        greet(dev(z, mod(x + k, XN), h))
        for jj in range(2):
            greet(dev(z, mod(x + k, XN), holder(k, jj)))
    for jj in range(2):

        @pl.when(h != holder(0, jj))
        def _():
            greet(dev(z, x, holder(0, jj)))

    @pl.when(jnp.logical_not(self_in))
    def _():
        greet(dev(z, x_part, h))

    for d in range(2):
        greet(dev(z_to[d], x, h))
    pl.semaphore_wait(barrier, jnp.where(self_in, 19, 21))

    def kv_lanes(t, head):
        return kv_ref.at[:, :, pl.ds(pl.multiple_of((t * HN + head) * HD, HD), HD)]

    def a2a_copy(t, k):
        target = mod(h + k, HN)
        mine = kall if t == 0 else vall
        dst = mine.at[pl.ds(2 * seq, 2), hp]
        return pltpu.make_async_remote_copy(
            src_ref=kv_lanes(t, target), dst_ref=dst, send_sem=a2a_s.at[t, k],
            recv_sem=a2a_r.at[t, 2 * x + hp], device_id=dev(z, x_part, target), device_id_type=MESH,
        )

    for t in range(2):
        for k in range(1, HN):
            a2a_copy(t, k).start()

        @pl.when(jnp.logical_not(self_in))
        def _():
            a2a_copy(t, 0).start()

        @pl.when(self_in)
        def _():
            pltpu.make_async_copy(
                kv_lanes(t, h), kv_all[t].at[pl.ds(2 * seq, 2), hp], a2a_r.at[t, 2 * x + hp]
            ).start()

    def a2a_wait(t, sub):
        for xx in (2 * sub, 2 * sub + 1):
            for jj in range(2):
                arrived(kv_all[t].at[pl.ds(2 * (z * XN + xx), 2), jj], a2a_r.at[t, 2 * xx + jj])

    def xg_ref(t, c, half):
        return xg_all[t].at[c, half]

    def xg_first(t):
        for pos in range(2):
            for d in range(2):
                half = d if pos == 0 else 1 - d
                ref = xg_ref(t, x, half)
                send(ref, ref, xg_s.at[t, d, pos], xg_r.at[t, d, pos], dev(z, x_to[d], h))

    def xg_wait(t, d, pos):
        c = x_opp if pos == 2 else x_to[1 - d]
        half = 1 - d if pos == 1 else d
        arrived(xg_ref(t, c, half), xg_r.at[t, d, pos])

    def xg_forward(t):
        for d in range(2):
            xg_wait(t, d, 0)
            ref = xg_ref(t, x_to[1 - d], d)
            send(ref, ref, xg_s.at[t, d, 2], xg_r.at[t, d, 2], dev(z, x_to[d], h))

    def ag_ref(t, zz, d, pos):
        sub = d if pos == 0 else 1 - d
        return kv_all[t].at[pl.ds(zz * 8 + 4 * sub, 4)]

    def ag_send(t, k, pos, ways=(0, 1)):
        for d in ways:
            zz = mod(z - (k - 1), ZN) if d == 0 else mod(z + (k - 1), ZN)
            ref = ag_ref(t, zz, d, pos)
            i = 2 * (k - 1) + pos
            send(ref, ref, ag_s.at[t, d, i], ag_r.at[t, d, i], dev(z_to[d], x, h))

    def ag_wait(t, k, pos):
        for d in range(2):
            zz = mod(z - k, ZN) if d == 0 else mod(z + k, ZN)
            arrived(ag_ref(t, zz, d, pos), ag_r.at[t, d, 2 * (k - 1) + pos])

    def ag_pass(t, k, pos):
        ag_wait(t, k - 1, pos)
        ag_send(t, k, pos)

    def ag_step(t, k):
        for pos in range(1 if k == 4 else 2):
            ag_pass(t, k, pos)

    def ag_end(t):
        ag_wait(t, 3, 1)
        ag_wait(t, 4, 0)

    for g in range(8):
        rows = q_ref[:, g * HD : (g + 1) * HD]
        qall[x, g // 4, (g % 4) * TOK : (g % 4 + 1) * TOK, :] = rows
    xg_first(0)

    def gate_row(g):
        return jnp.tanh(jnp.full((1, HD), gate_ref[g], F32))

    for g in range(8):
        rows = dg_ref[:, g * HD : (g + 1) * HD].astype(F32) * gate_row(g)
        daall[x, g // 4, (g % 4) * TOK : (g % 4 + 1) * TOK, :] = rows.astype(BF16)
    stat[...] = jnp.ones_like(stat)

    lane = lax.broadcasted_iota(jnp.int32, (1, HD), 1)
    inv_v[...] = jnp.full((8, HD), -1, jnp.int32)
    for c in range(XN):
        found = jnp.full((1, HD), -1, jnp.int32)
        for j in range(MEDIA):
            slot = place_ref[media_ref[j, z * XN + c]]
            slot = jnp.where(j < counts_ref[z * XN + c], slot, -1)
            found = jnp.where(lane == slot, j, found)
        inv_v[c : c + 1, :] = found
    inv_copy = pltpu.make_async_copy(inv_v, inv_ref, inv_sem)
    inv_copy.start()

    for t in range(2):
        a2a_wait(t, 0)
        ag_send(t, 1, 0, (0,))
        a2a_wait(t, 1)
        ag_send(t, 1, 0, (1,))
        if t == 0:
            ag_send(0, 1, 1)
    xg_forward(0)
    xg_first(1)
    ag_step(0, 2)
    ag_send(1, 1, 1)
    ag_step(0, 3)
    ag_pass(1, 2, 0)
    ag_step(0, 4)
    ag_pass(1, 2, 1)
    inv_copy.wait()
    ag_end(0)

    def pick(src, dst, dst_t, c):
        segment = z * XN + c

        for j in range(MEDIA):
            slot = place_ref[media_ref[j, segment]]
            dst[c, j * PART : (j + 1) * PART, :] = src[slot].reshape(PART, HD)
        for ch in range(KEYS // 256):
            block = dst[c, ch * 256 : (ch + 1) * 256, :]
            dst_t[c, :, ch * 256 : (ch + 1) * 256] = block.T

    def lanes(rb):
        return pl.ds(pl.multiple_of(rb * RB, RB), RB)

    def probs_of(c):
        pick(kall, kc, kt, c)
        live = (counts_ref[z * XN + c] - LOWEST) * PART

        def block(i, carry):
            for r in range(UNROLL):
                rb = i * UNROLL + r
                q_rows = qall[c, rb // 3, pl.ds(pl.multiple_of(lax.rem(rb, 3) * RB, RB), RB), :]
                top = None
                for m in range(KEYS // MS):
                    rows = slice(m * MS, (m + 1) * MS)
                    s = nt_dot(kc[c, rows, :], q_rows)
                    if m == KEYS // MS - 1:
                        first = LOWEST * PART - m * MS
                        row_ids = lax.broadcasted_iota(jnp.int32, (KEYS - LOWEST * PART, RB), 0)
                        last = jnp.where(row_ids < live, s[first:], -1e30)
                        s = jnp.concatenate([s[:first], last], axis=0) if first else last
                    sbuf[r, rows, :] = s
                    here = jnp.max(s, axis=0, keepdims=True)
                    top = here if top is None else jnp.maximum(top, here)
                total = jnp.zeros((1, RB), F32)
                for ch in range(4):
                    rows = slice(ch * 256, (ch + 1) * 256)
                    p = jnp.exp2((sbuf[r, rows, :] - top) * (LOG2E * INV_ROOT))
                    total = total + jnp.sum(p, axis=0, keepdims=True)
                    pmat[c, rows, lanes(rb)] = p.astype(BF16)
                stat[c, 0, pl.ds(rb, 1), :] = top
                stat[c, 1, pl.ds(rb, 1), :] = total
            return carry

        lax.fori_loop(0, 6 // UNROLL, block, 0)

    def turn(c):
        for half in range(2):
            for r in range(3):
                rb = half * 3 + r
                dat[c, :, rb * RB : (rb + 1) * RB] = daall[c, half, r * RB : (r + 1) * RB, :].T

    def outs_of(c):
        pick(vall, vc, vt, c)

        def block(i, carry):
            for r in range(UNROLL):
                rb = i * UNROLL + r
                da_t = dat[c, :, lanes(rb)]
                o = nn_dot(vt[c], pmat[c, :, lanes(rb)])
                ot[c, :, lanes(rb)] = o
                stat[c, 2, pl.ds(rb, 1), :] = jnp.sum(da_t.astype(F32) * o, axis=0, keepdims=True)
            return carry

        lax.fori_loop(0, 6 // UNROLL, block, 0)

    def stat_send(c, i):
        for k in range(1, XN):
            send(
                stat.at[c], statin.at[k - 1, c], st_s.at[i, k - 1], st_r.at[i, k - 1],
                dev(z, mod(x + k, XN), h),
            )

    c_right, c_left = x_to
    xg_forward(1)
    turn(x)
    probs_of(x)
    ag_step(1, 3)
    xg_wait(0, 0, 1)
    probs_of(c_left)
    ag_step(1, 4)
    xg_wait(0, 1, 1)
    probs_of(c_right)
    for d in range(2):
        xg_wait(0, d, 2)
    probs_of(x_opp)
    xg_wait(1, 0, 1)
    turn(c_left)
    xg_wait(1, 1, 1)
    turn(c_right)
    for d in range(2):
        xg_wait(1, d, 2)
    turn(x_opp)
    ag_end(1)

    for c in range(XN):
        outs_of(c)
        stat_send(c, c)

    def stat_wait(c):
        for k in range(1, XN):
            arrived(statin.at[k - 1, c], st_r.at[c, k - 1])

    def combine(c):
        stat_wait(c)
        tops = [stat[c, 0]] + [statin[k, c, 0] for k in range(XN - 1)]
        totals = [stat[c, 1]] + [statin[k, c, 1] for k in range(XN - 1)]
        dots = [stat[c, 2]] + [statin[k, c, 2] for k in range(XN - 1)]
        top = functools.reduce(jnp.maximum, tops)
        scales = [jnp.exp2((one - top) * (LOG2E * INV_ROOT)) for one in tops]
        total = sum(a * b for a, b in zip(scales, totals))
        delta = sum(a * b for a, b in zip(scales, dots)) / total
        own = scales[0] / total
        fac[c] = own
        dlt[c] = delta * own

        def block(rb, carry):
            half = rb // 3
            f = fac[c, pl.ds(rb, 1), :]
            cols = pl.ds(pl.multiple_of(lax.rem(rb, 3) * RB, RB), RB)
            xo[0, c, half, :, cols] = (ot[c, :, lanes(rb)] * f).astype(BF16)
            scaled = (dat[c, :, lanes(rb)].astype(F32) * f).astype(BF16)
            dat[c, :, lanes(rb)] = scaled
            dap[c, pl.ds(pl.multiple_of(rb * RB, RB), RB), :] = scaled.T
            return carry

        lax.fori_loop(0, 6, block, 0, unroll=True)

    def xr_opp(t):
        for d in range(2):
            send(xo.at[t, x_opp, d], xin.at[t, d, 0], xr_s.at[t, d, 0], xr_r.at[t, d, 0], dev(z, x_to[d], h))

    def xr_near(t, d):
        send(
            xo.at[t, x_to[d], 1 - d], xin.at[t, d, 1], xr_s.at[t, d, 1], xr_r.at[t, d, 1], dev(z, x_to[d], h)
        )

    def xr_add(t):
        for d in range(2):
            arrived(xin.at[t, d, 0], xr_r.at[t, d, 0])
            both = xo[t, x_to[d], d].astype(F32) + xin[t, d, 0].astype(F32)
            xo[t, x_to[d], d] = both.astype(BF16)
            send(
                xo.at[t, x_to[d], d], xin.at[t, d, 2], xr_s.at[t, d, 2], xr_r.at[t, d, 2], dev(z, x_to[d], h)
            )

    def xr_end(t):
        for d in range(2):
            for i in (1, 2):
                arrived(xin.at[t, d, i], xr_r.at[t, d, i])

    def xr_rows(t, half):
        both = xo[t, x, half].astype(F32) + xin[t, half, 2].astype(F32) + xin[t, 1 - half, 1].astype(F32)
        return both.T

    for c in range(XN):
        combine(c)
    xr_opp(0)
    xr_near(0, 0)
    xr_near(0, 1)

    def value_grads(c):
        for m in range(KEYS // MS):
            part = nn_dot(pmat[c, m * MS : (m + 1) * MS, :], dap[c])
            gv[c, m * MS // PART : (m + 1) * MS // PART] = part.astype(BF16).reshape(MS // PART, PART, HD)

    def over_segments(f):
        def one(c, carry):
            f(c)
            return carry

        lax.fori_loop(0, XN, one, 0)

    over_segments(value_grads)

    def own_part(t, slot):
        out = None
        for c in range(XN):
            entry = inv_ref[c, slot]
            block = grads[t][c, jnp.maximum(entry, 0)].astype(F32)
            block = jnp.where(entry >= 0, block, 0.0)
            out = block if out is None else out + block
        return out

    def rs_step(t, i):
        k = (i + 3) // 2
        for d in range(2):
            away = 5 - k
            zt = mod(z + away, ZN) if d == 0 else mod(z - away, ZN)
            sub = d if i % 2 == 0 else 1 - d
            if i >= 2:
                arrived(rin.at[t, d, i - 2], rs_r.at[t, d, i - 2])

            def one(sl, carry):
                part = own_part(t, zt * 8 + 4 * sub + sl)
                if i >= 2:
                    part = part + rin[t, d, i - 2, sl].astype(F32)
                rout[t, d, i, sl] = part.astype(BF16)
                return carry

            lax.fori_loop(0, 4, one, 0)
            send(rout.at[t, d, i], rin.at[t, d, i], rs_s.at[t, d, i], rs_r.at[t, d, i], dev(z_to[d], x, h))

    def rs_end(t):
        for i in (5, 6):
            for d in range(2):
                arrived(rin.at[t, d, i], rs_r.at[t, d, i])
        for sub in range(2):

            def one(sl, carry):
                part = own_part(t, z * 8 + 4 * sub + sl)
                for d in range(2):
                    part = part + rin[t, d, 6 if sub == d else 5, sl].astype(F32)
                fin[t, 4 * sub + sl] = part.astype(BF16).reshape(2, 32, HD)
                return carry

            lax.fori_loop(0, 4, one, 0)

    def fa_copy(t, k, jj):
        target = mod(x + k, XN)
        return pltpu.make_async_remote_copy(
            src_ref=fin.at[t, pl.ds(2 * target, 2), jj], dst_ref=dkvin.at[t, h], send_sem=fa_s.at[t, 2 * k + jj],
            recv_sem=fa_r.at[t, h], device_id=dev(z, target, holder(k, jj)), device_id_type=MESH,
        )

    def fa_start(t):
        for k in range(XN):
            for jj in range(2):
                if k:
                    fa_copy(t, k, jj).start()
                    continue
                own = h == holder(0, jj)

                @pl.when(jnp.logical_not(own))
                def _():
                    fa_copy(t, k, jj).start()

                @pl.when(own)
                def _():
                    pltpu.make_async_copy(fin.at[t, pl.ds(2 * x, 2), jj], dkvin.at[t, h], fa_r.at[t, h]).start()

    def fa_end(t):
        for hh in range(HN):
            arrived(dkvin.at[t, hh], fa_r.at[t, hh])

    def key_grads(c):
        def block(i, carry):
            for r in range(UNROLL):
                rb = i * UNROLL + r
                da_t = dat[c, :, lanes(rb)]
                d_row = dlt[c, pl.ds(rb, 1), :]
                for m in range(KEYS // MS):
                    rows = slice(m * MS, (m + 1) * MS)
                    dp = nn_dot(vc[c, rows, :], da_t) - d_row
                    ds = pmat[c, rows, lanes(rb)].astype(F32) * dp
                    pmat[c, rows, lanes(rb)] = ds.astype(BF16)
            return carry

        lax.fori_loop(0, 6 // UNROLL, block, 0)
        for m in range(KEYS // MS):
            part = nn_dot(pmat[c, m * MS : (m + 1) * MS, :], qall[c].reshape(ROWS, HD)) * INV_ROOT
            gk[c, m * MS // PART : (m + 1) * MS // PART] = part.astype(BF16).reshape(MS // PART, PART, HD)

    def query_grads(c):
        def block(i, carry):
            for r in range(UNROLL):
                rb = i * UNROLL + r
                part = nn_dot(kt[c], pmat[c, :, lanes(rb)]) * INV_ROOT
                cols = pl.ds(pl.multiple_of(lax.rem(rb, 3) * RB, RB), RB)
                xo[1, c, rb // 3, :, cols] = part.astype(BF16)
            return carry

        lax.fori_loop(0, 6 // UNROLL, block, 0)

    rs_step(1, 0)
    rs_step(1, 1)
    key_grads(x_opp)
    xr_add(0)
    rs_step(1, 2)
    rs_step(1, 3)
    query_grads(x_opp)
    xr_opp(1)
    key_grads(c_right)
    rs_step(1, 4)
    key_grads(c_left)
    rs_step(1, 5)
    key_grads(x)
    rs_step(0, 0)
    rs_step(0, 1)
    rs_step(1, 6)
    query_grads(c_right)
    xr_near(1, 0)
    query_grads(c_left)
    xr_near(1, 1)
    rs_step(0, 2)
    rs_step(0, 3)
    xr_add(1)
    query_grads(x)
    rs_end(1)
    fa_start(1)
    rs_step(0, 4)
    rs_step(0, 5)
    xr_end(0)
    for half in range(2):
        rows = xr_rows(0, half)
        for gg in range(4):
            g = half * 4 + gg
            gated_ref[:, g * HD : (g + 1) * HD] = (rows[gg * TOK : (gg + 1) * TOK, :] * gate_row(g)).astype(BF16)
    rs_step(0, 6)
    rs_end(0)
    fa_start(0)
    xr_end(1)
    for half in range(2):
        rows = xr_rows(1, half)
        for gg in range(4):
            g = half * 4 + gg
            dq_ref[:, g * HD : (g + 1) * HD] = rows[gg * TOK : (gg + 1) * TOK, :].astype(BF16)
    for t in (1, 0):
        fa_end(t)
        for hh in range(HN):
            dkv_ref[:, :, (t * HN + hh) * HD : (t * HN + hh + 1) * HD] = dkvin[t, hh]

    for copy in pending:
        copy.wait_send()
    for t in range(2):
        for k in range(1, HN):
            a2a_copy(t, k).wait_send()

        @pl.when(jnp.logical_not(self_in))
        def _():
            a2a_copy(t, 0).wait_send()

        for k in range(XN):
            for jj in range(2):
                if k:
                    fa_copy(t, k, jj).wait_send()
                    continue

                @pl.when(h != holder(0, jj))
                def _():
                    fa_copy(t, k, jj).wait_send()


def on_device(queries, image_kv, gate_logit, d_gated, media_list, media_count, image_slot):
    kv = image_kv.reshape(2, 32, 2 * HN * HD)
    smem = pl.BlockSpec(memory_space=pltpu.SMEM)
    vmem = pl.BlockSpec(memory_space=pltpu.VMEM)
    dma = pltpu.SemaphoreType.DMA
    gated, d_queries, d_kv = pl.pallas_call(
        kernel,
        out_shape=(
            jax.ShapeDtypeStruct((TOK, HN * HD), BF16),
            jax.ShapeDtypeStruct((TOK, HN * HD), BF16),
            jax.ShapeDtypeStruct((2, 32, 2 * HN * HD), BF16),
        ),
        in_specs=[smem] * 4 + [vmem] * 3,
        out_specs=(vmem,) * 3,
        scratch_shapes=[
            pltpu.VMEM((SLOTS, 2, 32, HD), BF16),
            pltpu.VMEM((SLOTS, 2, 32, HD), BF16),
            pltpu.VMEM((XN, 2, HALF, HD), BF16),
            pltpu.VMEM((XN, 2, HALF, HD), BF16),
            pltpu.VMEM((XN, HD, ROWS), BF16),
            pltpu.VMEM((XN, ROWS, HD), BF16),
            pltpu.VMEM((XN, KEYS, ROWS), BF16),
            pltpu.VMEM((XN, KEYS, HD), BF16),
            pltpu.VMEM((XN, HD, KEYS), BF16),
            pltpu.VMEM((XN, KEYS, HD), BF16),
            pltpu.VMEM((XN, HD, KEYS), BF16),
            pltpu.VMEM((UNROLL, KEYS, RB), F32),
            pltpu.VMEM((XN, HD, ROWS), F32),
            pltpu.VMEM((XN, 3, 8, RB), F32),
            pltpu.VMEM((XN - 1, XN, 3, 8, RB), F32),
            pltpu.VMEM((XN, 8, RB), F32),
            pltpu.VMEM((XN, 8, RB), F32),
            pltpu.VMEM((2, XN, 2, HD, HALF), BF16),
            pltpu.VMEM((2, 2, 3, HD, HALF), BF16),
            pltpu.VMEM((XN, MEDIA, PART, HD), BF16),
            pltpu.VMEM((XN, MEDIA, PART, HD), BF16),
            pltpu.VMEM((2, 2, 7, 4, PART, HD), BF16),
            pltpu.VMEM((2, 2, 7, 4, PART, HD), BF16),
            pltpu.VMEM((2, 8, 2, 32, HD), BF16),
            pltpu.VMEM((2, HN, 2, 32, HD), BF16),
            pltpu.VMEM((8, HD), jnp.int32),
            pltpu.SMEM((8, HD), jnp.int32),
            dma,
            dma((2, 8)), dma((2, 8)),
            dma((2, 2, 7)), dma((2, 2, 7)),
            dma((2, 2, 3)), dma((2, 2, 3)),
            dma((4, 3)), dma((4, 3)),
            dma((2, 2, 3)), dma((2, 2, 3)),
            dma((2, 2, 7)), dma((2, 2, 7)),
            dma((2, 8)), dma((2, 8)),
        ],
        compiler_params=pltpu.CompilerParams(
            collective_id=0, has_side_effects=True, vmem_limit_bytes=60 * 1024 * 1024
        ),
        name="attend",
    )(media_list.T, media_count, image_slot, gate_logit, queries, d_gated, kv)
    d_image_kv = d_kv.reshape(2, 32, 2, HN * HD)
    return gated, d_queries, d_image_kv


def solution(mesh):
    return jax.shard_map(
        on_device,
        mesh=mesh,
        in_specs=(
            P("seq", "head"),
            P("seq", "head", None, None),
            P("head"),
            P("seq", "head"),
            P(),
            P(),
            P(),
        ),
        out_specs=(P("seq", "head"), P("seq", "head"), P("seq", "head", None, None)),
        check_vma=False,
    )
```

```python
import functools

import jax
import jax.numpy as jnp
from jax import lax
from jax.experimental import pallas as pl
from jax.experimental.pallas import tpu as pltpu
from jax.sharding import PartitionSpec as P

MESH = pl.DeviceIdType.MESH
HD = 128
XN = 4
ZN = 8
HN = 8
MEDIA = 16
LOWEST = 12
TOK = 192
ROWS = 1536
HALF = 768
RB = 256
KEYS = 1024
PART = 64
SLOTS = 64
MS = 256
UNROLL = 6
LOG2E = 1.4426950408889634
INV_ROOT = HD ** (-0.5)
F32 = jnp.float32
BF16 = jnp.bfloat16


def mod(value, n):
    return lax.rem(value + n, n)


def nt_dot(a, b):
    return lax.dot_general(a, b, (((1,), (1,)), ((), ())), preferred_element_type=F32)


def nn_dot(a, b):
    return jnp.dot(a, b, preferred_element_type=F32)


def kernel(
    media_ref, counts_ref, place_ref, gate_ref, q_ref, dg_ref, kv_ref,
    gated_ref, dq_ref, dkv_ref,
    kall, vall, qall, daall, dat, dap, pmat, kc, kt, vc, vt, sbuf, ot,
    stat, statin, fac, dlt, xo, xin, gk, gv, rout, rin, sums, fin, dkvin, inv_v, inv_ref, inv_sem,
    a2a_s, a2a_r, ag_s, ag_r, xg_s, xg_r, st_s, st_r, xr_s, xr_r, rs_s, rs_r, fa_s, fa_r,
):
    seq = lax.axis_index("seq")
    h = lax.axis_index("head")
    z = seq // XN
    x = lax.rem(seq, XN)
    hq = h // 2
    hp = lax.rem(h, 2)
    kv_all = (kall, vall)
    xg_all = (qall, daall)
    grads = (gk, gv)
    pending = []

    def dev(zz, xx, hh):
        return (zz * XN + xx, hh)

    def send(src, dst, ssem, rsem, device):
        copy = pltpu.make_async_remote_copy(
            src_ref=src, dst_ref=dst, send_sem=ssem, recv_sem=rsem, device_id=device, device_id_type=MESH
        )
        copy.start()
        pending.append(copy)

    def arrived(ref, sem):
        pltpu.make_async_copy(ref, ref, sem).wait()

    z_to = (mod(z + 1, ZN), mod(z - 1, ZN))
    x_to = (mod(x + 1, XN), mod(x - 1, XN))
    x_opp = mod(x + 2, XN)
    x_part = lax.rem(x + hq + 2 * hp, XN)
    self_in = x_part == x

    def holder(k, jj):
        return 2 * ((2 * XN - k - 2 * jj) % XN) + jj

    barrier = pltpu.get_barrier_semaphore()

    def greet(device):
        pl.semaphore_signal(barrier, inc=1, device_id=device, device_id_type=MESH)

    for k in range(1, HN):
        greet(dev(z, x_part, mod(h + k, HN)))
    for k in range(1, XN):
        greet(dev(z, mod(x + k, XN), h))
        for jj in range(2):
            greet(dev(z, mod(x + k, XN), holder(k, jj)))
    for jj in range(2):

        @pl.when(h != holder(0, jj))
        def _():
            greet(dev(z, x, holder(0, jj)))

    @pl.when(jnp.logical_not(self_in))
    def _():
        greet(dev(z, x_part, h))

    for d in range(2):
        greet(dev(z_to[d], x, h))
    pl.semaphore_wait(barrier, jnp.where(self_in, 19, 21))

    def kv_lanes(t, head):
        return kv_ref.at[:, :, pl.ds(pl.multiple_of((t * HN + head) * HD, HD), HD)]

    def a2a_copy(t, k):
        target = mod(h + k, HN)
        mine = kall if t == 0 else vall
        dst = mine.at[pl.ds(2 * seq, 2), hp]
        return pltpu.make_async_remote_copy(
            src_ref=kv_lanes(t, target), dst_ref=dst, send_sem=a2a_s.at[t, k],
            recv_sem=a2a_r.at[t, 2 * x + hp], device_id=dev(z, x_part, target), device_id_type=MESH,
        )

    for t in range(2):
        for k in range(1, HN):
            a2a_copy(t, k).start()

        @pl.when(jnp.logical_not(self_in))
        def _():
            a2a_copy(t, 0).start()

        @pl.when(self_in)
        def _():
            pltpu.make_async_copy(
                kv_lanes(t, h), kv_all[t].at[pl.ds(2 * seq, 2), hp], a2a_r.at[t, 2 * x + hp]
            ).start()

    def a2a_wait(t, sub):
        for xx in (2 * sub, 2 * sub + 1):
            for jj in range(2):
                arrived(kv_all[t].at[pl.ds(2 * (z * XN + xx), 2), jj], a2a_r.at[t, 2 * xx + jj])

    def xg_ref(t, c, half):
        return xg_all[t].at[c, half]

    def xg_first(t):
        for pos in range(2):
            for d in range(2):
                half = d if pos == 0 else 1 - d
                ref = xg_ref(t, x, half)
                send(ref, ref, xg_s.at[t, d, pos], xg_r.at[t, d, pos], dev(z, x_to[d], h))

    def xg_wait(t, d, pos):
        c = x_opp if pos == 2 else x_to[1 - d]
        half = 1 - d if pos == 1 else d
        arrived(xg_ref(t, c, half), xg_r.at[t, d, pos])

    def xg_forward(t):
        for d in range(2):
            xg_wait(t, d, 0)
            ref = xg_ref(t, x_to[1 - d], d)
            send(ref, ref, xg_s.at[t, d, 2], xg_r.at[t, d, 2], dev(z, x_to[d], h))

    def ag_ref(t, zz, d, pos):
        sub = d if pos == 0 else 1 - d
        return kv_all[t].at[pl.ds(zz * 8 + 4 * sub, 4)]

    def ag_send(t, k, pos, ways=(0, 1)):
        for d in ways:
            zz = mod(z - (k - 1), ZN) if d == 0 else mod(z + (k - 1), ZN)
            ref = ag_ref(t, zz, d, pos)
            i = 2 * (k - 1) + pos
            send(ref, ref, ag_s.at[t, d, i], ag_r.at[t, d, i], dev(z_to[d], x, h))

    def ag_wait(t, k, pos):
        for d in range(2):
            zz = mod(z - k, ZN) if d == 0 else mod(z + k, ZN)
            arrived(ag_ref(t, zz, d, pos), ag_r.at[t, d, 2 * (k - 1) + pos])

    def ag_pass(t, k, pos):
        ag_wait(t, k - 1, pos)
        ag_send(t, k, pos)

    def ag_step(t, k):
        for pos in range(1 if k == 4 else 2):
            ag_pass(t, k, pos)

    def ag_end(t):
        ag_wait(t, 3, 1)
        ag_wait(t, 4, 0)

    for g in range(8):
        rows = q_ref[:, g * HD : (g + 1) * HD]
        qall[x, g // 4, (g % 4) * TOK : (g % 4 + 1) * TOK, :] = rows
    xg_first(0)

    def gate_row(g):
        return jnp.tanh(jnp.full((1, HD), gate_ref[g], F32))

    for g in range(8):
        rows = dg_ref[:, g * HD : (g + 1) * HD].astype(F32) * gate_row(g)
        daall[x, g // 4, (g % 4) * TOK : (g % 4 + 1) * TOK, :] = rows.astype(BF16)
    stat[...] = jnp.ones_like(stat)

    lane = lax.broadcasted_iota(jnp.int32, (1, HD), 1)
    inv_v[...] = jnp.full((8, HD), -1, jnp.int32)
    for c in range(XN):
        found = jnp.full((1, HD), -1, jnp.int32)
        for j in range(MEDIA):
            slot = place_ref[media_ref[j, z * XN + c]]
            slot = jnp.where(j < counts_ref[z * XN + c], slot, -1)
            found = jnp.where(lane == slot, j, found)
        inv_v[c : c + 1, :] = found
    inv_copy = pltpu.make_async_copy(inv_v, inv_ref, inv_sem)
    inv_copy.start()

    for t in range(2):
        a2a_wait(t, 0)
        ag_send(t, 1, 0, (0,))
        a2a_wait(t, 1)
        ag_send(t, 1, 0, (1,))
        if t == 0:
            ag_send(0, 1, 1)
    xg_forward(0)
    xg_first(1)
    ag_step(0, 2)
    ag_send(1, 1, 1)
    ag_step(0, 3)
    ag_pass(1, 2, 0)
    ag_step(0, 4)
    ag_pass(1, 2, 1)
    inv_copy.wait()
    ag_end(0)

    def pick(src, dst, dst_t, c):
        segment = z * XN + c

        for j in range(MEDIA):
            slot = place_ref[media_ref[j, segment]]
            dst[c, j * PART : (j + 1) * PART, :] = src[slot].reshape(PART, HD)
        for ch in range(KEYS // 256):
            block = dst[c, ch * 256 : (ch + 1) * 256, :]
            dst_t[c, :, ch * 256 : (ch + 1) * 256] = block.T

    def lanes(rb):
        return pl.ds(pl.multiple_of(rb * RB, RB), RB)

    def probs_of(c):
        pick(kall, kc, kt, c)
        live = (counts_ref[z * XN + c] - LOWEST) * PART

        def block(i, carry):
            for r in range(UNROLL):
                rb = i * UNROLL + r
                q_rows = qall[c, rb // 3, pl.ds(pl.multiple_of(lax.rem(rb, 3) * RB, RB), RB), :]
                top = None
                for m in range(KEYS // MS):
                    rows = slice(m * MS, (m + 1) * MS)
                    s = nt_dot(kc[c, rows, :], q_rows)
                    if m == KEYS // MS - 1:
                        first = LOWEST * PART - m * MS
                        row_ids = lax.broadcasted_iota(jnp.int32, (KEYS - LOWEST * PART, RB), 0)
                        last = jnp.where(row_ids < live, s[first:], -1e30)
                        s = jnp.concatenate([s[:first], last], axis=0) if first else last
                    sbuf[r, rows, :] = s
                    here = jnp.max(s, axis=0, keepdims=True)
                    top = here if top is None else jnp.maximum(top, here)
                total = jnp.zeros((1, RB), F32)
                for ch in range(4):
                    rows = slice(ch * 256, (ch + 1) * 256)
                    p = jnp.exp2((sbuf[r, rows, :] - top) * (LOG2E * INV_ROOT))
                    total = total + jnp.sum(p, axis=0, keepdims=True)
                    pmat[c, rows, lanes(rb)] = p.astype(BF16)
                stat[c, 0, pl.ds(rb, 1), :] = top
                stat[c, 1, pl.ds(rb, 1), :] = total
            return carry

        lax.fori_loop(0, 6 // UNROLL, block, 0)

    def turn(c):
        for half in range(2):
            for r in range(3):
                rb = half * 3 + r
                dat[c, :, rb * RB : (rb + 1) * RB] = daall[c, half, r * RB : (r + 1) * RB, :].T

    def outs_of(c):
        pick(vall, vc, vt, c)

        def block(i, carry):
            for r in range(UNROLL):
                rb = i * UNROLL + r
                da_t = dat[c, :, lanes(rb)]
                o = nn_dot(vt[c], pmat[c, :, lanes(rb)])
                ot[c, :, lanes(rb)] = o
                stat[c, 2, pl.ds(rb, 1), :] = jnp.sum(da_t.astype(F32) * o, axis=0, keepdims=True)
            return carry

        lax.fori_loop(0, 6 // UNROLL, block, 0)

    def stat_send(c, i):
        for k in range(1, XN):
            send(
                stat.at[c], statin.at[k - 1, c], st_s.at[i, k - 1], st_r.at[i, k - 1],
                dev(z, mod(x + k, XN), h),
            )

    c_right, c_left = x_to
    xg_forward(1)
    turn(x)
    probs_of(x)
    ag_step(1, 3)
    xg_wait(0, 0, 1)
    probs_of(c_left)
    ag_step(1, 4)
    xg_wait(0, 1, 1)
    probs_of(c_right)
    for d in range(2):
        xg_wait(0, d, 2)
    probs_of(x_opp)
    xg_wait(1, 0, 1)
    turn(c_left)
    xg_wait(1, 1, 1)
    turn(c_right)
    for d in range(2):
        xg_wait(1, d, 2)
    turn(x_opp)
    ag_end(1)

    for c in range(XN):
        outs_of(c)
        stat_send(c, c)

    def stat_wait(c):
        for k in range(1, XN):
            arrived(statin.at[k - 1, c], st_r.at[c, k - 1])

    def combine(c):
        stat_wait(c)
        tops = [stat[c, 0]] + [statin[k, c, 0] for k in range(XN - 1)]
        totals = [stat[c, 1]] + [statin[k, c, 1] for k in range(XN - 1)]
        dots = [stat[c, 2]] + [statin[k, c, 2] for k in range(XN - 1)]
        top = functools.reduce(jnp.maximum, tops)
        scales = [jnp.exp2((one - top) * (LOG2E * INV_ROOT)) for one in tops]
        total = sum(a * b for a, b in zip(scales, totals))
        delta = sum(a * b for a, b in zip(scales, dots)) / total
        own = scales[0] / total
        fac[c] = own
        dlt[c] = delta * own

        def block(rb, carry):
            half = rb // 3
            f = fac[c, pl.ds(rb, 1), :]
            cols = pl.ds(pl.multiple_of(lax.rem(rb, 3) * RB, RB), RB)
            xo[0, c, half, :, cols] = (ot[c, :, lanes(rb)] * f).astype(BF16)
            scaled = (dat[c, :, lanes(rb)].astype(F32) * f).astype(BF16)
            dat[c, :, lanes(rb)] = scaled
            dap[c, pl.ds(pl.multiple_of(rb * RB, RB), RB), :] = scaled.T
            return carry

        lax.fori_loop(0, 6, block, 0, unroll=True)

    def xr_opp(t):
        for d in range(2):
            send(xo.at[t, x_opp, d], xin.at[t, d, 0], xr_s.at[t, d, 0], xr_r.at[t, d, 0], dev(z, x_to[d], h))

    def xr_near(t, d):
        send(
            xo.at[t, x_to[d], 1 - d], xin.at[t, d, 1], xr_s.at[t, d, 1], xr_r.at[t, d, 1], dev(z, x_to[d], h)
        )

    def xr_add(t):
        for d in range(2):
            arrived(xin.at[t, d, 0], xr_r.at[t, d, 0])
            both = xo[t, x_to[d], d].astype(F32) + xin[t, d, 0].astype(F32)
            xo[t, x_to[d], d] = both.astype(BF16)
            send(
                xo.at[t, x_to[d], d], xin.at[t, d, 2], xr_s.at[t, d, 2], xr_r.at[t, d, 2], dev(z, x_to[d], h)
            )

    def xr_end(t):
        for d in range(2):
            for i in (1, 2):
                arrived(xin.at[t, d, i], xr_r.at[t, d, i])

    def xr_rows(t, half):
        both = xo[t, x, half].astype(F32) + xin[t, half, 2].astype(F32) + xin[t, 1 - half, 1].astype(F32)
        return both.T

    for c in range(XN):
        combine(c)
    xr_opp(0)
    xr_near(0, 0)
    xr_near(0, 1)

    def value_grads(c):
        for m in range(KEYS // MS):
            part = nn_dot(pmat[c, m * MS : (m + 1) * MS, :], dap[c])
            gv[c, m * MS // PART : (m + 1) * MS // PART] = part.astype(BF16).reshape(MS // PART, PART, HD)

    def over_segments(f):
        def one(c, carry):
            f(c)
            return carry

        lax.fori_loop(0, XN, one, 0)

    over_segments(value_grads)

    def own_part(t, slot):
        out = None
        for c in range(XN):
            entry = inv_ref[c, slot]
            block = grads[t][c, jnp.maximum(entry, 0)].astype(F32)
            block = jnp.where(entry >= 0, block, 0.0)
            out = block if out is None else out + block
        return out

    def rs_prep(t):
        def one(i, carry):
            for r in range(8):
                slot = i * 8 + r
                sums[t, slot] = own_part(t, slot)
            return carry

        lax.fori_loop(0, SLOTS // 8, one, 0)

    def rs_step(t, i):
        k = (i + 3) // 2
        for d in range(2):
            away = 5 - k
            zt = mod(z + away, ZN) if d == 0 else mod(z - away, ZN)
            sub = d if i % 2 == 0 else 1 - d
            if i >= 2:
                arrived(rin.at[t, d, i - 2], rs_r.at[t, d, i - 2])

            first = zt * 8 + 4 * sub
            if i < 2:
                for sl in range(4):
                    rout[t, d, i, sl] = own_part(t, first + sl).astype(BF16)
            else:
                both = sums[t, pl.ds(first, 4)] + rin[t, d, i - 2].astype(F32)
                rout[t, d, i] = both.astype(BF16)
            send(rout.at[t, d, i], rin.at[t, d, i], rs_s.at[t, d, i], rs_r.at[t, d, i], dev(z_to[d], x, h))

    def rs_end(t):
        for i in (5, 6):
            for d in range(2):
                arrived(rin.at[t, d, i], rs_r.at[t, d, i])
        for sub in range(2):
            part = sums[t, pl.ds(z * 8 + 4 * sub, 4)]
            for d in range(2):
                part = part + rin[t, d, 6 if sub == d else 5].astype(F32)
            fin[t, 4 * sub : 4 * sub + 4] = part.astype(BF16).reshape(4, 2, 32, HD)

    def fa_copy(t, k, jj):
        target = mod(x + k, XN)
        return pltpu.make_async_remote_copy(
            src_ref=fin.at[t, pl.ds(2 * target, 2), jj], dst_ref=dkvin.at[t, h], send_sem=fa_s.at[t, 2 * k + jj],
            recv_sem=fa_r.at[t, h], device_id=dev(z, target, holder(k, jj)), device_id_type=MESH,
        )

    def fa_start(t):
        for k in range(XN):
            for jj in range(2):
                if k:
                    fa_copy(t, k, jj).start()
                    continue
                own = h == holder(0, jj)

                @pl.when(jnp.logical_not(own))
                def _():
                    fa_copy(t, k, jj).start()

                @pl.when(own)
                def _():
                    pltpu.make_async_copy(fin.at[t, pl.ds(2 * x, 2), jj], dkvin.at[t, h], fa_r.at[t, h]).start()

    def fa_end(t):
        for hh in range(HN):
            arrived(dkvin.at[t, hh], fa_r.at[t, hh])

    def key_grads(c):
        def block(i, carry):
            for r in range(UNROLL):
                rb = i * UNROLL + r
                da_t = dat[c, :, lanes(rb)]
                d_row = dlt[c, pl.ds(rb, 1), :]
                for m in range(KEYS // MS):
                    rows = slice(m * MS, (m + 1) * MS)
                    dp = nn_dot(vc[c, rows, :], da_t) - d_row
                    ds = pmat[c, rows, lanes(rb)].astype(F32) * dp
                    pmat[c, rows, lanes(rb)] = ds.astype(BF16)
            return carry

        lax.fori_loop(0, 6 // UNROLL, block, 0)
        for m in range(KEYS // MS):
            part = nn_dot(pmat[c, m * MS : (m + 1) * MS, :], qall[c].reshape(ROWS, HD)) * INV_ROOT
            gk[c, m * MS // PART : (m + 1) * MS // PART] = part.astype(BF16).reshape(MS // PART, PART, HD)

    def query_grads(c):
        def block(i, carry):
            for r in range(UNROLL):
                rb = i * UNROLL + r
                part = nn_dot(kt[c], pmat[c, :, lanes(rb)]) * INV_ROOT
                cols = pl.ds(pl.multiple_of(lax.rem(rb, 3) * RB, RB), RB)
                xo[1, c, rb // 3, :, cols] = part.astype(BF16)
            return carry

        lax.fori_loop(0, 6 // UNROLL, block, 0)

    rs_step(1, 0)
    rs_step(1, 1)
    rs_prep(1)
    key_grads(x_opp)
    rs_step(1, 2)
    xr_add(0)
    key_grads(c_right)
    rs_step(1, 3)
    query_grads(x_opp)
    xr_opp(1)
    rs_step(1, 4)
    key_grads(c_left)
    rs_step(1, 5)
    key_grads(x)
    rs_step(0, 0)
    rs_step(0, 1)
    rs_step(1, 6)
    rs_prep(0)
    query_grads(c_right)
    xr_near(1, 0)
    query_grads(c_left)
    xr_near(1, 1)
    rs_step(0, 2)
    rs_step(0, 3)
    rs_end(1)
    fa_start(1)
    query_grads(x)
    rs_step(0, 4)
    xr_add(1)
    rs_step(0, 5)
    xr_end(0)
    for half in range(2):
        rows = xr_rows(0, half)
        for gg in range(4):
            g = half * 4 + gg
            gated_ref[:, g * HD : (g + 1) * HD] = (rows[gg * TOK : (gg + 1) * TOK, :] * gate_row(g)).astype(BF16)
    rs_step(0, 6)
    rs_end(0)
    fa_start(0)
    xr_end(1)
    for half in range(2):
        rows = xr_rows(1, half)
        for gg in range(4):
            g = half * 4 + gg
            dq_ref[:, g * HD : (g + 1) * HD] = rows[gg * TOK : (gg + 1) * TOK, :].astype(BF16)
    for t in (1, 0):
        fa_end(t)
        for hh in range(HN):
            dkv_ref[:, :, (t * HN + hh) * HD : (t * HN + hh + 1) * HD] = dkvin[t, hh]

    for copy in pending:
        copy.wait_send()
    for t in range(2):
        for k in range(1, HN):
            a2a_copy(t, k).wait_send()

        @pl.when(jnp.logical_not(self_in))
        def _():
            a2a_copy(t, 0).wait_send()

        for k in range(XN):
            for jj in range(2):
                if k:
                    fa_copy(t, k, jj).wait_send()
                    continue

                @pl.when(h != holder(0, jj))
                def _():
                    fa_copy(t, k, jj).wait_send()


def on_device(queries, image_kv, gate_logit, d_gated, media_list, media_count, image_slot):
    kv = image_kv.reshape(2, 32, 2 * HN * HD)
    smem = pl.BlockSpec(memory_space=pltpu.SMEM)
    vmem = pl.BlockSpec(memory_space=pltpu.VMEM)
    dma = pltpu.SemaphoreType.DMA
    gated, d_queries, d_kv = pl.pallas_call(
        kernel,
        out_shape=(
            jax.ShapeDtypeStruct((TOK, HN * HD), BF16),
            jax.ShapeDtypeStruct((TOK, HN * HD), BF16),
            jax.ShapeDtypeStruct((2, 32, 2 * HN * HD), BF16),
        ),
        in_specs=[smem] * 4 + [vmem] * 3,
        out_specs=(vmem,) * 3,
        scratch_shapes=[
            pltpu.VMEM((SLOTS, 2, 32, HD), BF16),
            pltpu.VMEM((SLOTS, 2, 32, HD), BF16),
            pltpu.VMEM((XN, 2, HALF, HD), BF16),
            pltpu.VMEM((XN, 2, HALF, HD), BF16),
            pltpu.VMEM((XN, HD, ROWS), BF16),
            pltpu.VMEM((XN, ROWS, HD), BF16),
            pltpu.VMEM((XN, KEYS, ROWS), BF16),
            pltpu.VMEM((XN, KEYS, HD), BF16),
            pltpu.VMEM((XN, HD, KEYS), BF16),
            pltpu.VMEM((XN, KEYS, HD), BF16),
            pltpu.VMEM((XN, HD, KEYS), BF16),
            pltpu.VMEM((UNROLL, KEYS, RB), F32),
            pltpu.VMEM((XN, HD, ROWS), F32),
            pltpu.VMEM((XN, 3, 8, RB), F32),
            pltpu.VMEM((XN - 1, XN, 3, 8, RB), F32),
            pltpu.VMEM((XN, 8, RB), F32),
            pltpu.VMEM((XN, 8, RB), F32),
            pltpu.VMEM((2, XN, 2, HD, HALF), BF16),
            pltpu.VMEM((2, 2, 3, HD, HALF), BF16),
            pltpu.VMEM((XN, MEDIA, PART, HD), BF16),
            pltpu.VMEM((XN, MEDIA, PART, HD), BF16),
            pltpu.VMEM((2, 2, 7, 4, PART, HD), BF16),
            pltpu.VMEM((2, 2, 7, 4, PART, HD), BF16),
            pltpu.VMEM((2, SLOTS, PART, HD), F32),
            pltpu.VMEM((2, 8, 2, 32, HD), BF16),
            pltpu.VMEM((2, HN, 2, 32, HD), BF16),
            pltpu.VMEM((8, HD), jnp.int32),
            pltpu.SMEM((8, HD), jnp.int32),
            dma,
            dma((2, 8)), dma((2, 8)),
            dma((2, 2, 7)), dma((2, 2, 7)),
            dma((2, 2, 3)), dma((2, 2, 3)),
            dma((4, 3)), dma((4, 3)),
            dma((2, 2, 3)), dma((2, 2, 3)),
            dma((2, 2, 7)), dma((2, 2, 7)),
            dma((2, 8)), dma((2, 8)),
        ],
        compiler_params=pltpu.CompilerParams(
            collective_id=0, has_side_effects=True, vmem_limit_bytes=60 * 1024 * 1024
        ),
        name="attend",
    )(media_list.T, media_count, image_slot, gate_logit, queries, d_gated, kv)
    d_image_kv = d_kv.reshape(2, 32, 2, HN * HD)
    return gated, d_queries, d_image_kv


def solution(mesh):
    return jax.shard_map(
        on_device,
        mesh=mesh,
        in_specs=(
            P("seq", "head"),
            P("seq", "head", None, None),
            P("head"),
            P("seq", "head"),
            P(),
            P(),
            P(),
        ),
        out_specs=(P("seq", "head"), P("seq", "head"), P("seq", "head", None, None)),
        check_vma=False,
    )
```

```python
import functools

import jax
import jax.numpy as jnp
from jax import lax
from jax.experimental import pallas as pl
from jax.experimental.pallas import tpu as pltpu
from jax.sharding import PartitionSpec as P

MESH = pl.DeviceIdType.MESH
HD = 128
XN = 4
ZN = 8
HN = 8
MEDIA = 16
LOWEST = 12
TOK = 192
ROWS = 1536
HALF = 768
RB = 256
KEYS = 1024
PART = 64
SLOTS = 64
MS = 256
UNROLL = 6
LOG2E = 1.4426950408889634
INV_ROOT = HD ** (-0.5)
F32 = jnp.float32
BF16 = jnp.bfloat16


def mod(value, n):
    return lax.rem(value + n, n)


def nt_dot(a, b):
    return lax.dot_general(a, b, (((1,), (1,)), ((), ())), preferred_element_type=F32)


def nn_dot(a, b):
    return jnp.dot(a, b, preferred_element_type=F32)


def kernel(
    media_ref, counts_ref, place_ref, gate_ref, q_ref, dg_ref, kv_ref,
    gated_ref, dq_ref, dkv_ref,
    kall, vall, qall, daall, dat, dap, pmat, kc, kt, vc, vt, sbuf, ot,
    stat, statin, fac, dlt, xo, xin, gk, gv, rout, rin, sums, fin, dkvin, kvlin, inv_v, inv_ref, inv_sem,
    a2a_s, a2a_r, ag_s, ag_r, xg_s, xg_r, st_s, st_r, xr_s, xr_r, rs_s, rs_r, fa_s, fa_r,
):
    seq = lax.axis_index("seq")
    h = lax.axis_index("head")
    z = seq // XN
    x = lax.rem(seq, XN)
    hq = h // 2
    hp = lax.rem(h, 2)
    kv_all = (kall, vall)
    xg_all = (qall, daall)
    grads = (gk, gv)
    pending = []

    def dev(zz, xx, hh):
        return (zz * XN + xx, hh)

    def send(src, dst, ssem, rsem, device):
        copy = pltpu.make_async_remote_copy(
            src_ref=src, dst_ref=dst, send_sem=ssem, recv_sem=rsem, device_id=device, device_id_type=MESH
        )
        copy.start()
        pending.append(copy)

    def arrived(ref, sem):
        pltpu.make_async_copy(ref, ref, sem).wait()

    z_to = (mod(z + 1, ZN), mod(z - 1, ZN))
    x_to = (mod(x + 1, XN), mod(x - 1, XN))
    x_opp = mod(x + 2, XN)
    x_part = lax.rem(x + hq + 2 * hp, XN)
    self_in = x_part == x

    def holder(k, jj):
        return 2 * ((2 * XN - k - 2 * jj) % XN) + jj

    barrier = pltpu.get_barrier_semaphore()

    def greet(device):
        pl.semaphore_signal(barrier, inc=1, device_id=device, device_id_type=MESH)

    for k in range(1, HN):
        greet(dev(z, x_part, mod(h + k, HN)))
    for k in range(1, XN):
        greet(dev(z, mod(x + k, XN), h))
        for jj in range(2):
            greet(dev(z, mod(x + k, XN), holder(k, jj)))
    for jj in range(2):

        @pl.when(h != holder(0, jj))
        def _():
            greet(dev(z, x, holder(0, jj)))

    @pl.when(jnp.logical_not(self_in))
    def _():
        greet(dev(z, x_part, h))

    for d in range(2):
        greet(dev(z_to[d], x, h))
    for i in range(2):
        for t in range(2):
            kvlin[i, :, t * HN * HD : (t + 1) * HN * HD] = kv_ref[i, :, t, :]
    for g in range(8):
        rows = q_ref[:, g * HD : (g + 1) * HD]
        qall[x, g // 4, (g % 4) * TOK : (g % 4 + 1) * TOK, :] = rows

    def gate_row(g):
        return jnp.tanh(jnp.full((1, HD), gate_ref[g], F32))

    for g in range(8):
        rows = dg_ref[:, g * HD : (g + 1) * HD].astype(F32) * gate_row(g)
        daall[x, g // 4, (g % 4) * TOK : (g % 4 + 1) * TOK, :] = rows.astype(BF16)
    stat[...] = jnp.ones_like(stat)

    lane = lax.broadcasted_iota(jnp.int32, (1, HD), 1)
    inv_v[...] = jnp.full((8, HD), -1, jnp.int32)
    for c in range(XN):
        found = jnp.full((1, HD), -1, jnp.int32)
        for j in range(MEDIA):
            slot = place_ref[media_ref[j, z * XN + c]]
            slot = jnp.where(j < counts_ref[z * XN + c], slot, -1)
            found = jnp.where(lane == slot, j, found)
        inv_v[c : c + 1, :] = found
    inv_copy = pltpu.make_async_copy(inv_v, inv_ref, inv_sem)

    pl.semaphore_wait(barrier, jnp.where(self_in, 19, 21))

    def kv_lanes(t, head):
        return kvlin.at[:, :, pl.ds(pl.multiple_of((t * HN + head) * HD, HD), HD)]

    def a2a_copy(t, k):
        target = mod(h + k, HN)
        mine = kall if t == 0 else vall
        dst = mine.at[pl.ds(2 * seq, 2), hp]
        return pltpu.make_async_remote_copy(
            src_ref=kv_lanes(t, target), dst_ref=dst, send_sem=a2a_s.at[t, k],
            recv_sem=a2a_r.at[t, 2 * x + hp], device_id=dev(z, x_part, target), device_id_type=MESH,
        )

    for t in range(2):
        for k in range(1, HN):
            a2a_copy(t, k).start()

        @pl.when(jnp.logical_not(self_in))
        def _():
            a2a_copy(t, 0).start()

        @pl.when(self_in)
        def _():
            pltpu.make_async_copy(
                kv_lanes(t, h), kv_all[t].at[pl.ds(2 * seq, 2), hp], a2a_r.at[t, 2 * x + hp]
            ).start()

    def a2a_wait(t, sub):
        for xx in (2 * sub, 2 * sub + 1):
            for jj in range(2):
                arrived(kv_all[t].at[pl.ds(2 * (z * XN + xx), 2), jj], a2a_r.at[t, 2 * xx + jj])

    def xg_ref(t, c, half):
        return xg_all[t].at[c, half]

    def xg_first(t):
        for pos in range(2):
            for d in range(2):
                half = d if pos == 0 else 1 - d
                ref = xg_ref(t, x, half)
                send(ref, ref, xg_s.at[t, d, pos], xg_r.at[t, d, pos], dev(z, x_to[d], h))

    def xg_wait(t, d, pos):
        c = x_opp if pos == 2 else x_to[1 - d]
        half = 1 - d if pos == 1 else d
        arrived(xg_ref(t, c, half), xg_r.at[t, d, pos])

    def xg_forward(t):
        for d in range(2):
            xg_wait(t, d, 0)
            ref = xg_ref(t, x_to[1 - d], d)
            send(ref, ref, xg_s.at[t, d, 2], xg_r.at[t, d, 2], dev(z, x_to[d], h))

    def ag_ref(t, zz, d, pos):
        sub = d if pos == 0 else 1 - d
        return kv_all[t].at[pl.ds(zz * 8 + 4 * sub, 4)]

    def ag_send(t, k, pos, ways=(0, 1)):
        for d in ways:
            zz = mod(z - (k - 1), ZN) if d == 0 else mod(z + (k - 1), ZN)
            ref = ag_ref(t, zz, d, pos)
            i = 2 * (k - 1) + pos
            send(ref, ref, ag_s.at[t, d, i], ag_r.at[t, d, i], dev(z_to[d], x, h))

    def ag_wait(t, k, pos):
        for d in range(2):
            zz = mod(z - k, ZN) if d == 0 else mod(z + k, ZN)
            arrived(ag_ref(t, zz, d, pos), ag_r.at[t, d, 2 * (k - 1) + pos])

    def ag_pass(t, k, pos):
        ag_wait(t, k - 1, pos)
        ag_send(t, k, pos)

    def ag_step(t, k):
        for pos in range(1 if k == 4 else 2):
            ag_pass(t, k, pos)

    def ag_end(t):
        ag_wait(t, 3, 1)
        ag_wait(t, 4, 0)

    xg_first(0)
    inv_copy.start()

    for t in range(2):
        a2a_wait(t, 0)
        ag_send(t, 1, 0, (0,))
        a2a_wait(t, 1)
        ag_send(t, 1, 0, (1,))
        if t == 0:
            ag_send(0, 1, 1)
    xg_forward(0)
    xg_first(1)
    ag_step(0, 2)
    ag_send(1, 1, 1)
    ag_step(0, 3)
    ag_pass(1, 2, 0)
    ag_step(0, 4)
    ag_pass(1, 2, 1)
    inv_copy.wait()
    ag_end(0)

    def pick(src, dst, dst_t, c):
        segment = z * XN + c

        for j in range(MEDIA):
            slot = place_ref[media_ref[j, segment]]
            dst[c, j * PART : (j + 1) * PART, :] = src[slot].reshape(PART, HD)
        for ch in range(KEYS // 256):
            block = dst[c, ch * 256 : (ch + 1) * 256, :]
            dst_t[c, :, ch * 256 : (ch + 1) * 256] = block.T

    def lanes(rb):
        return pl.ds(pl.multiple_of(rb * RB, RB), RB)

    def probs_of(c):
        pick(kall, kc, kt, c)
        live = (counts_ref[z * XN + c] - LOWEST) * PART

        def block(i, carry):
            for r in range(UNROLL):
                rb = i * UNROLL + r
                q_rows = qall[c, rb // 3, pl.ds(pl.multiple_of(lax.rem(rb, 3) * RB, RB), RB), :]
                top = None
                for m in range(KEYS // MS):
                    rows = slice(m * MS, (m + 1) * MS)
                    s = nt_dot(kc[c, rows, :], q_rows)
                    if m == KEYS // MS - 1:
                        first = LOWEST * PART - m * MS
                        row_ids = lax.broadcasted_iota(jnp.int32, (KEYS - LOWEST * PART, RB), 0)
                        last = jnp.where(row_ids < live, s[first:], -1e30)
                        s = jnp.concatenate([s[:first], last], axis=0) if first else last
                    sbuf[r, rows, :] = s
                    here = jnp.max(s, axis=0, keepdims=True)
                    top = here if top is None else jnp.maximum(top, here)
                total = jnp.zeros((1, RB), F32)
                for ch in range(4):
                    rows = slice(ch * 256, (ch + 1) * 256)
                    p = jnp.exp2((sbuf[r, rows, :] - top) * (LOG2E * INV_ROOT))
                    total = total + jnp.sum(p, axis=0, keepdims=True)
                    pmat[c, rows, lanes(rb)] = p.astype(BF16)
                stat[c, 0, pl.ds(rb, 1), :] = top
                stat[c, 1, pl.ds(rb, 1), :] = total
            return carry

        lax.fori_loop(0, 6 // UNROLL, block, 0)

    def turn(c):
        for half in range(2):
            for r in range(3):
                rb = half * 3 + r
                dat[c, :, rb * RB : (rb + 1) * RB] = daall[c, half, r * RB : (r + 1) * RB, :].T

    def outs_of(c):
        pick(vall, vc, vt, c)

        def block(i, carry):
            for r in range(UNROLL):
                rb = i * UNROLL + r
                da_t = dat[c, :, lanes(rb)]
                o = nn_dot(vt[c], pmat[c, :, lanes(rb)])
                ot[c, :, lanes(rb)] = o
                stat[c, 2, pl.ds(rb, 1), :] = jnp.sum(da_t.astype(F32) * o, axis=0, keepdims=True)
            return carry

        lax.fori_loop(0, 6 // UNROLL, block, 0)

    def stat_send(c, i):
        for k in range(1, XN):
            send(
                stat.at[c], statin.at[k - 1, c], st_s.at[i, k - 1], st_r.at[i, k - 1],
                dev(z, mod(x + k, XN), h),
            )

    c_right, c_left = x_to
    xg_forward(1)
    turn(x)
    probs_of(x)
    ag_step(1, 3)
    xg_wait(0, 0, 1)
    probs_of(c_left)
    ag_step(1, 4)
    xg_wait(0, 1, 1)
    probs_of(c_right)
    for d in range(2):
        xg_wait(0, d, 2)
    probs_of(x_opp)
    xg_wait(1, 0, 1)
    turn(c_left)
    xg_wait(1, 1, 1)
    turn(c_right)
    for d in range(2):
        xg_wait(1, d, 2)
    turn(x_opp)
    ag_end(1)

    for c in range(XN):
        outs_of(c)
        stat_send(c, c)

    def stat_wait(c):
        for k in range(1, XN):
            arrived(statin.at[k - 1, c], st_r.at[c, k - 1])

    def combine(c):
        stat_wait(c)
        tops = [stat[c, 0]] + [statin[k, c, 0] for k in range(XN - 1)]
        totals = [stat[c, 1]] + [statin[k, c, 1] for k in range(XN - 1)]
        dots = [stat[c, 2]] + [statin[k, c, 2] for k in range(XN - 1)]
        top = functools.reduce(jnp.maximum, tops)
        scales = [jnp.exp2((one - top) * (LOG2E * INV_ROOT)) for one in tops]
        total = sum(a * b for a, b in zip(scales, totals))
        delta = sum(a * b for a, b in zip(scales, dots)) / total
        own = scales[0] / total
        fac[c] = own
        dlt[c] = delta * own

        def block(rb, carry):
            half = rb // 3
            f = fac[c, pl.ds(rb, 1), :]
            cols = pl.ds(pl.multiple_of(lax.rem(rb, 3) * RB, RB), RB)
            xo[0, c, half, :, cols] = (ot[c, :, lanes(rb)] * f).astype(BF16)
            scaled = (dat[c, :, lanes(rb)].astype(F32) * f).astype(BF16)
            dat[c, :, lanes(rb)] = scaled
            dap[c, pl.ds(pl.multiple_of(rb * RB, RB), RB), :] = scaled.T
            return carry

        lax.fori_loop(0, 6, block, 0, unroll=True)

    def xr_opp(t):
        for d in range(2):
            send(xo.at[t, x_opp, d], xin.at[t, d, 0], xr_s.at[t, d, 0], xr_r.at[t, d, 0], dev(z, x_to[d], h))

    def xr_near(t, d):
        send(
            xo.at[t, x_to[d], 1 - d], xin.at[t, d, 1], xr_s.at[t, d, 1], xr_r.at[t, d, 1], dev(z, x_to[d], h)
        )

    def xr_add(t):
        for d in range(2):
            arrived(xin.at[t, d, 0], xr_r.at[t, d, 0])
            both = xo[t, x_to[d], d].astype(F32) + xin[t, d, 0].astype(F32)
            xo[t, x_to[d], d] = both.astype(BF16)
            send(
                xo.at[t, x_to[d], d], xin.at[t, d, 2], xr_s.at[t, d, 2], xr_r.at[t, d, 2], dev(z, x_to[d], h)
            )

    def xr_end(t):
        for d in range(2):
            for i in (1, 2):
                arrived(xin.at[t, d, i], xr_r.at[t, d, i])

    def xr_rows(t, half):
        both = xo[t, x, half].astype(F32) + xin[t, half, 2].astype(F32) + xin[t, 1 - half, 1].astype(F32)
        return both.T

    for c in range(XN):
        combine(c)
    xr_opp(0)
    xr_near(0, 0)
    xr_near(0, 1)

    def value_grads(c):
        for m in range(KEYS // MS):
            part = nn_dot(pmat[c, m * MS : (m + 1) * MS, :], dap[c])
            gv[c, m * MS // PART : (m + 1) * MS // PART] = part.astype(BF16).reshape(MS // PART, PART, HD)

    def over_segments(f):
        def one(c, carry):
            f(c)
            return carry

        lax.fori_loop(0, XN, one, 0)

    over_segments(value_grads)

    def own_part(t, slot):
        out = None
        for c in range(XN):
            entry = inv_ref[c, slot]
            block = grads[t][c, jnp.maximum(entry, 0)].astype(F32)
            block = jnp.where(entry >= 0, block, 0.0)
            out = block if out is None else out + block
        return out

    def rs_prep(t):
        def one(i, carry):
            for r in range(8):
                slot = i * 8 + r
                sums[t, slot] = own_part(t, slot)
            return carry

        lax.fori_loop(0, SLOTS // 8, one, 0)

    def rs_step(t, i):
        away = 5 - (i + 3) // 2
        for m in range(2):
            for d in range(2):
                zt = mod(z + away, ZN) if d == 0 else mod(z - away, ZN)
                sub = d if i % 2 == 0 else 1 - d
                first = zt * 8 + 4 * sub + 2 * m
                j = 2 * i + m
                if i < 2:
                    for sl in range(2):
                        rout[t, d, j, sl] = own_part(t, first + sl).astype(BF16)
                else:
                    arrived(rin.at[t, d, j - 4], rs_r.at[t, d, j - 4])
                    both = sums[t, pl.ds(first, 2)] + rin[t, d, j - 4].astype(F32)
                    rout[t, d, j] = both.astype(BF16)
                send(rout.at[t, d, j], rin.at[t, d, j], rs_s.at[t, d, j], rs_r.at[t, d, j], dev(z_to[d], x, h))

    def rs_end(t):
        for j in range(10, 14):
            for d in range(2):
                arrived(rin.at[t, d, j], rs_r.at[t, d, j])
        for sub in range(2):
            for m in range(2):
                first = 4 * sub + 2 * m
                part = sums[t, pl.ds(z * 8 + first, 2)]
                for d in range(2):
                    part = part + rin[t, d, (12 if sub == d else 10) + m].astype(F32)
                fin[t, first : first + 2] = part.astype(BF16).reshape(2, 2, 32, HD)

    def fa_copy(t, k, jj):
        target = mod(x + k, XN)
        return pltpu.make_async_remote_copy(
            src_ref=fin.at[t, pl.ds(2 * target, 2), jj], dst_ref=dkvin.at[t, h], send_sem=fa_s.at[t, 2 * k + jj],
            recv_sem=fa_r.at[t, h], device_id=dev(z, target, holder(k, jj)), device_id_type=MESH,
        )

    def fa_start(t):
        for k in range(XN):
            for jj in range(2):
                if k:
                    fa_copy(t, k, jj).start()
                    continue
                own = h == holder(0, jj)

                @pl.when(jnp.logical_not(own))
                def _():
                    fa_copy(t, k, jj).start()

                @pl.when(own)
                def _():
                    pltpu.make_async_copy(fin.at[t, pl.ds(2 * x, 2), jj], dkvin.at[t, h], fa_r.at[t, h]).start()

    def fa_end(t):
        for hh in range(HN):
            arrived(dkvin.at[t, hh], fa_r.at[t, hh])

    def key_grads(c):
        def block(i, carry):
            for r in range(UNROLL):
                rb = i * UNROLL + r
                da_t = dat[c, :, lanes(rb)]
                d_row = dlt[c, pl.ds(rb, 1), :]
                for m in range(KEYS // MS):
                    rows = slice(m * MS, (m + 1) * MS)
                    dp = nn_dot(vc[c, rows, :], da_t) - d_row
                    ds = pmat[c, rows, lanes(rb)].astype(F32) * dp
                    pmat[c, rows, lanes(rb)] = ds.astype(BF16)
            return carry

        lax.fori_loop(0, 6 // UNROLL, block, 0)
        for m in range(KEYS // MS):
            part = nn_dot(pmat[c, m * MS : (m + 1) * MS, :], qall[c].reshape(ROWS, HD)) * INV_ROOT
            gk[c, m * MS // PART : (m + 1) * MS // PART] = part.astype(BF16).reshape(MS // PART, PART, HD)

    def query_grads(c):
        def block(i, carry):
            for r in range(UNROLL):
                rb = i * UNROLL + r
                part = nn_dot(kt[c], pmat[c, :, lanes(rb)]) * INV_ROOT
                cols = pl.ds(pl.multiple_of(lax.rem(rb, 3) * RB, RB), RB)
                xo[1, c, rb // 3, :, cols] = part.astype(BF16)
            return carry

        lax.fori_loop(0, 6 // UNROLL, block, 0)

    rs_step(1, 0)
    rs_step(1, 1)
    rs_prep(1)
    key_grads(x_opp)
    key_grads(c_right)
    rs_step(1, 2)
    xr_add(0)
    rs_step(1, 3)
    query_grads(x_opp)
    xr_opp(1)
    key_grads(c_left)
    key_grads(x)
    rs_step(0, 0)
    rs_step(0, 1)
    rs_step(1, 4)
    rs_prep(0)
    query_grads(c_right)
    xr_near(1, 0)
    query_grads(c_left)
    xr_near(1, 1)
    rs_step(0, 2)
    rs_step(0, 3)
    rs_step(1, 5)
    query_grads(x)
    rs_step(0, 4)
    rs_step(0, 5)
    rs_step(1, 6)
    xr_add(1)
    xr_end(0)
    for half in range(2):
        rows = xr_rows(0, half)
        for gg in range(4):
            g = half * 4 + gg
            gated_ref[:, g * HD : (g + 1) * HD] = (rows[gg * TOK : (gg + 1) * TOK, :] * gate_row(g)).astype(BF16)
    rs_step(0, 6)
    rs_end(1)
    fa_start(1)
    rs_end(0)
    fa_start(0)
    xr_end(1)
    for half in range(2):
        rows = xr_rows(1, half)
        for gg in range(4):
            g = half * 4 + gg
            dq_ref[:, g * HD : (g + 1) * HD] = rows[gg * TOK : (gg + 1) * TOK, :].astype(BF16)
    for t in (1, 0):
        fa_end(t)
        for hh in range(HN):
            dkv_ref[:, :, t, hh * HD : (hh + 1) * HD] = dkvin[t, hh]

    for copy in pending:
        copy.wait_send()
    for t in range(2):
        for k in range(1, HN):
            a2a_copy(t, k).wait_send()

        @pl.when(jnp.logical_not(self_in))
        def _():
            a2a_copy(t, 0).wait_send()

        for k in range(XN):
            for jj in range(2):
                if k:
                    fa_copy(t, k, jj).wait_send()
                    continue

                @pl.when(h != holder(0, jj))
                def _():
                    fa_copy(t, k, jj).wait_send()


def on_device(queries, image_kv, gate_logit, d_gated, media_list, media_count, image_slot):
    smem = pl.BlockSpec(memory_space=pltpu.SMEM)
    vmem = pl.BlockSpec(memory_space=pltpu.VMEM)
    dma = pltpu.SemaphoreType.DMA
    return pl.pallas_call(
        kernel,
        out_shape=(
            jax.ShapeDtypeStruct((TOK, HN * HD), BF16),
            jax.ShapeDtypeStruct((TOK, HN * HD), BF16),
            jax.ShapeDtypeStruct((2, 32, 2, HN * HD), BF16),
        ),
        in_specs=[smem] * 4 + [vmem] * 3,
        out_specs=(vmem,) * 3,
        scratch_shapes=[
            pltpu.VMEM((SLOTS, 2, 32, HD), BF16),
            pltpu.VMEM((SLOTS, 2, 32, HD), BF16),
            pltpu.VMEM((XN, 2, HALF, HD), BF16),
            pltpu.VMEM((XN, 2, HALF, HD), BF16),
            pltpu.VMEM((XN, HD, ROWS), BF16),
            pltpu.VMEM((XN, ROWS, HD), BF16),
            pltpu.VMEM((XN, KEYS, ROWS), BF16),
            pltpu.VMEM((XN, KEYS, HD), BF16),
            pltpu.VMEM((XN, HD, KEYS), BF16),
            pltpu.VMEM((XN, KEYS, HD), BF16),
            pltpu.VMEM((XN, HD, KEYS), BF16),
            pltpu.VMEM((UNROLL, KEYS, RB), F32),
            pltpu.VMEM((XN, HD, ROWS), F32),
            pltpu.VMEM((XN, 3, 8, RB), F32),
            pltpu.VMEM((XN - 1, XN, 3, 8, RB), F32),
            pltpu.VMEM((XN, 8, RB), F32),
            pltpu.VMEM((XN, 8, RB), F32),
            pltpu.VMEM((2, XN, 2, HD, HALF), BF16),
            pltpu.VMEM((2, 2, 3, HD, HALF), BF16),
            pltpu.VMEM((XN, MEDIA, PART, HD), BF16),
            pltpu.VMEM((XN, MEDIA, PART, HD), BF16),
            pltpu.VMEM((2, 2, 14, 2, PART, HD), BF16),
            pltpu.VMEM((2, 2, 14, 2, PART, HD), BF16),
            pltpu.VMEM((2, SLOTS, PART, HD), F32),
            pltpu.VMEM((2, 8, 2, 32, HD), BF16),
            pltpu.VMEM((2, HN, 2, 32, HD), BF16),
            pltpu.VMEM((2, 32, 2 * HN * HD), BF16),
            pltpu.VMEM((8, HD), jnp.int32),
            pltpu.SMEM((8, HD), jnp.int32),
            dma,
            dma((2, 8)), dma((2, 8)),
            dma((2, 2, 7)), dma((2, 2, 7)),
            dma((2, 2, 3)), dma((2, 2, 3)),
            dma((4, 3)), dma((4, 3)),
            dma((2, 2, 3)), dma((2, 2, 3)),
            dma((2, 2, 14)), dma((2, 2, 14)),
            dma((2, 8)), dma((2, 8)),
        ],
        compiler_params=pltpu.CompilerParams(
            collective_id=0, has_side_effects=True, vmem_limit_bytes=60 * 1024 * 1024
        ),
        name="attend",
    )(media_list.T, media_count, image_slot, gate_logit, queries, d_gated, image_kv)


def solution(mesh):
    return jax.shard_map(
        on_device,
        mesh=mesh,
        in_specs=(
            P("seq", "head"),
            P("seq", "head", None, None),
            P("head"),
            P("seq", "head"),
            P(),
            P(),
            P(),
        ),
        out_specs=(P("seq", "head"), P("seq", "head"), P("seq", "head", None, None)),
        check_vma=False,
    )
```

```python
import functools

import jax
import jax.numpy as jnp
from jax import lax
from jax.experimental import pallas as pl
from jax.experimental.pallas import tpu as pltpu
from jax.sharding import PartitionSpec as P

MESH = pl.DeviceIdType.MESH
HD = 128
XN = 4
ZN = 8
HN = 8
MEDIA = 16
LOWEST = 12
TOK = 192
ROWS = 1536
HALF = 768
RB = 256
KEYS = 1024
PART = 64
SLOTS = 64
MS = 256
UNROLL = 6
LOG2E = 1.4426950408889634
INV_ROOT = HD ** (-0.5)
F32 = jnp.float32
BF16 = jnp.bfloat16


def mod(value, n):
    return lax.rem(value + n, n)


def nt_dot(a, b):
    return lax.dot_general(a, b, (((1,), (1,)), ((), ())), preferred_element_type=F32)


def nn_dot(a, b):
    return jnp.dot(a, b, preferred_element_type=F32)


def kernel(
    media_ref, counts_ref, place_ref, gate_ref, q_ref, dg_ref, kv_ref,
    gated_ref, dq_ref, dkv_ref,
    kall, vall, qall, daall, dat, dap, pmat, kc, kt, vc, vt, sbuf, ot,
    stat, statin, fac, wgt, dlt, xo, xin, gk, gv, rout, rin, sums, fin, dkvin, kvlin, inv_v, inv_ref, inv_sem,
    a2a_s, a2a_r, ag_s, ag_r, xg_s, xg_r, st_s, st_r, xr_s, xr_r, rs_s, rs_r, fa_s, fa_r,
):
    seq = lax.axis_index("seq")
    h = lax.axis_index("head")
    z = seq // XN
    x = lax.rem(seq, XN)
    hq = h // 2
    hp = lax.rem(h, 2)
    kv_all = (kall, vall)
    xg_all = (qall, daall)
    grads = (gk, gv)
    pending = []

    def dev(zz, xx, hh):
        return (zz * XN + xx, hh)

    def send(src, dst, ssem, rsem, device):
        copy = pltpu.make_async_remote_copy(
            src_ref=src, dst_ref=dst, send_sem=ssem, recv_sem=rsem, device_id=device, device_id_type=MESH
        )
        copy.start()
        pending.append(copy)

    def arrived(ref, sem):
        pltpu.make_async_copy(ref, ref, sem).wait()

    z_to = (mod(z + 1, ZN), mod(z - 1, ZN))
    x_to = (mod(x + 1, XN), mod(x - 1, XN))
    x_opp = mod(x + 2, XN)
    x_part = lax.rem(x + hq + 2 * hp, XN)
    self_in = x_part == x

    def holder(k, jj):
        return 2 * ((2 * XN - k - 2 * jj) % XN) + jj

    barrier = pltpu.get_barrier_semaphore()

    def greet(device):
        pl.semaphore_signal(barrier, inc=1, device_id=device, device_id_type=MESH)

    for k in range(1, HN):
        greet(dev(z, x_part, mod(h + k, HN)))
    for k in range(1, XN):
        greet(dev(z, mod(x + k, XN), h))
        for jj in range(2):
            greet(dev(z, mod(x + k, XN), holder(k, jj)))
    for jj in range(2):

        @pl.when(h != holder(0, jj))
        def _():
            greet(dev(z, x, holder(0, jj)))

    @pl.when(jnp.logical_not(self_in))
    def _():
        greet(dev(z, x_part, h))

    for d in range(2):
        greet(dev(z_to[d], x, h))
    for i in range(2):
        for t in range(2):
            kvlin[i, :, t * HN * HD : (t + 1) * HN * HD] = kv_ref[i, :, t, :]
    for g in range(8):
        rows = q_ref[:, g * HD : (g + 1) * HD]
        qall[x, g // 4, (g % 4) * TOK : (g % 4 + 1) * TOK, :] = rows

    def gate_row(g):
        return jnp.tanh(jnp.full((1, HD), gate_ref[g], F32))

    for g in range(8):
        rows = dg_ref[:, g * HD : (g + 1) * HD].astype(F32) * gate_row(g)
        daall[x, g // 4, (g % 4) * TOK : (g % 4 + 1) * TOK, :] = rows.astype(BF16)
    stat[...] = jnp.ones_like(stat)

    lane = lax.broadcasted_iota(jnp.int32, (1, HD), 1)
    inv_v[...] = jnp.full((8, HD), -1, jnp.int32)
    for c in range(XN):
        found = jnp.full((1, HD), -1, jnp.int32)
        for j in range(MEDIA):
            slot = place_ref[media_ref[j, z * XN + c]]
            slot = jnp.where(j < counts_ref[z * XN + c], slot, -1)
            found = jnp.where(lane == slot, j, found)
        inv_v[c : c + 1, :] = found
    inv_copy = pltpu.make_async_copy(inv_v, inv_ref, inv_sem)

    pl.semaphore_wait(barrier, jnp.where(self_in, 19, 21))

    def kv_lanes(t, head):
        return kvlin.at[:, :, pl.ds(pl.multiple_of((t * HN + head) * HD, HD), HD)]

    def a2a_copy(t, k):
        target = mod(h + k, HN)
        mine = kall if t == 0 else vall
        dst = mine.at[pl.ds(2 * seq, 2), hp]
        return pltpu.make_async_remote_copy(
            src_ref=kv_lanes(t, target), dst_ref=dst, send_sem=a2a_s.at[t, k],
            recv_sem=a2a_r.at[t, 2 * x + hp], device_id=dev(z, x_part, target), device_id_type=MESH,
        )

    for t in range(2):
        for k in range(1, HN):
            a2a_copy(t, k).start()

        @pl.when(jnp.logical_not(self_in))
        def _():
            a2a_copy(t, 0).start()

        @pl.when(self_in)
        def _():
            pltpu.make_async_copy(
                kv_lanes(t, h), kv_all[t].at[pl.ds(2 * seq, 2), hp], a2a_r.at[t, 2 * x + hp]
            ).start()

    def a2a_wait(t, sub):
        for xx in (2 * sub, 2 * sub + 1):
            for jj in range(2):
                arrived(kv_all[t].at[pl.ds(2 * (z * XN + xx), 2), jj], a2a_r.at[t, 2 * xx + jj])

    def xg_ref(t, c, half):
        return xg_all[t].at[c, half]

    def xg_first(t):
        for pos in range(2):
            for d in range(2):
                half = d if pos == 0 else 1 - d
                ref = xg_ref(t, x, half)
                send(ref, ref, xg_s.at[t, d, pos], xg_r.at[t, d, pos], dev(z, x_to[d], h))

    def xg_wait(t, d, pos):
        c = x_opp if pos == 2 else x_to[1 - d]
        half = 1 - d if pos == 1 else d
        arrived(xg_ref(t, c, half), xg_r.at[t, d, pos])

    def xg_forward(t):
        for d in range(2):
            xg_wait(t, d, 0)
            ref = xg_ref(t, x_to[1 - d], d)
            send(ref, ref, xg_s.at[t, d, 2], xg_r.at[t, d, 2], dev(z, x_to[d], h))

    def ag_ref(t, zz, d, pos):
        sub = d if pos == 0 else 1 - d
        return kv_all[t].at[pl.ds(zz * 8 + 4 * sub, 4)]

    def ag_send(t, k, pos, ways=(0, 1)):
        for d in ways:
            zz = mod(z - (k - 1), ZN) if d == 0 else mod(z + (k - 1), ZN)
            ref = ag_ref(t, zz, d, pos)
            i = 2 * (k - 1) + pos
            send(ref, ref, ag_s.at[t, d, i], ag_r.at[t, d, i], dev(z_to[d], x, h))

    def ag_wait(t, k, pos):
        for d in range(2):
            zz = mod(z - k, ZN) if d == 0 else mod(z + k, ZN)
            arrived(ag_ref(t, zz, d, pos), ag_r.at[t, d, 2 * (k - 1) + pos])

    def ag_pass(t, k, pos):
        ag_wait(t, k - 1, pos)
        ag_send(t, k, pos)

    def ag_step(t, k):
        for pos in range(1 if k == 4 else 2):
            ag_pass(t, k, pos)

    def ag_end(t):
        ag_wait(t, 3, 1)
        ag_wait(t, 4, 0)

    xg_first(0)
    inv_copy.start()

    for t in range(2):
        a2a_wait(t, 0)
        ag_send(t, 1, 0, (0,))
        a2a_wait(t, 1)
        ag_send(t, 1, 0, (1,))
        if t == 0:
            ag_send(0, 1, 1)
    xg_forward(0)
    xg_first(1)
    ag_step(0, 2)
    ag_send(1, 1, 1)
    ag_step(0, 3)
    ag_pass(1, 2, 0)
    ag_step(0, 4)
    ag_pass(1, 2, 1)
    inv_copy.wait()
    ag_end(0)

    def pick(src, dst, dst_t, c):
        segment = z * XN + c

        for j in range(MEDIA):
            slot = place_ref[media_ref[j, segment]]
            dst[c, j * PART : (j + 1) * PART, :] = src[slot].reshape(PART, HD)
        for ch in range(KEYS // 256):
            block = dst[c, ch * 256 : (ch + 1) * 256, :]
            dst_t[c, :, ch * 256 : (ch + 1) * 256] = block.T

    def lanes(rb):
        return pl.ds(pl.multiple_of(rb * RB, RB), RB)

    def probs_of(c):
        pick(kall, kc, kt, c)
        live = (counts_ref[z * XN + c] - LOWEST) * PART

        def block(i, carry):
            for r in range(UNROLL):
                rb = i * UNROLL + r
                q_rows = qall[c, rb // 3, pl.ds(pl.multiple_of(lax.rem(rb, 3) * RB, RB), RB), :]
                top = None
                for m in range(KEYS // MS):
                    rows = slice(m * MS, (m + 1) * MS)
                    s = nt_dot(kc[c, rows, :], q_rows)
                    if m == KEYS // MS - 1:
                        first = LOWEST * PART - m * MS
                        row_ids = lax.broadcasted_iota(jnp.int32, (KEYS - LOWEST * PART, RB), 0)
                        last = jnp.where(row_ids < live, s[first:], -1e30)
                        s = jnp.concatenate([s[:first], last], axis=0) if first else last
                    sbuf[r, rows, :] = s
                    here = jnp.max(s, axis=0, keepdims=True)
                    top = here if top is None else jnp.maximum(top, here)
                total = jnp.zeros((1, RB), F32)
                for ch in range(4):
                    rows = slice(ch * 256, (ch + 1) * 256)
                    p = jnp.exp2((sbuf[r, rows, :] - top) * (LOG2E * INV_ROOT))
                    total = total + jnp.sum(p, axis=0, keepdims=True)
                    pmat[c, rows, lanes(rb)] = p.astype(BF16)
                stat[c, 0, pl.ds(rb, 1), :] = top
                stat[c, 1, pl.ds(rb, 1), :] = total
            return carry

        lax.fori_loop(0, 6 // UNROLL, block, 0)

    def turn(c):
        for half in range(2):
            for r in range(3):
                rb = half * 3 + r
                dat[c, :, rb * RB : (rb + 1) * RB] = daall[c, half, r * RB : (r + 1) * RB, :].T

    def outs_of(c):
        pick(vall, vc, vt, c)

        def block(i, carry):
            for r in range(UNROLL):
                rb = i * UNROLL + r
                da_t = dat[c, :, lanes(rb)]
                o = nn_dot(vt[c], pmat[c, :, lanes(rb)])
                ot[c, :, lanes(rb)] = o
                cols = pl.ds(pl.multiple_of(lax.rem(rb, 3) * RB, RB), RB)
                xo[0, c, rb // 3, :, cols] = (o / stat[c, 1, pl.ds(rb, 1), :]).astype(BF16)
                stat[c, 2, pl.ds(rb, 1), :] = jnp.sum(da_t.astype(F32) * o, axis=0, keepdims=True)
            return carry

        lax.fori_loop(0, 6 // UNROLL, block, 0)

    def stat_send(c, i):
        for k in range(1, XN):
            send(
                stat.at[c], statin.at[k - 1, c], st_s.at[i, k - 1], st_r.at[i, k - 1],
                dev(z, mod(x + k, XN), h),
            )

    c_right, c_left = x_to
    xg_forward(1)
    turn(x)
    probs_of(x)
    ag_step(1, 3)
    xg_wait(0, 0, 1)
    probs_of(c_left)
    ag_step(1, 4)
    xg_wait(0, 1, 1)
    probs_of(c_right)
    for d in range(2):
        xg_wait(0, d, 2)
    probs_of(x_opp)
    xg_wait(1, 0, 1)
    turn(c_left)
    xg_wait(1, 1, 1)
    turn(c_right)
    for d in range(2):
        xg_wait(1, d, 2)
    turn(x_opp)
    ag_end(1)

    def xr_copy(t, d, i):
        c, half = ((x_opp, d), (x_to[d], 1 - d), (x_to[d], d))[i]
        return pltpu.make_async_remote_copy(
            src_ref=xo.at[t, c, half], dst_ref=xin.at[t, d, i], send_sem=xr_s.at[t, d, i],
            recv_sem=xr_r.at[t, d, i], device_id=dev(z, x_to[d], h), device_id_type=MESH,
        )

    def xr_opp(t):
        for d in range(2):
            xr_copy(t, d, 0).start()

    def xr_near(t, d):
        xr_copy(t, d, 1).start()

    def row_of(ref, c, half):
        return jnp.concatenate([ref[c, pl.ds(half * 3 + r, 1), :] for r in range(3)], axis=1)

    def part_of(t, c, half):
        if t == 1:
            return xo[1, c, half].astype(F32)
        return ot[c, :, half * HALF : (half + 1) * HALF] * row_of(fac, c, half)

    def weighed(t, c, half, d, i):
        got = xin[t, d, i].astype(F32)
        return got * row_of(wgt.at[:, d], c, half) if t == 0 else got

    def xr_add(t):
        for d in range(2):
            arrived(xin.at[t, d, 0], xr_r.at[t, d, 0])
            both = part_of(t, x_to[d], d) + weighed(t, x_to[d], d, d, 0)
            xo[t, x_to[d], d] = both.astype(BF16)
            xr_copy(t, d, 2).start()

    def xr_end(t):
        for d in range(2):
            for i in (1, 2):
                arrived(xin.at[t, d, i], xr_r.at[t, d, i])

    def xr_rows(t, half):
        both = part_of(t, x, half) + xin[t, half, 2].astype(F32) + weighed(t, x, half, 1 - half, 1)
        return both.T

    for c in range(XN):
        outs_of(c)
        stat_send(c, c)

        @pl.when(x_opp == c)
        def _():
            xr_opp(0)

        for d in range(2):

            @pl.when(x_to[d] == c)
            def _():
                xr_near(0, d)

    def stat_wait(c):
        for k in range(1, XN):
            arrived(statin.at[k - 1, c], st_r.at[c, k - 1])

    def combine(c):
        stat_wait(c)
        tops = [stat[c, 0]] + [statin[k, c, 0] for k in range(XN - 1)]
        totals = [stat[c, 1]] + [statin[k, c, 1] for k in range(XN - 1)]
        dots = [stat[c, 2]] + [statin[k, c, 2] for k in range(XN - 1)]
        top = functools.reduce(jnp.maximum, tops)
        scales = [jnp.exp2((one - top) * (LOG2E * INV_ROOT)) for one in tops]
        total = sum(a * b for a, b in zip(scales, totals))
        delta = sum(a * b for a, b in zip(scales, dots)) / total
        own = scales[0] / total
        wgt[c, 0] = scales[1] * totals[1] / total
        wgt[c, 1] = scales[3] * totals[3] / total
        fac[c] = own
        dlt[c] = delta * own

        def block(rb, carry):
            f = fac[c, pl.ds(rb, 1), :]
            scaled = (dat[c, :, lanes(rb)].astype(F32) * f).astype(BF16)
            dat[c, :, lanes(rb)] = scaled
            dap[c, pl.ds(pl.multiple_of(rb * RB, RB), RB), :] = scaled.T
            return carry

        lax.fori_loop(0, 6, block, 0, unroll=True)

    def value_grads(c):
        for m in range(KEYS // MS):
            part = nn_dot(pmat[c, m * MS : (m + 1) * MS, :], dap[c])
            gv[c, m * MS // PART : (m + 1) * MS // PART] = part.astype(BF16).reshape(MS // PART, PART, HD)

    for c in range(XN):
        combine(c)
        value_grads(c)

    def own_part(t, slot):
        out = None
        for c in range(XN):
            entry = inv_ref[c, slot]
            block = grads[t][c, jnp.maximum(entry, 0)].astype(F32)
            block = jnp.where(entry >= 0, block, 0.0)
            out = block if out is None else out + block
        return out

    def rs_prep(t):
        def one(i, carry):
            for r in range(8):
                slot = i * 8 + r
                sums[t, slot] = own_part(t, slot)
            return carry

        lax.fori_loop(0, SLOTS // 8, one, 0)

    def rs_step(t, i):
        away = 5 - (i + 3) // 2
        for m in range(2):
            for d in range(2):
                zt = mod(z + away, ZN) if d == 0 else mod(z - away, ZN)
                sub = d if i % 2 == 0 else 1 - d
                first = zt * 8 + 4 * sub + 2 * m
                j = 2 * i + m
                if i < 2:
                    for sl in range(2):
                        rout[t, d, j, sl] = own_part(t, first + sl).astype(BF16)
                else:
                    arrived(rin.at[t, d, j - 4], rs_r.at[t, d, j - 4])
                    both = sums[t, pl.ds(first, 2)] + rin[t, d, j - 4].astype(F32)
                    rout[t, d, j] = both.astype(BF16)
                send(rout.at[t, d, j], rin.at[t, d, j], rs_s.at[t, d, j], rs_r.at[t, d, j], dev(z_to[d], x, h))

    def rs_end(t):
        for j in range(10, 14):
            for d in range(2):
                arrived(rin.at[t, d, j], rs_r.at[t, d, j])
        for sub in range(2):
            for m in range(2):
                first = 4 * sub + 2 * m
                part = sums[t, pl.ds(z * 8 + first, 2)]
                for d in range(2):
                    part = part + rin[t, d, (12 if sub == d else 10) + m].astype(F32)
                fin[t, first : first + 2] = part.astype(BF16).reshape(2, 2, 32, HD)

    def fa_copy(t, k, jj):
        target = mod(x + k, XN)
        return pltpu.make_async_remote_copy(
            src_ref=fin.at[t, pl.ds(2 * target, 2), jj], dst_ref=dkvin.at[t, h], send_sem=fa_s.at[t, 2 * k + jj],
            recv_sem=fa_r.at[t, h], device_id=dev(z, target, holder(k, jj)), device_id_type=MESH,
        )

    def fa_start(t):
        for k in range(XN):
            for jj in range(2):
                if k:
                    fa_copy(t, k, jj).start()
                    continue
                own = h == holder(0, jj)

                @pl.when(jnp.logical_not(own))
                def _():
                    fa_copy(t, k, jj).start()

                @pl.when(own)
                def _():
                    pltpu.make_async_copy(fin.at[t, pl.ds(2 * x, 2), jj], dkvin.at[t, h], fa_r.at[t, h]).start()

    def fa_end(t):
        for hh in range(HN):
            arrived(dkvin.at[t, hh], fa_r.at[t, hh])

    def key_grads(c):
        def block(i, carry):
            for r in range(UNROLL):
                rb = i * UNROLL + r
                da_t = dat[c, :, lanes(rb)]
                d_row = dlt[c, pl.ds(rb, 1), :]
                for m in range(KEYS // MS):
                    rows = slice(m * MS, (m + 1) * MS)
                    dp = nn_dot(vc[c, rows, :], da_t) - d_row
                    ds = pmat[c, rows, lanes(rb)].astype(F32) * dp
                    pmat[c, rows, lanes(rb)] = ds.astype(BF16)
            return carry

        lax.fori_loop(0, 6 // UNROLL, block, 0)
        for m in range(KEYS // MS):
            part = nn_dot(pmat[c, m * MS : (m + 1) * MS, :], qall[c].reshape(ROWS, HD)) * INV_ROOT
            gk[c, m * MS // PART : (m + 1) * MS // PART] = part.astype(BF16).reshape(MS // PART, PART, HD)

    def query_grads(c):
        def block(i, carry):
            for r in range(UNROLL):
                rb = i * UNROLL + r
                part = nn_dot(kt[c], pmat[c, :, lanes(rb)]) * INV_ROOT
                cols = pl.ds(pl.multiple_of(lax.rem(rb, 3) * RB, RB), RB)
                xo[1, c, rb // 3, :, cols] = part.astype(BF16)
            return carry

        lax.fori_loop(0, 6 // UNROLL, block, 0)

    rs_step(1, 0)
    rs_step(1, 1)
    xr_add(0)
    rs_prep(1)
    key_grads(x_opp)
    query_grads(x_opp)
    xr_opp(1)
    rs_step(1, 2)
    key_grads(c_right)
    rs_step(1, 3)
    key_grads(c_left)
    key_grads(x)
    rs_step(0, 0)
    rs_step(0, 1)
    rs_step(1, 4)
    rs_prep(0)
    query_grads(c_right)
    xr_near(1, 0)
    query_grads(c_left)
    xr_near(1, 1)
    rs_step(0, 2)
    rs_step(0, 3)
    rs_step(1, 5)
    query_grads(x)
    rs_step(0, 4)
    rs_step(0, 5)
    rs_step(1, 6)
    xr_add(1)
    xr_end(0)
    for half in range(2):
        rows = xr_rows(0, half)
        for gg in range(4):
            g = half * 4 + gg
            gated_ref[:, g * HD : (g + 1) * HD] = (rows[gg * TOK : (gg + 1) * TOK, :] * gate_row(g)).astype(BF16)
    rs_step(0, 6)
    rs_end(1)
    fa_start(1)
    rs_end(0)
    fa_start(0)
    xr_end(1)
    for half in range(2):
        rows = xr_rows(1, half)
        for gg in range(4):
            g = half * 4 + gg
            dq_ref[:, g * HD : (g + 1) * HD] = rows[gg * TOK : (gg + 1) * TOK, :].astype(BF16)
    for t in (1, 0):
        fa_end(t)
        for hh in range(HN):
            dkv_ref[:, :, t, hh * HD : (hh + 1) * HD] = dkvin[t, hh]

    for copy in pending:
        copy.wait_send()
    for t in range(2):
        for d in range(2):
            for i in range(3):
                xr_copy(t, d, i).wait_send()
    for t in range(2):
        for k in range(1, HN):
            a2a_copy(t, k).wait_send()

        @pl.when(jnp.logical_not(self_in))
        def _():
            a2a_copy(t, 0).wait_send()

        for k in range(XN):
            for jj in range(2):
                if k:
                    fa_copy(t, k, jj).wait_send()
                    continue

                @pl.when(h != holder(0, jj))
                def _():
                    fa_copy(t, k, jj).wait_send()


def on_device(queries, image_kv, gate_logit, d_gated, media_list, media_count, image_slot):
    smem = pl.BlockSpec(memory_space=pltpu.SMEM)
    vmem = pl.BlockSpec(memory_space=pltpu.VMEM)
    dma = pltpu.SemaphoreType.DMA
    return pl.pallas_call(
        kernel,
        out_shape=(
            jax.ShapeDtypeStruct((TOK, HN * HD), BF16),
            jax.ShapeDtypeStruct((TOK, HN * HD), BF16),
            jax.ShapeDtypeStruct((2, 32, 2, HN * HD), BF16),
        ),
        in_specs=[smem] * 4 + [vmem] * 3,
        out_specs=(vmem,) * 3,
        scratch_shapes=[
            pltpu.VMEM((SLOTS, 2, 32, HD), BF16),
            pltpu.VMEM((SLOTS, 2, 32, HD), BF16),
            pltpu.VMEM((XN, 2, HALF, HD), BF16),
            pltpu.VMEM((XN, 2, HALF, HD), BF16),
            pltpu.VMEM((XN, HD, ROWS), BF16),
            pltpu.VMEM((XN, ROWS, HD), BF16),
            pltpu.VMEM((XN, KEYS, ROWS), BF16),
            pltpu.VMEM((XN, KEYS, HD), BF16),
            pltpu.VMEM((XN, HD, KEYS), BF16),
            pltpu.VMEM((XN, KEYS, HD), BF16),
            pltpu.VMEM((XN, HD, KEYS), BF16),
            pltpu.VMEM((UNROLL, KEYS, RB), F32),
            pltpu.VMEM((XN, HD, ROWS), F32),
            pltpu.VMEM((XN, 3, 8, RB), F32),
            pltpu.VMEM((XN - 1, XN, 3, 8, RB), F32),
            pltpu.VMEM((XN, 8, RB), F32),
            pltpu.VMEM((XN, 2, 8, RB), F32),
            pltpu.VMEM((XN, 8, RB), F32),
            pltpu.VMEM((2, XN, 2, HD, HALF), BF16),
            pltpu.VMEM((2, 2, 3, HD, HALF), BF16),
            pltpu.VMEM((XN, MEDIA, PART, HD), BF16),
            pltpu.VMEM((XN, MEDIA, PART, HD), BF16),
            pltpu.VMEM((2, 2, 14, 2, PART, HD), BF16),
            pltpu.VMEM((2, 2, 14, 2, PART, HD), BF16),
            pltpu.VMEM((2, SLOTS, PART, HD), F32),
            pltpu.VMEM((2, 8, 2, 32, HD), BF16),
            pltpu.VMEM((2, HN, 2, 32, HD), BF16),
            pltpu.VMEM((2, 32, 2 * HN * HD), BF16),
            pltpu.VMEM((8, HD), jnp.int32),
            pltpu.SMEM((8, HD), jnp.int32),
            dma,
            dma((2, 8)), dma((2, 8)),
            dma((2, 2, 7)), dma((2, 2, 7)),
            dma((2, 2, 3)), dma((2, 2, 3)),
            dma((4, 3)), dma((4, 3)),
            dma((2, 2, 3)), dma((2, 2, 3)),
            dma((2, 2, 14)), dma((2, 2, 14)),
            dma((2, 8)), dma((2, 8)),
        ],
        compiler_params=pltpu.CompilerParams(
            collective_id=0, has_side_effects=True, vmem_limit_bytes=60 * 1024 * 1024
        ),
        name="attend",
    )(media_list.T, media_count, image_slot, gate_logit, queries, d_gated, image_kv)


def solution(mesh):
    return jax.shard_map(
        on_device,
        mesh=mesh,
        in_specs=(
            P("seq", "head"),
            P("seq", "head", None, None),
            P("head"),
            P("seq", "head"),
            P(),
            P(),
            P(),
        ),
        out_specs=(P("seq", "head"), P("seq", "head"), P("seq", "head", None, None)),
        check_vma=False,
    )
```

```python
import functools

import jax
import jax.numpy as jnp
from jax import lax
from jax.experimental import pallas as pl
from jax.experimental.pallas import tpu as pltpu
from jax.sharding import PartitionSpec as P

MESH = pl.DeviceIdType.MESH
HD = 128
XN = 4
ZN = 8
HN = 8
MEDIA = 16
LOWEST = 12
TOK = 192
ROWS = 1536
HALF = 768
RB = 256
KEYS = 1024
PART = 64
SLOTS = 64
MS = 256
UNROLL = 6
LOG2E = 1.4426950408889634
INV_ROOT = HD ** (-0.5)
F32 = jnp.float32
BF16 = jnp.bfloat16


def mod(value, n):
    return lax.rem(value + n, n)


def nt_dot(a, b):
    return lax.dot_general(a, b, (((1,), (1,)), ((), ())), preferred_element_type=F32)


def nn_dot(a, b):
    return jnp.dot(a, b, preferred_element_type=F32)


def kernel(
    media_ref, counts_ref, place_ref, gate_ref, q_ref, dg_ref, kv_ref,
    gated_ref, dq_ref, dkv_ref,
    kall, vall, qall, daall, dat, dap, pmat, kc, kt, vc, vt, sbuf, ot,
    stat, statin, fac, wgt, dlt, xo, xin, gk, gv, rout, rin, sums, fin, dkvin, kvlin, inv_v, inv_ref, inv_sem,
    a2a_s, a2a_r, ag_s, ag_r, xg_s, xg_r, st_s, st_r, xr_s, xr_r, rs_s, rs_r, fa_s, fa_r,
):
    seq = lax.axis_index("seq")
    h = lax.axis_index("head")
    z = seq // XN
    x = lax.rem(seq, XN)
    hq = h // 2
    hp = lax.rem(h, 2)
    kv_all = (kall, vall)
    xg_all = (qall, daall)
    grads = (gk, gv)
    pending = []

    def dev(zz, xx, hh):
        return (zz * XN + xx, hh)

    def send(src, dst, ssem, rsem, device):
        copy = pltpu.make_async_remote_copy(
            src_ref=src, dst_ref=dst, send_sem=ssem, recv_sem=rsem, device_id=device, device_id_type=MESH
        )
        copy.start()
        pending.append(copy)

    def arrived(ref, sem):
        pltpu.make_async_copy(ref, ref, sem).wait()

    z_to = (mod(z + 1, ZN), mod(z - 1, ZN))
    x_to = (mod(x + 1, XN), mod(x - 1, XN))
    x_opp = mod(x + 2, XN)
    x_part = lax.rem(x + hq + 2 * hp, XN)
    self_in = x_part == x

    def holder(k, jj):
        return 2 * ((2 * XN - k - 2 * jj) % XN) + jj

    barrier = pltpu.get_barrier_semaphore()

    def greet(device):
        pl.semaphore_signal(barrier, inc=1, device_id=device, device_id_type=MESH)

    for k in range(1, HN):
        greet(dev(z, x_part, mod(h + k, HN)))
    for k in range(1, XN):
        greet(dev(z, mod(x + k, XN), h))
        for jj in range(2):
            greet(dev(z, mod(x + k, XN), holder(k, jj)))
    for jj in range(2):

        @pl.when(h != holder(0, jj))
        def _():
            greet(dev(z, x, holder(0, jj)))

    @pl.when(jnp.logical_not(self_in))
    def _():
        greet(dev(z, x_part, h))

    for d in range(2):
        greet(dev(z_to[d], x, h))
    for i in range(2):
        for t in range(2):
            kvlin[i, :, t * HN * HD : (t + 1) * HN * HD] = kv_ref[i, :, t, :]
    for g in range(8):
        rows = q_ref[:, g * HD : (g + 1) * HD]
        qall[x, g // 4, (g % 4) * TOK : (g % 4 + 1) * TOK, :] = rows

    def gate_row(g):
        return jnp.tanh(jnp.full((1, HD), gate_ref[g], F32))

    for g in range(8):
        rows = dg_ref[:, g * HD : (g + 1) * HD].astype(F32) * gate_row(g)
        daall[x, g // 4, (g % 4) * TOK : (g % 4 + 1) * TOK, :] = rows.astype(BF16)
    stat[...] = jnp.ones_like(stat)

    lane = lax.broadcasted_iota(jnp.int32, (1, HD), 1)
    inv_v[...] = jnp.full((8, HD), -1, jnp.int32)
    for c in range(XN):
        found = jnp.full((1, HD), -1, jnp.int32)
        for j in range(MEDIA):
            slot = place_ref[media_ref[j, z * XN + c]]
            slot = jnp.where(j < counts_ref[z * XN + c], slot, -1)
            found = jnp.where(lane == slot, j, found)
        inv_v[c : c + 1, :] = found
    inv_copy = pltpu.make_async_copy(inv_v, inv_ref, inv_sem)

    pl.semaphore_wait(barrier, jnp.where(self_in, 19, 21))

    def kv_lanes(t, head):
        return kvlin.at[:, :, pl.ds(pl.multiple_of((t * HN + head) * HD, HD), HD)]

    def a2a_copy(t, k):
        target = mod(h + k, HN)
        mine = kall if t == 0 else vall
        dst = mine.at[pl.ds(2 * seq, 2), hp]
        return pltpu.make_async_remote_copy(
            src_ref=kv_lanes(t, target), dst_ref=dst, send_sem=a2a_s.at[t, k],
            recv_sem=a2a_r.at[t, 2 * x + hp], device_id=dev(z, x_part, target), device_id_type=MESH,
        )

    for t in range(2):
        for k in range(1, HN):
            a2a_copy(t, k).start()

        @pl.when(jnp.logical_not(self_in))
        def _():
            a2a_copy(t, 0).start()

        @pl.when(self_in)
        def _():
            pltpu.make_async_copy(
                kv_lanes(t, h), kv_all[t].at[pl.ds(2 * seq, 2), hp], a2a_r.at[t, 2 * x + hp]
            ).start()

    def a2a_wait(t, sub):
        for xx in (2 * sub, 2 * sub + 1):
            for jj in range(2):
                arrived(kv_all[t].at[pl.ds(2 * (z * XN + xx), 2), jj], a2a_r.at[t, 2 * xx + jj])

    def xg_ref(t, c, half):
        return xg_all[t].at[c, half]

    def xg_first(t):
        for pos in range(2):
            for d in range(2):
                half = d if pos == 0 else 1 - d
                ref = xg_ref(t, x, half)
                send(ref, ref, xg_s.at[t, d, pos], xg_r.at[t, d, pos], dev(z, x_to[d], h))

    def xg_wait(t, d, pos):
        c = x_opp if pos == 2 else x_to[1 - d]
        half = 1 - d if pos == 1 else d
        arrived(xg_ref(t, c, half), xg_r.at[t, d, pos])

    def xg_forward(t):
        for d in range(2):
            xg_wait(t, d, 0)
            ref = xg_ref(t, x_to[1 - d], d)
            send(ref, ref, xg_s.at[t, d, 2], xg_r.at[t, d, 2], dev(z, x_to[d], h))

    def ag_ref(t, zz, d, pos):
        sub = d if pos == 0 else 1 - d
        return kv_all[t].at[pl.ds(zz * 8 + 4 * sub, 4)]

    def ag_send(t, k, pos, ways=(0, 1)):
        for d in ways:
            zz = mod(z - (k - 1), ZN) if d == 0 else mod(z + (k - 1), ZN)
            ref = ag_ref(t, zz, d, pos)
            i = 2 * (k - 1) + pos
            send(ref, ref, ag_s.at[t, d, i], ag_r.at[t, d, i], dev(z_to[d], x, h))

    def ag_wait(t, k, pos):
        for d in range(2):
            zz = mod(z - k, ZN) if d == 0 else mod(z + k, ZN)
            arrived(ag_ref(t, zz, d, pos), ag_r.at[t, d, 2 * (k - 1) + pos])

    def ag_pass(t, k, pos):
        ag_wait(t, k - 1, pos)
        ag_send(t, k, pos)

    def ag_step(t, k):
        for pos in range(1 if k == 4 else 2):
            ag_pass(t, k, pos)

    def ag_end(t):
        ag_wait(t, 3, 1)
        ag_wait(t, 4, 0)

    xg_first(0)
    inv_copy.start()

    for t in range(2):
        a2a_wait(t, 0)
        ag_send(t, 1, 0, (0,))
        a2a_wait(t, 1)
        ag_send(t, 1, 0, (1,))
        if t == 0:
            ag_send(0, 1, 1)
    xg_forward(0)
    xg_first(1)
    ag_step(0, 2)
    ag_send(1, 1, 1)
    ag_step(0, 3)
    ag_pass(1, 2, 0)
    ag_step(0, 4)
    ag_pass(1, 2, 1)
    inv_copy.wait()
    ag_end(0)

    def pick(src, dst, dst_t, c):
        segment = z * XN + c

        for j in range(MEDIA):
            slot = place_ref[media_ref[j, segment]]
            dst[c, j * PART : (j + 1) * PART, :] = src[slot].reshape(PART, HD)
        for ch in range(KEYS // 256):
            block = dst[c, ch * 256 : (ch + 1) * 256, :]
            dst_t[c, :, ch * 256 : (ch + 1) * 256] = block.T

    def lanes(rb):
        return pl.ds(pl.multiple_of(rb * RB, RB), RB)

    def probs_of(c):
        pick(kall, kc, kt, c)
        live = (counts_ref[z * XN + c] - LOWEST) * PART

        def block(i, carry):
            for r in range(UNROLL):
                rb = i * UNROLL + r
                q_rows = qall[c, rb // 3, pl.ds(pl.multiple_of(lax.rem(rb, 3) * RB, RB), RB), :]
                top = None
                for m in range(KEYS // MS):
                    rows = slice(m * MS, (m + 1) * MS)
                    s = nt_dot(kc[c, rows, :], q_rows)
                    if m == KEYS // MS - 1:
                        first = LOWEST * PART - m * MS
                        row_ids = lax.broadcasted_iota(jnp.int32, (KEYS - LOWEST * PART, RB), 0)
                        last = jnp.where(row_ids < live, s[first:], -1e30)
                        s = jnp.concatenate([s[:first], last], axis=0) if first else last
                    sbuf[r, rows, :] = s
                    here = jnp.max(s, axis=0, keepdims=True)
                    top = here if top is None else jnp.maximum(top, here)
                total = jnp.zeros((1, RB), F32)
                for ch in range(4):
                    rows = slice(ch * 256, (ch + 1) * 256)
                    p = jnp.exp2((sbuf[r, rows, :] - top) * (LOG2E * INV_ROOT))
                    total = total + jnp.sum(p, axis=0, keepdims=True)
                    pmat[c, rows, lanes(rb)] = p.astype(BF16)
                stat[c, 0, pl.ds(rb, 1), :] = top
                stat[c, 1, pl.ds(rb, 1), :] = total
            return carry

        lax.fori_loop(0, 6 // UNROLL, block, 0)

    def turn(c):
        for half in range(2):
            for r in range(3):
                rb = half * 3 + r
                dat[c, :, rb * RB : (rb + 1) * RB] = daall[c, half, r * RB : (r + 1) * RB, :].T

    def outs_of(c):
        pick(vall, vc, vt, c)

        def block(i, carry):
            for r in range(UNROLL):
                rb = i * UNROLL + r
                da_t = dat[c, :, lanes(rb)]
                o = nn_dot(vt[c], pmat[c, :, lanes(rb)])
                ot[c, :, lanes(rb)] = o
                cols = pl.ds(pl.multiple_of(lax.rem(rb, 3) * RB, RB), RB)
                xo[0, c, rb // 3, :, cols] = (o / stat[c, 1, pl.ds(rb, 1), :]).astype(BF16)
                stat[c, 2, pl.ds(rb, 1), :] = jnp.sum(da_t.astype(F32) * o, axis=0, keepdims=True)
            return carry

        lax.fori_loop(0, 6 // UNROLL, block, 0)

    def stat_send(c, i):
        for k in range(1, XN):
            send(
                stat.at[c], statin.at[k - 1, c], st_s.at[i, k - 1], st_r.at[i, k - 1],
                dev(z, mod(x + k, XN), h),
            )

    c_right, c_left = x_to
    xg_forward(1)
    turn(x)
    probs_of(x)
    ag_step(1, 3)
    xg_wait(0, 0, 1)
    probs_of(c_left)
    ag_step(1, 4)
    xg_wait(0, 1, 1)
    probs_of(c_right)
    for d in range(2):
        xg_wait(0, d, 2)
    probs_of(x_opp)
    xg_wait(1, 0, 1)
    turn(c_left)
    xg_wait(1, 1, 1)
    turn(c_right)
    for d in range(2):
        xg_wait(1, d, 2)
    turn(x_opp)
    ag_end(1)

    def xr_copy(t, d, i):
        c, half = ((x_opp, d), (x_to[d], 1 - d), (x_to[d], d))[i]
        return pltpu.make_async_remote_copy(
            src_ref=xo.at[t, c, half], dst_ref=xin.at[t, d, i], send_sem=xr_s.at[t, d, i],
            recv_sem=xr_r.at[t, d, i], device_id=dev(z, x_to[d], h), device_id_type=MESH,
        )

    def xr_opp(t):
        for d in range(2):
            xr_copy(t, d, 0).start()

    def xr_near(t, d):
        xr_copy(t, d, 1).start()

    def row_of(ref, c, half):
        return jnp.concatenate([ref[c, pl.ds(half * 3 + r, 1), :] for r in range(3)], axis=1)

    def part_of(t, c, half):
        if t == 1:
            return xo[1, c, half].astype(F32)
        return ot[c, :, half * HALF : (half + 1) * HALF] * row_of(fac, c, half)

    def weighed(t, c, half, d, i):
        got = xin[t, d, i].astype(F32)
        return got * row_of(wgt.at[:, d], c, half) if t == 0 else got

    def xr_add(t):
        for d in range(2):
            arrived(xin.at[t, d, 0], xr_r.at[t, d, 0])
            both = part_of(t, x_to[d], d) + weighed(t, x_to[d], d, d, 0)
            xo[t, x_to[d], d] = both.astype(BF16)
            xr_copy(t, d, 2).start()

    def xr_end(t):
        for d in range(2):
            for i in (1, 2):
                arrived(xin.at[t, d, i], xr_r.at[t, d, i])

    def xr_rows(t, half):
        both = part_of(t, x, half) + xin[t, half, 2].astype(F32) + weighed(t, x, half, 1 - half, 1)
        return both.T

    for c in range(XN):
        outs_of(c)
        stat_send(c, c)
    xr_opp(0)
    xr_near(0, 0)
    xr_near(0, 1)

    def stat_wait(c):
        for k in range(1, XN):
            arrived(statin.at[k - 1, c], st_r.at[c, k - 1])

    def combine(c):
        stat_wait(c)
        tops = [stat[c, 0]] + [statin[k, c, 0] for k in range(XN - 1)]
        totals = [stat[c, 1]] + [statin[k, c, 1] for k in range(XN - 1)]
        dots = [stat[c, 2]] + [statin[k, c, 2] for k in range(XN - 1)]
        top = functools.reduce(jnp.maximum, tops)
        scales = [jnp.exp2((one - top) * (LOG2E * INV_ROOT)) for one in tops]
        total = sum(a * b for a, b in zip(scales, totals))
        delta = sum(a * b for a, b in zip(scales, dots)) / total
        own = scales[0] / total
        wgt[c, 0] = scales[1] * totals[1] / total
        wgt[c, 1] = scales[3] * totals[3] / total
        fac[c] = own
        dlt[c] = delta * own

        def block(rb, carry):
            f = fac[c, pl.ds(rb, 1), :]
            scaled = (dat[c, :, lanes(rb)].astype(F32) * f).astype(BF16)
            dat[c, :, lanes(rb)] = scaled
            dap[c, pl.ds(pl.multiple_of(rb * RB, RB), RB), :] = scaled.T
            return carry

        lax.fori_loop(0, 6, block, 0, unroll=True)

    def value_grads(c):
        for m in range(KEYS // MS):
            part = nn_dot(pmat[c, m * MS : (m + 1) * MS, :], dap[c])
            gv[c, m * MS // PART : (m + 1) * MS // PART] = part.astype(BF16).reshape(MS // PART, PART, HD)

    for c in range(XN):
        combine(c)
        value_grads(c)

    def own_part(t, slot):
        out = None
        for c in range(XN):
            entry = inv_ref[c, slot]
            block = grads[t][c, jnp.maximum(entry, 0)].astype(F32)
            block = jnp.where(entry >= 0, block, 0.0)
            out = block if out is None else out + block
        return out

    def rs_prep(t):
        def one(i, carry):
            for r in range(8):
                slot = i * 8 + r
                sums[t, slot] = own_part(t, slot)
            return carry

        lax.fori_loop(0, SLOTS // 8, one, 0)

    def rs_step(t, i):
        away = 5 - (i + 3) // 2
        for m in range(2):
            for d in range(2):
                zt = mod(z + away, ZN) if d == 0 else mod(z - away, ZN)
                sub = d if i % 2 == 0 else 1 - d
                first = zt * 8 + 4 * sub + 2 * m
                j = 2 * i + m
                if i < 2:
                    for sl in range(2):
                        rout[t, d, j, sl] = own_part(t, first + sl).astype(BF16)
                else:
                    arrived(rin.at[t, d, j - 4], rs_r.at[t, d, j - 4])
                    both = sums[t, pl.ds(first, 2)] + rin[t, d, j - 4].astype(F32)
                    rout[t, d, j] = both.astype(BF16)
                send(rout.at[t, d, j], rin.at[t, d, j], rs_s.at[t, d, j], rs_r.at[t, d, j], dev(z_to[d], x, h))

    def rs_end(t):
        for j in range(10, 14):
            for d in range(2):
                arrived(rin.at[t, d, j], rs_r.at[t, d, j])
        for sub in range(2):
            for m in range(2):
                first = 4 * sub + 2 * m
                part = sums[t, pl.ds(z * 8 + first, 2)]
                for d in range(2):
                    part = part + rin[t, d, (12 if sub == d else 10) + m].astype(F32)
                fin[t, first : first + 2] = part.astype(BF16).reshape(2, 2, 32, HD)

    def fa_copy(t, k, jj):
        target = mod(x + k, XN)
        return pltpu.make_async_remote_copy(
            src_ref=fin.at[t, pl.ds(2 * target, 2), jj], dst_ref=dkvin.at[t, h], send_sem=fa_s.at[t, 2 * k + jj],
            recv_sem=fa_r.at[t, h], device_id=dev(z, target, holder(k, jj)), device_id_type=MESH,
        )

    def fa_start(t):
        for k in range(XN):
            for jj in range(2):
                if k:
                    fa_copy(t, k, jj).start()
                    continue
                own = h == holder(0, jj)

                @pl.when(jnp.logical_not(own))
                def _():
                    fa_copy(t, k, jj).start()

                @pl.when(own)
                def _():
                    pltpu.make_async_copy(fin.at[t, pl.ds(2 * x, 2), jj], dkvin.at[t, h], fa_r.at[t, h]).start()

    def fa_end(t):
        for hh in range(HN):
            arrived(dkvin.at[t, hh], fa_r.at[t, hh])

    def key_grads(c):
        def block(i, carry):
            for r in range(UNROLL):
                rb = i * UNROLL + r
                da_t = dat[c, :, lanes(rb)]
                d_row = dlt[c, pl.ds(rb, 1), :]
                for m in range(KEYS // MS):
                    rows = slice(m * MS, (m + 1) * MS)
                    dp = nn_dot(vc[c, rows, :], da_t) - d_row
                    ds = pmat[c, rows, lanes(rb)].astype(F32) * dp
                    pmat[c, rows, lanes(rb)] = ds.astype(BF16)
            return carry

        lax.fori_loop(0, 6 // UNROLL, block, 0)
        for m in range(KEYS // MS):
            part = nn_dot(pmat[c, m * MS : (m + 1) * MS, :], qall[c].reshape(ROWS, HD)) * INV_ROOT
            gk[c, m * MS // PART : (m + 1) * MS // PART] = part.astype(BF16).reshape(MS // PART, PART, HD)

    def query_grads(c):
        def block(i, carry):
            for r in range(UNROLL):
                rb = i * UNROLL + r
                part = nn_dot(kt[c], pmat[c, :, lanes(rb)]) * INV_ROOT
                cols = pl.ds(pl.multiple_of(lax.rem(rb, 3) * RB, RB), RB)
                xo[1, c, rb // 3, :, cols] = part.astype(BF16)
            return carry

        lax.fori_loop(0, 6 // UNROLL, block, 0)

    rs_step(1, 0)
    rs_step(1, 1)
    rs_prep(1)
    key_grads(x_opp)
    xr_add(0)
    query_grads(x_opp)
    xr_opp(1)
    rs_step(1, 2)
    key_grads(c_right)
    rs_step(1, 3)
    key_grads(c_left)
    key_grads(x)
    rs_step(0, 0)
    rs_step(0, 1)
    rs_step(1, 4)
    rs_prep(0)
    query_grads(c_right)
    xr_near(1, 0)
    query_grads(c_left)
    xr_near(1, 1)
    rs_step(0, 2)
    rs_step(0, 3)
    rs_step(1, 5)
    query_grads(x)
    rs_step(0, 4)
    rs_step(0, 5)
    rs_step(1, 6)
    xr_add(1)
    xr_end(0)
    for half in range(2):
        rows = xr_rows(0, half)
        for gg in range(4):
            g = half * 4 + gg
            gated_ref[:, g * HD : (g + 1) * HD] = (rows[gg * TOK : (gg + 1) * TOK, :] * gate_row(g)).astype(BF16)
    rs_step(0, 6)
    rs_end(1)
    fa_start(1)
    rs_end(0)
    fa_start(0)
    xr_end(1)
    for half in range(2):
        rows = xr_rows(1, half)
        for gg in range(4):
            g = half * 4 + gg
            dq_ref[:, g * HD : (g + 1) * HD] = rows[gg * TOK : (gg + 1) * TOK, :].astype(BF16)
    for t in (1, 0):
        fa_end(t)
        for hh in range(HN):
            dkv_ref[:, :, t, hh * HD : (hh + 1) * HD] = dkvin[t, hh]

    for copy in pending:
        copy.wait_send()
    for t in range(2):
        for d in range(2):
            for i in range(3):
                xr_copy(t, d, i).wait_send()
    for t in range(2):
        for k in range(1, HN):
            a2a_copy(t, k).wait_send()

        @pl.when(jnp.logical_not(self_in))
        def _():
            a2a_copy(t, 0).wait_send()

        for k in range(XN):
            for jj in range(2):
                if k:
                    fa_copy(t, k, jj).wait_send()
                    continue

                @pl.when(h != holder(0, jj))
                def _():
                    fa_copy(t, k, jj).wait_send()


def on_device(queries, image_kv, gate_logit, d_gated, media_list, media_count, image_slot):
    smem = pl.BlockSpec(memory_space=pltpu.SMEM)
    vmem = pl.BlockSpec(memory_space=pltpu.VMEM)
    dma = pltpu.SemaphoreType.DMA
    return pl.pallas_call(
        kernel,
        out_shape=(
            jax.ShapeDtypeStruct((TOK, HN * HD), BF16),
            jax.ShapeDtypeStruct((TOK, HN * HD), BF16),
            jax.ShapeDtypeStruct((2, 32, 2, HN * HD), BF16),
        ),
        in_specs=[smem] * 4 + [vmem] * 3,
        out_specs=(vmem,) * 3,
        scratch_shapes=[
            pltpu.VMEM((SLOTS, 2, 32, HD), BF16),
            pltpu.VMEM((SLOTS, 2, 32, HD), BF16),
            pltpu.VMEM((XN, 2, HALF, HD), BF16),
            pltpu.VMEM((XN, 2, HALF, HD), BF16),
            pltpu.VMEM((XN, HD, ROWS), BF16),
            pltpu.VMEM((XN, ROWS, HD), BF16),
            pltpu.VMEM((XN, KEYS, ROWS), BF16),
            pltpu.VMEM((XN, KEYS, HD), BF16),
            pltpu.VMEM((XN, HD, KEYS), BF16),
            pltpu.VMEM((XN, KEYS, HD), BF16),
            pltpu.VMEM((XN, HD, KEYS), BF16),
            pltpu.VMEM((UNROLL, KEYS, RB), F32),
            pltpu.VMEM((XN, HD, ROWS), F32),
            pltpu.VMEM((XN, 3, 8, RB), F32),
            pltpu.VMEM((XN - 1, XN, 3, 8, RB), F32),
            pltpu.VMEM((XN, 8, RB), F32),
            pltpu.VMEM((XN, 2, 8, RB), F32),
            pltpu.VMEM((XN, 8, RB), F32),
            pltpu.VMEM((2, XN, 2, HD, HALF), BF16),
            pltpu.VMEM((2, 2, 3, HD, HALF), BF16),
            pltpu.VMEM((XN, MEDIA, PART, HD), BF16),
            pltpu.VMEM((XN, MEDIA, PART, HD), BF16),
            pltpu.VMEM((2, 2, 14, 2, PART, HD), BF16),
            pltpu.VMEM((2, 2, 14, 2, PART, HD), BF16),
            pltpu.VMEM((2, SLOTS, PART, HD), F32),
            pltpu.VMEM((2, 8, 2, 32, HD), BF16),
            pltpu.VMEM((2, HN, 2, 32, HD), BF16),
            pltpu.VMEM((2, 32, 2 * HN * HD), BF16),
            pltpu.VMEM((8, HD), jnp.int32),
            pltpu.SMEM((8, HD), jnp.int32),
            dma,
            dma((2, 8)), dma((2, 8)),
            dma((2, 2, 7)), dma((2, 2, 7)),
            dma((2, 2, 3)), dma((2, 2, 3)),
            dma((4, 3)), dma((4, 3)),
            dma((2, 2, 3)), dma((2, 2, 3)),
            dma((2, 2, 14)), dma((2, 2, 14)),
            dma((2, 8)), dma((2, 8)),
        ],
        compiler_params=pltpu.CompilerParams(
            collective_id=0, has_side_effects=True, vmem_limit_bytes=60 * 1024 * 1024
        ),
        name="attend",
    )(media_list.T, media_count, image_slot, gate_logit, queries, d_gated, image_kv)


def solution(mesh):
    return jax.shard_map(
        on_device,
        mesh=mesh,
        in_specs=(
            P("seq", "head"),
            P("seq", "head", None, None),
            P("head"),
            P("seq", "head"),
            P(),
            P(),
            P(),
        ),
        out_specs=(P("seq", "head"), P("seq", "head"), P("seq", "head", None, None)),
        check_vma=False,
    )
```

```python
import functools

import jax
import jax.numpy as jnp
from jax import lax
from jax.experimental import pallas as pl
from jax.experimental.pallas import tpu as pltpu
from jax.sharding import PartitionSpec as P

MESH = pl.DeviceIdType.MESH
HD = 128
XN = 4
ZN = 8
HN = 8
MEDIA = 16
LOWEST = 12
TOK = 192
ROWS = 1536
HALF = 768
RB = 256
KEYS = 1024
PART = 64
SLOTS = 64
MS = 256
UNROLL = 6
LOG2E = 1.4426950408889634
INV_ROOT = HD ** (-0.5)
F32 = jnp.float32
BF16 = jnp.bfloat16


def mod(value, n):
    return lax.rem(value + n, n)


def nt_dot(a, b):
    return lax.dot_general(a, b, (((1,), (1,)), ((), ())), preferred_element_type=F32)


def nn_dot(a, b):
    return jnp.dot(a, b, preferred_element_type=F32)


def kernel(
    media_ref, counts_ref, place_ref, gate_ref, q_hbm, dg_hbm, kv_hbm,
    gated_hbm, dq_hbm, dkv_hbm,
    q_ref, dg_ref, kv_ref, gated_ref, dq_ref, dkv_ref,
    kall, vall, qall, daall, dat, dap, pmat, kc, kt, vc, vt, sbuf, ot,
    stat, statin, fac, wgt, dlt, xo, xin, gk, gv, rout, rin, sums, fin, dkvin, kvlin, inv_v, inv_ref, inv_sem,
    a2a_s, a2a_r, ag_s, ag_r, xg_s, xg_r, st_s, st_r, xr_s, xr_r, rs_s, rs_r, fa_s, fa_r, in_sem, out_sem,
):
    seq = lax.axis_index("seq")
    h = lax.axis_index("head")
    z = seq // XN
    x = lax.rem(seq, XN)
    hq = h // 2
    hp = lax.rem(h, 2)
    kv_all = (kall, vall)
    xg_all = (qall, daall)
    grads = (gk, gv)
    pending = []

    def dev(zz, xx, hh):
        return (zz * XN + xx, hh)

    def send(src, dst, ssem, rsem, device):
        copy = pltpu.make_async_remote_copy(
            src_ref=src, dst_ref=dst, send_sem=ssem, recv_sem=rsem, device_id=device, device_id_type=MESH
        )
        copy.start()
        pending.append(copy)

    def arrived(ref, sem):
        pltpu.make_async_copy(ref, ref, sem).wait()

    z_to = (mod(z + 1, ZN), mod(z - 1, ZN))
    x_to = (mod(x + 1, XN), mod(x - 1, XN))
    x_opp = mod(x + 2, XN)
    x_part = lax.rem(x + hq + 2 * hp, XN)
    self_in = x_part == x

    def holder(k, jj):
        return 2 * ((2 * XN - k - 2 * jj) % XN) + jj

    ins = [
        pltpu.make_async_copy(src, dst, in_sem.at[i])
        for i, (src, dst) in enumerate(((kv_hbm, kv_ref), (q_hbm, q_ref), (dg_hbm, dg_ref)))
    ]
    outs = [
        pltpu.make_async_copy(src, dst, out_sem.at[i])
        for i, (src, dst) in enumerate(((gated_ref, gated_hbm), (dq_ref, dq_hbm), (dkv_ref, dkv_hbm)))
    ]
    for copy in ins:
        copy.start()

    barrier = pltpu.get_barrier_semaphore()

    def greet(device):
        pl.semaphore_signal(barrier, inc=1, device_id=device, device_id_type=MESH)

    for k in range(1, HN):
        greet(dev(z, x_part, mod(h + k, HN)))
    for k in range(1, XN):
        greet(dev(z, mod(x + k, XN), h))
        for jj in range(2):
            greet(dev(z, mod(x + k, XN), holder(k, jj)))
    for jj in range(2):

        @pl.when(h != holder(0, jj))
        def _():
            greet(dev(z, x, holder(0, jj)))

    @pl.when(jnp.logical_not(self_in))
    def _():
        greet(dev(z, x_part, h))

    for d in range(2):
        greet(dev(z_to[d], x, h))
    ins[0].wait()
    for i in range(2):
        for t in range(2):
            kvlin[i, :, t * HN * HD : (t + 1) * HN * HD] = kv_ref[i, :, t, :]
    ins[1].wait()
    for g in range(8):
        rows = q_ref[:, g * HD : (g + 1) * HD]
        qall[x, g // 4, (g % 4) * TOK : (g % 4 + 1) * TOK, :] = rows

    def gate_row(g):
        return jnp.tanh(jnp.full((1, HD), gate_ref[g], F32))

    ins[2].wait()
    for g in range(8):
        rows = dg_ref[:, g * HD : (g + 1) * HD].astype(F32) * gate_row(g)
        daall[x, g // 4, (g % 4) * TOK : (g % 4 + 1) * TOK, :] = rows.astype(BF16)
    stat[...] = jnp.ones_like(stat)

    lane = lax.broadcasted_iota(jnp.int32, (1, HD), 1)
    inv_v[...] = jnp.full((8, HD), -1, jnp.int32)
    for c in range(XN):
        found = jnp.full((1, HD), -1, jnp.int32)
        for j in range(MEDIA):
            slot = place_ref[media_ref[j, z * XN + c]]
            slot = jnp.where(j < counts_ref[z * XN + c], slot, -1)
            found = jnp.where(lane == slot, j, found)
        inv_v[c : c + 1, :] = found
    inv_copy = pltpu.make_async_copy(inv_v, inv_ref, inv_sem)

    pl.semaphore_wait(barrier, jnp.where(self_in, 19, 21))

    def kv_lanes(t, head):
        return kvlin.at[:, :, pl.ds(pl.multiple_of((t * HN + head) * HD, HD), HD)]

    def a2a_copy(t, k):
        target = mod(h + k, HN)
        mine = kall if t == 0 else vall
        dst = mine.at[pl.ds(2 * seq, 2), hp]
        return pltpu.make_async_remote_copy(
            src_ref=kv_lanes(t, target), dst_ref=dst, send_sem=a2a_s.at[t, k],
            recv_sem=a2a_r.at[t, 2 * x + hp], device_id=dev(z, x_part, target), device_id_type=MESH,
        )

    for t in range(2):
        for k in range(1, HN):
            a2a_copy(t, k).start()

        @pl.when(jnp.logical_not(self_in))
        def _():
            a2a_copy(t, 0).start()

        @pl.when(self_in)
        def _():
            pltpu.make_async_copy(
                kv_lanes(t, h), kv_all[t].at[pl.ds(2 * seq, 2), hp], a2a_r.at[t, 2 * x + hp]
            ).start()

    def a2a_wait(t, sub):
        for xx in (2 * sub, 2 * sub + 1):
            for jj in range(2):
                arrived(kv_all[t].at[pl.ds(2 * (z * XN + xx), 2), jj], a2a_r.at[t, 2 * xx + jj])

    def xg_ref(t, c, half):
        return xg_all[t].at[c, half]

    def xg_first(t):
        for pos in range(2):
            for d in range(2):
                half = d if pos == 0 else 1 - d
                ref = xg_ref(t, x, half)
                send(ref, ref, xg_s.at[t, d, pos], xg_r.at[t, d, pos], dev(z, x_to[d], h))

    def xg_wait(t, d, pos):
        c = x_opp if pos == 2 else x_to[1 - d]
        half = 1 - d if pos == 1 else d
        arrived(xg_ref(t, c, half), xg_r.at[t, d, pos])

    def xg_forward(t):
        for d in range(2):
            xg_wait(t, d, 0)
            ref = xg_ref(t, x_to[1 - d], d)
            send(ref, ref, xg_s.at[t, d, 2], xg_r.at[t, d, 2], dev(z, x_to[d], h))

    def ag_ref(t, zz, d, pos):
        sub = d if pos == 0 else 1 - d
        return kv_all[t].at[pl.ds(zz * 8 + 4 * sub, 4)]

    def ag_send(t, k, pos, ways=(0, 1)):
        for d in ways:
            zz = mod(z - (k - 1), ZN) if d == 0 else mod(z + (k - 1), ZN)
            ref = ag_ref(t, zz, d, pos)
            i = 2 * (k - 1) + pos
            send(ref, ref, ag_s.at[t, d, i], ag_r.at[t, d, i], dev(z_to[d], x, h))

    def ag_wait(t, k, pos):
        for d in range(2):
            zz = mod(z - k, ZN) if d == 0 else mod(z + k, ZN)
            arrived(ag_ref(t, zz, d, pos), ag_r.at[t, d, 2 * (k - 1) + pos])

    def ag_pass(t, k, pos):
        ag_wait(t, k - 1, pos)
        ag_send(t, k, pos)

    def ag_step(t, k):
        for pos in range(1 if k == 4 else 2):
            ag_pass(t, k, pos)

    def ag_end(t):
        ag_wait(t, 3, 1)
        ag_wait(t, 4, 0)

    xg_first(0)
    inv_copy.start()

    for t in range(2):
        a2a_wait(t, 0)
        ag_send(t, 1, 0, (0,))
        a2a_wait(t, 1)
        ag_send(t, 1, 0, (1,))
        if t == 0:
            ag_send(0, 1, 1)
    xg_forward(0)
    xg_first(1)
    ag_step(0, 2)
    ag_send(1, 1, 1)
    ag_step(0, 3)
    ag_pass(1, 2, 0)
    ag_step(0, 4)
    ag_pass(1, 2, 1)
    inv_copy.wait()
    ag_end(0)

    def pick(src, dst, dst_t, c):
        segment = z * XN + c

        for j in range(MEDIA):
            slot = place_ref[media_ref[j, segment]]
            dst[c, j * PART : (j + 1) * PART, :] = src[slot].reshape(PART, HD)
        for ch in range(KEYS // 256):
            block = dst[c, ch * 256 : (ch + 1) * 256, :]
            dst_t[c, :, ch * 256 : (ch + 1) * 256] = block.T

    def lanes(rb):
        return pl.ds(pl.multiple_of(rb * RB, RB), RB)

    def probs_of(c):
        pick(kall, kc, kt, c)
        live = (counts_ref[z * XN + c] - LOWEST) * PART

        def block(i, carry):
            for r in range(UNROLL):
                rb = i * UNROLL + r
                q_rows = qall[c, rb // 3, pl.ds(pl.multiple_of(lax.rem(rb, 3) * RB, RB), RB), :]
                top = None
                for m in range(KEYS // MS):
                    rows = slice(m * MS, (m + 1) * MS)
                    s = nt_dot(kc[c, rows, :], q_rows)
                    if m == KEYS // MS - 1:
                        first = LOWEST * PART - m * MS
                        row_ids = lax.broadcasted_iota(jnp.int32, (KEYS - LOWEST * PART, RB), 0)
                        last = jnp.where(row_ids < live, s[first:], -1e30)
                        s = jnp.concatenate([s[:first], last], axis=0) if first else last
                    sbuf[r, rows, :] = s
                    here = jnp.max(s, axis=0, keepdims=True)
                    top = here if top is None else jnp.maximum(top, here)
                total = jnp.zeros((1, RB), F32)
                for ch in range(4):
                    rows = slice(ch * 256, (ch + 1) * 256)
                    p = jnp.exp2((sbuf[r, rows, :] - top) * (LOG2E * INV_ROOT))
                    total = total + jnp.sum(p, axis=0, keepdims=True)
                    pmat[c, rows, lanes(rb)] = p.astype(BF16)
                stat[c, 0, pl.ds(rb, 1), :] = top
                stat[c, 1, pl.ds(rb, 1), :] = total
            return carry

        lax.fori_loop(0, 6 // UNROLL, block, 0)

    def turn(c):
        for half in range(2):
            for r in range(3):
                rb = half * 3 + r
                dat[c, :, rb * RB : (rb + 1) * RB] = daall[c, half, r * RB : (r + 1) * RB, :].T

    def outs_of(c):
        pick(vall, vc, vt, c)

        def block(i, carry):
            for r in range(UNROLL):
                rb = i * UNROLL + r
                da_t = dat[c, :, lanes(rb)]
                o = nn_dot(vt[c], pmat[c, :, lanes(rb)])
                ot[c, :, lanes(rb)] = o
                cols = pl.ds(pl.multiple_of(lax.rem(rb, 3) * RB, RB), RB)
                xo[0, c, rb // 3, :, cols] = (o / stat[c, 1, pl.ds(rb, 1), :]).astype(BF16)
                stat[c, 2, pl.ds(rb, 1), :] = jnp.sum(da_t.astype(F32) * o, axis=0, keepdims=True)
            return carry

        lax.fori_loop(0, 6 // UNROLL, block, 0)

    def stat_send(c, i):
        for k in range(1, XN):
            send(
                stat.at[c], statin.at[k - 1, c], st_s.at[i, k - 1], st_r.at[i, k - 1],
                dev(z, mod(x + k, XN), h),
            )

    c_right, c_left = x_to
    xg_forward(1)
    turn(x)
    probs_of(x)
    ag_step(1, 3)
    xg_wait(0, 0, 1)
    probs_of(c_left)
    ag_step(1, 4)
    xg_wait(0, 1, 1)
    probs_of(c_right)
    for d in range(2):
        xg_wait(0, d, 2)
    probs_of(x_opp)
    xg_wait(1, 0, 1)
    turn(c_left)
    xg_wait(1, 1, 1)
    turn(c_right)
    for d in range(2):
        xg_wait(1, d, 2)
    turn(x_opp)
    ag_end(1)

    def xr_copy(t, d, i):
        c, half = ((x_opp, d), (x_to[d], 1 - d), (x_to[d], d))[i]
        return pltpu.make_async_remote_copy(
            src_ref=xo.at[t, c, half], dst_ref=xin.at[t, d, i], send_sem=xr_s.at[t, d, i],
            recv_sem=xr_r.at[t, d, i], device_id=dev(z, x_to[d], h), device_id_type=MESH,
        )

    def xr_opp(t):
        for d in range(2):
            xr_copy(t, d, 0).start()

    def xr_near(t, d):
        xr_copy(t, d, 1).start()

    def row_of(ref, c, half):
        return jnp.concatenate([ref[c, pl.ds(half * 3 + r, 1), :] for r in range(3)], axis=1)

    def part_of(t, c, half):
        if t == 1:
            return xo[1, c, half].astype(F32)
        return ot[c, :, half * HALF : (half + 1) * HALF] * row_of(fac, c, half)

    def weighed(t, c, half, d, i):
        got = xin[t, d, i].astype(F32)
        return got * row_of(wgt.at[:, d], c, half) if t == 0 else got

    def xr_add(t):
        for d in range(2):
            arrived(xin.at[t, d, 0], xr_r.at[t, d, 0])
            both = part_of(t, x_to[d], d) + weighed(t, x_to[d], d, d, 0)
            xo[t, x_to[d], d] = both.astype(BF16)
            xr_copy(t, d, 2).start()

    def xr_end(t):
        for d in range(2):
            for i in (1, 2):
                arrived(xin.at[t, d, i], xr_r.at[t, d, i])

    def xr_rows(t, half):
        both = part_of(t, x, half) + xin[t, half, 2].astype(F32) + weighed(t, x, half, 1 - half, 1)
        return both.T

    for c in range(XN):
        outs_of(c)
        stat_send(c, c)
    xr_opp(0)
    xr_near(0, 0)
    xr_near(0, 1)

    def stat_wait(c):
        for k in range(1, XN):
            arrived(statin.at[k - 1, c], st_r.at[c, k - 1])

    def combine(c):
        stat_wait(c)
        tops = [stat[c, 0]] + [statin[k, c, 0] for k in range(XN - 1)]
        totals = [stat[c, 1]] + [statin[k, c, 1] for k in range(XN - 1)]
        dots = [stat[c, 2]] + [statin[k, c, 2] for k in range(XN - 1)]
        top = functools.reduce(jnp.maximum, tops)
        scales = [jnp.exp2((one - top) * (LOG2E * INV_ROOT)) for one in tops]
        total = sum(a * b for a, b in zip(scales, totals))
        delta = sum(a * b for a, b in zip(scales, dots)) / total
        own = scales[0] / total
        wgt[c, 0] = scales[1] * totals[1] / total
        wgt[c, 1] = scales[3] * totals[3] / total
        fac[c] = own
        dlt[c] = delta * own

        def block(rb, carry):
            f = fac[c, pl.ds(rb, 1), :]
            scaled = (dat[c, :, lanes(rb)].astype(F32) * f).astype(BF16)
            dat[c, :, lanes(rb)] = scaled
            dap[c, pl.ds(pl.multiple_of(rb * RB, RB), RB), :] = scaled.T
            return carry

        lax.fori_loop(0, 6, block, 0, unroll=True)

    def value_grads(c):
        for m in range(KEYS // MS):
            part = nn_dot(pmat[c, m * MS : (m + 1) * MS, :], dap[c])
            gv[c, m * MS // PART : (m + 1) * MS // PART] = part.astype(BF16).reshape(MS // PART, PART, HD)

    for c in range(XN):
        combine(c)
        value_grads(c)

    def own_part(t, slot):
        out = None
        for c in range(XN):
            entry = inv_ref[c, slot]
            block = grads[t][c, jnp.maximum(entry, 0)].astype(F32)
            block = jnp.where(entry >= 0, block, 0.0)
            out = block if out is None else out + block
        return out

    def rs_prep(t):
        def one(i, carry):
            for r in range(8):
                slot = i * 8 + r
                sums[t, slot] = own_part(t, slot)
            return carry

        lax.fori_loop(0, SLOTS // 8, one, 0)

    def rs_step(t, i):
        away = 5 - (i + 3) // 2
        for m in range(2):
            for d in range(2):
                zt = mod(z + away, ZN) if d == 0 else mod(z - away, ZN)
                sub = d if i % 2 == 0 else 1 - d
                first = zt * 8 + 4 * sub + 2 * m
                j = 2 * i + m
                if i < 2:
                    for sl in range(2):
                        rout[t, d, j, sl] = own_part(t, first + sl).astype(BF16)
                else:
                    arrived(rin.at[t, d, j - 4], rs_r.at[t, d, j - 4])
                    both = sums[t, pl.ds(first, 2)] + rin[t, d, j - 4].astype(F32)
                    rout[t, d, j] = both.astype(BF16)
                send(rout.at[t, d, j], rin.at[t, d, j], rs_s.at[t, d, j], rs_r.at[t, d, j], dev(z_to[d], x, h))

    def rs_end(t):
        for j in range(10, 14):
            for d in range(2):
                arrived(rin.at[t, d, j], rs_r.at[t, d, j])
        for sub in range(2):
            for m in range(2):
                first = 4 * sub + 2 * m
                part = sums[t, pl.ds(z * 8 + first, 2)]
                for d in range(2):
                    part = part + rin[t, d, (12 if sub == d else 10) + m].astype(F32)
                fin[t, first : first + 2] = part.astype(BF16).reshape(2, 2, 32, HD)

    def fa_copy(t, k, jj):
        target = mod(x + k, XN)
        return pltpu.make_async_remote_copy(
            src_ref=fin.at[t, pl.ds(2 * target, 2), jj], dst_ref=dkvin.at[t, h], send_sem=fa_s.at[t, 2 * k + jj],
            recv_sem=fa_r.at[t, h], device_id=dev(z, target, holder(k, jj)), device_id_type=MESH,
        )

    def fa_start(t):
        for k in range(XN):
            for jj in range(2):
                if k:
                    fa_copy(t, k, jj).start()
                    continue
                own = h == holder(0, jj)

                @pl.when(jnp.logical_not(own))
                def _():
                    fa_copy(t, k, jj).start()

                @pl.when(own)
                def _():
                    pltpu.make_async_copy(fin.at[t, pl.ds(2 * x, 2), jj], dkvin.at[t, h], fa_r.at[t, h]).start()

    def fa_end(t):
        for hh in range(HN):
            arrived(dkvin.at[t, hh], fa_r.at[t, hh])

    def key_grads(c):
        def block(i, carry):
            for r in range(UNROLL):
                rb = i * UNROLL + r
                da_t = dat[c, :, lanes(rb)]
                d_row = dlt[c, pl.ds(rb, 1), :]
                for m in range(KEYS // MS):
                    rows = slice(m * MS, (m + 1) * MS)
                    dp = nn_dot(vc[c, rows, :], da_t) - d_row
                    ds = pmat[c, rows, lanes(rb)].astype(F32) * dp
                    pmat[c, rows, lanes(rb)] = ds.astype(BF16)
            return carry

        lax.fori_loop(0, 6 // UNROLL, block, 0)
        for m in range(KEYS // MS):
            part = nn_dot(pmat[c, m * MS : (m + 1) * MS, :], qall[c].reshape(ROWS, HD)) * INV_ROOT
            gk[c, m * MS // PART : (m + 1) * MS // PART] = part.astype(BF16).reshape(MS // PART, PART, HD)

    def query_grads(c):
        def block(i, carry):
            for r in range(UNROLL):
                rb = i * UNROLL + r
                part = nn_dot(kt[c], pmat[c, :, lanes(rb)]) * INV_ROOT
                cols = pl.ds(pl.multiple_of(lax.rem(rb, 3) * RB, RB), RB)
                xo[1, c, rb // 3, :, cols] = part.astype(BF16)
            return carry

        lax.fori_loop(0, 6 // UNROLL, block, 0)

    rs_step(1, 0)
    rs_step(1, 1)
    rs_prep(1)
    key_grads(x_opp)
    xr_add(0)
    query_grads(x_opp)
    xr_opp(1)
    rs_step(1, 2)
    key_grads(c_right)
    rs_step(1, 3)
    key_grads(c_left)
    key_grads(x)
    rs_step(0, 0)
    rs_step(0, 1)
    rs_step(1, 4)
    rs_prep(0)
    query_grads(c_right)
    xr_near(1, 0)
    query_grads(c_left)
    xr_near(1, 1)
    rs_step(0, 2)
    rs_step(0, 3)
    rs_step(1, 5)
    query_grads(x)
    xr_add(1)
    rs_step(0, 4)
    rs_step(0, 5)
    rs_step(1, 6)
    xr_end(0)
    for half in range(2):
        rows = xr_rows(0, half)
        for gg in range(4):
            g = half * 4 + gg
            gated_ref[:, g * HD : (g + 1) * HD] = (rows[gg * TOK : (gg + 1) * TOK, :] * gate_row(g)).astype(BF16)
    outs[0].start()
    rs_step(0, 6)
    rs_end(1)
    fa_start(1)
    rs_end(0)
    fa_start(0)
    xr_end(1)
    for half in range(2):
        rows = xr_rows(1, half)
        for gg in range(4):
            g = half * 4 + gg
            dq_ref[:, g * HD : (g + 1) * HD] = rows[gg * TOK : (gg + 1) * TOK, :].astype(BF16)
    outs[1].start()
    for t in (1, 0):
        fa_end(t)
        for hh in range(HN):
            dkv_ref[:, :, t, hh * HD : (hh + 1) * HD] = dkvin[t, hh]
    outs[2].start()

    for copy in pending:
        copy.wait_send()
    for copy in outs:
        copy.wait()
    for t in range(2):
        for d in range(2):
            for i in range(3):
                xr_copy(t, d, i).wait_send()
    for t in range(2):
        for k in range(1, HN):
            a2a_copy(t, k).wait_send()

        @pl.when(jnp.logical_not(self_in))
        def _():
            a2a_copy(t, 0).wait_send()

        for k in range(XN):
            for jj in range(2):
                if k:
                    fa_copy(t, k, jj).wait_send()
                    continue

                @pl.when(h != holder(0, jj))
                def _():
                    fa_copy(t, k, jj).wait_send()


def hand_over(a, b, c, a_out, b_out, c_out, sem):
    copies = [
        pltpu.make_async_copy(src, dst, sem.at[i])
        for i, (src, dst) in enumerate(((a, a_out), (b, b_out), (c, c_out)))
    ]
    for copy in copies:
        copy.start()
    for copy in copies:
        copy.wait()


def on_device(queries, image_kv, gate_logit, d_gated, media_list, media_count, image_slot):
    smem = pl.BlockSpec(memory_space=pltpu.SMEM)
    anywhere = pl.BlockSpec(memory_space=pl.ANY)
    dma = pltpu.SemaphoreType.DMA
    results = pl.pallas_call(
        kernel,
        out_shape=(
            jax.ShapeDtypeStruct((TOK, HN * HD), BF16),
            jax.ShapeDtypeStruct((TOK, HN * HD), BF16),
            jax.ShapeDtypeStruct((2, 32, 2, HN * HD), BF16),
        ),
        in_specs=[smem] * 4 + [anywhere] * 3,
        out_specs=(anywhere,) * 3,
        scratch_shapes=[
            pltpu.VMEM((TOK, HN * HD), BF16),
            pltpu.VMEM((TOK, HN * HD), BF16),
            pltpu.VMEM((2, 32, 2, HN * HD), BF16),
            pltpu.VMEM((TOK, HN * HD), BF16),
            pltpu.VMEM((TOK, HN * HD), BF16),
            pltpu.VMEM((2, 32, 2, HN * HD), BF16),
            pltpu.VMEM((SLOTS, 2, 32, HD), BF16),
            pltpu.VMEM((SLOTS, 2, 32, HD), BF16),
            pltpu.VMEM((XN, 2, HALF, HD), BF16),
            pltpu.VMEM((XN, 2, HALF, HD), BF16),
            pltpu.VMEM((XN, HD, ROWS), BF16),
            pltpu.VMEM((XN, ROWS, HD), BF16),
            pltpu.VMEM((XN, KEYS, ROWS), BF16),
            pltpu.VMEM((XN, KEYS, HD), BF16),
            pltpu.VMEM((XN, HD, KEYS), BF16),
            pltpu.VMEM((XN, KEYS, HD), BF16),
            pltpu.VMEM((XN, HD, KEYS), BF16),
            pltpu.VMEM((UNROLL, KEYS, RB), F32),
            pltpu.VMEM((XN, HD, ROWS), F32),
            pltpu.VMEM((XN, 3, 8, RB), F32),
            pltpu.VMEM((XN - 1, XN, 3, 8, RB), F32),
            pltpu.VMEM((XN, 8, RB), F32),
            pltpu.VMEM((XN, 2, 8, RB), F32),
            pltpu.VMEM((XN, 8, RB), F32),
            pltpu.VMEM((2, XN, 2, HD, HALF), BF16),
            pltpu.VMEM((2, 2, 3, HD, HALF), BF16),
            pltpu.VMEM((XN, MEDIA, PART, HD), BF16),
            pltpu.VMEM((XN, MEDIA, PART, HD), BF16),
            pltpu.VMEM((2, 2, 14, 2, PART, HD), BF16),
            pltpu.VMEM((2, 2, 14, 2, PART, HD), BF16),
            pltpu.VMEM((2, SLOTS, PART, HD), F32),
            pltpu.VMEM((2, 8, 2, 32, HD), BF16),
            pltpu.VMEM((2, HN, 2, 32, HD), BF16),
            pltpu.VMEM((2, 32, 2 * HN * HD), BF16),
            pltpu.VMEM((8, HD), jnp.int32),
            pltpu.SMEM((8, HD), jnp.int32),
            dma,
            dma((2, 8)), dma((2, 8)),
            dma((2, 2, 7)), dma((2, 2, 7)),
            dma((2, 2, 3)), dma((2, 2, 3)),
            dma((4, 3)), dma((4, 3)),
            dma((2, 2, 3)), dma((2, 2, 3)),
            dma((2, 2, 14)), dma((2, 2, 14)),
            dma((2, 8)), dma((2, 8)),
            dma((3,)), dma((3,)),
        ],
        compiler_params=pltpu.CompilerParams(
            collective_id=0, has_side_effects=True, vmem_limit_bytes=60 * 1024 * 1024
        ),
        name="attend",
    )(media_list.T, media_count, image_slot, gate_logit, queries, d_gated, image_kv)
    return pl.pallas_call(
        hand_over,
        out_shape=tuple(jax.ShapeDtypeStruct(one.shape, one.dtype) for one in results),
        in_specs=[anywhere] * 3,
        out_specs=(anywhere,) * 3,
        scratch_shapes=[dma((3,))],
        compiler_params=pltpu.CompilerParams(vmem_limit_bytes=60 * 1024 * 1024),
        name="hand_over",
    )(*results)


def solution(mesh):
    return jax.shard_map(
        on_device,
        mesh=mesh,
        in_specs=(
            P("seq", "head"),
            P("seq", "head", None, None),
            P("head"),
            P("seq", "head"),
            P(),
            P(),
            P(),
        ),
        out_specs=(P("seq", "head"), P("seq", "head"), P("seq", "head", None, None)),
        check_vma=False,
    )
```

```python
import functools

import jax
import jax.numpy as jnp
from jax import lax
from jax.experimental import pallas as pl
from jax.experimental.pallas import tpu as pltpu
from jax.sharding import PartitionSpec as P

MESH = pl.DeviceIdType.MESH
HD = 128
XN = 4
ZN = 8
HN = 8
MEDIA = 16
LOWEST = 12
TOK = 192
ROWS = 1536
HALF = 768
RB = 256
KEYS = 1024
PART = 64
SLOTS = 64
MS = 256
UNROLL = 6
LOG2E = 1.4426950408889634
INV_ROOT = HD ** (-0.5)
F32 = jnp.float32
BF16 = jnp.bfloat16


def mod(value, n):
    return lax.rem(value + n, n)


def nt_dot(a, b):
    return lax.dot_general(a, b, (((1,), (1,)), ((), ())), preferred_element_type=F32)


def nn_dot(a, b):
    return jnp.dot(a, b, preferred_element_type=F32)


def kernel(
    media_ref, counts_ref, place_ref, gate_ref, q_hbm, dg_hbm, kv_hbm,
    gated_hbm, dq_hbm, dkv_hbm,
    q_ref, dg_ref, kv_ref, gated_ref, dq_ref, dkv_ref,
    kall, vall, qall, daall, dat, dap, pmat, kc, kt, vc, vt, sbuf, ot,
    stat, statin, fac, wgt, dlt, xo, xin, gk, gv, rout, rin, sums, fin, dkvin, kvlin, inv_v, inv_ref, inv_sem,
    a2a_s, a2a_r, ag_s, ag_r, xg_s, xg_r, st_s, st_r, xr_s, xr_r, rs_s, rs_r, fa_s, fa_r, in_sem, out_sem,
):
    seq = lax.axis_index("seq")
    h = lax.axis_index("head")
    z = seq // XN
    x = lax.rem(seq, XN)
    hq = h // 2
    hp = lax.rem(h, 2)
    kv_all = (kall, vall)
    xg_all = (qall, daall)
    grads = (gk, gv)
    pending = []

    def dev(zz, xx, hh):
        return (zz * XN + xx, hh)

    def send(src, dst, ssem, rsem, device):
        copy = pltpu.make_async_remote_copy(
            src_ref=src, dst_ref=dst, send_sem=ssem, recv_sem=rsem, device_id=device, device_id_type=MESH
        )
        copy.start()
        pending.append(copy)

    def arrived(ref, sem):
        pltpu.make_async_copy(ref, ref, sem).wait()

    z_to = (mod(z + 1, ZN), mod(z - 1, ZN))
    x_to = (mod(x + 1, XN), mod(x - 1, XN))
    x_opp = mod(x + 2, XN)
    x_part = lax.rem(x + hq + 2 * hp, XN)
    self_in = x_part == x

    def holder(k, jj):
        return 2 * ((2 * XN - k - 2 * jj) % XN) + jj

    ins = [
        pltpu.make_async_copy(src, dst, in_sem.at[i])
        for i, (src, dst) in enumerate(((kv_hbm, kv_ref), (q_hbm, q_ref), (dg_hbm, dg_ref)))
    ]
    outs = [
        pltpu.make_async_copy(src, dst, out_sem.at[i])
        for i, (src, dst) in enumerate(((gated_ref, gated_hbm), (dq_ref, dq_hbm), (dkv_ref, dkv_hbm)))
    ]
    for copy in ins:
        copy.start()

    barrier = pltpu.get_barrier_semaphore()

    def greet(device):
        pl.semaphore_signal(barrier, inc=1, device_id=device, device_id_type=MESH)

    for k in range(1, HN):
        greet(dev(z, x_part, mod(h + k, HN)))
    for k in range(1, XN):
        greet(dev(z, mod(x + k, XN), h))
        for jj in range(2):
            greet(dev(z, mod(x + k, XN), holder(k, jj)))
    for jj in range(2):

        @pl.when(h != holder(0, jj))
        def _():
            greet(dev(z, x, holder(0, jj)))

    @pl.when(jnp.logical_not(self_in))
    def _():
        greet(dev(z, x_part, h))

    for d in range(2):
        greet(dev(z_to[d], x, h))
    ins[0].wait()
    for i in range(2):
        for t in range(2):
            kvlin[i, :, t * HN * HD : (t + 1) * HN * HD] = kv_ref[i, :, t, :]
    ins[1].wait()
    for g in range(8):
        rows = q_ref[:, g * HD : (g + 1) * HD]
        qall[x, g // 4, (g % 4) * TOK : (g % 4 + 1) * TOK, :] = rows

    def gate_row(g):
        return jnp.tanh(jnp.full((1, HD), gate_ref[g], F32))

    ins[2].wait()
    for g in range(8):
        rows = dg_ref[:, g * HD : (g + 1) * HD].astype(F32) * gate_row(g)
        daall[x, g // 4, (g % 4) * TOK : (g % 4 + 1) * TOK, :] = rows.astype(BF16)
    stat[...] = jnp.ones_like(stat)

    lane = lax.broadcasted_iota(jnp.int32, (1, HD), 1)
    inv_v[...] = jnp.full((8, HD), -1, jnp.int32)
    for c in range(XN):
        found = jnp.full((1, HD), -1, jnp.int32)
        for j in range(MEDIA):
            slot = place_ref[media_ref[j, z * XN + c]]
            slot = jnp.where(j < counts_ref[z * XN + c], slot, -1)
            found = jnp.where(lane == slot, j, found)
        inv_v[c : c + 1, :] = found
    inv_copy = pltpu.make_async_copy(inv_v, inv_ref, inv_sem)

    pl.semaphore_wait(barrier, jnp.where(self_in, 19, 21))

    def kv_lanes(t, head):
        return kvlin.at[:, :, pl.ds(pl.multiple_of((t * HN + head) * HD, HD), HD)]

    def a2a_copy(t, k):
        target = mod(h + k, HN)
        mine = kall if t == 0 else vall
        dst = mine.at[pl.ds(2 * seq, 2), hp]
        return pltpu.make_async_remote_copy(
            src_ref=kv_lanes(t, target), dst_ref=dst, send_sem=a2a_s.at[t, k],
            recv_sem=a2a_r.at[t, 2 * x + hp], device_id=dev(z, x_part, target), device_id_type=MESH,
        )

    for t in range(2):
        for k in range(1, HN):
            a2a_copy(t, k).start()

        @pl.when(jnp.logical_not(self_in))
        def _():
            a2a_copy(t, 0).start()

        @pl.when(self_in)
        def _():
            pltpu.make_async_copy(
                kv_lanes(t, h), kv_all[t].at[pl.ds(2 * seq, 2), hp], a2a_r.at[t, 2 * x + hp]
            ).start()

    def a2a_wait(t, sub):
        for xx in (2 * sub, 2 * sub + 1):
            for jj in range(2):
                arrived(kv_all[t].at[pl.ds(2 * (z * XN + xx), 2), jj], a2a_r.at[t, 2 * xx + jj])

    def xg_ref(t, c, half):
        return xg_all[t].at[c, half]

    def xg_first(t):
        for pos in range(2):
            for d in range(2):
                half = d if pos == 0 else 1 - d
                ref = xg_ref(t, x, half)
                send(ref, ref, xg_s.at[t, d, pos], xg_r.at[t, d, pos], dev(z, x_to[d], h))

    def xg_wait(t, d, pos):
        c = x_opp if pos == 2 else x_to[1 - d]
        half = 1 - d if pos == 1 else d
        arrived(xg_ref(t, c, half), xg_r.at[t, d, pos])

    def xg_forward(t):
        for d in range(2):
            xg_wait(t, d, 0)
            ref = xg_ref(t, x_to[1 - d], d)
            send(ref, ref, xg_s.at[t, d, 2], xg_r.at[t, d, 2], dev(z, x_to[d], h))

    def ag_ref(t, zz, d, pos):
        sub = d if pos == 0 else 1 - d
        return kv_all[t].at[pl.ds(zz * 8 + 4 * sub, 4)]

    def ag_send(t, k, pos, ways=(0, 1)):
        for d in ways:
            zz = mod(z - (k - 1), ZN) if d == 0 else mod(z + (k - 1), ZN)
            ref = ag_ref(t, zz, d, pos)
            i = 2 * (k - 1) + pos
            send(ref, ref, ag_s.at[t, d, i], ag_r.at[t, d, i], dev(z_to[d], x, h))

    def ag_wait(t, k, pos):
        for d in range(2):
            zz = mod(z - k, ZN) if d == 0 else mod(z + k, ZN)
            arrived(ag_ref(t, zz, d, pos), ag_r.at[t, d, 2 * (k - 1) + pos])

    def ag_pass(t, k, pos):
        ag_wait(t, k - 1, pos)
        ag_send(t, k, pos)

    def ag_step(t, k):
        for pos in range(1 if k == 4 else 2):
            ag_pass(t, k, pos)

    def ag_end(t):
        ag_wait(t, 3, 1)
        ag_wait(t, 4, 0)

    xg_first(0)
    inv_copy.start()

    for t in range(2):
        a2a_wait(t, 0)
        ag_send(t, 1, 0, (0,))
        a2a_wait(t, 1)
        ag_send(t, 1, 0, (1,))
        if t == 0:
            ag_send(0, 1, 1)
    xg_forward(0)
    xg_first(1)
    ag_step(0, 2)
    ag_send(1, 1, 1)
    ag_step(0, 3)
    ag_pass(1, 2, 0)
    ag_step(0, 4)
    ag_pass(1, 2, 1)
    inv_copy.wait()
    ag_end(0)

    def pick(src, dst, dst_t, c):
        segment = z * XN + c

        for j in range(MEDIA):
            slot = place_ref[media_ref[j, segment]]
            dst[c, j * PART : (j + 1) * PART, :] = src[slot].reshape(PART, HD)
        for ch in range(KEYS // 256):
            block = dst[c, ch * 256 : (ch + 1) * 256, :]
            dst_t[c, :, ch * 256 : (ch + 1) * 256] = block.T

    def lanes(rb):
        return pl.ds(pl.multiple_of(rb * RB, RB), RB)

    def probs_of(c):
        pick(kall, kc, kt, c)
        live = (counts_ref[z * XN + c] - LOWEST) * PART

        def block(i, carry):
            for r in range(UNROLL):
                rb = i * UNROLL + r
                q_rows = qall[c, rb // 3, pl.ds(pl.multiple_of(lax.rem(rb, 3) * RB, RB), RB), :]
                top = None
                for m in range(KEYS // MS):
                    rows = slice(m * MS, (m + 1) * MS)
                    s = nt_dot(kc[c, rows, :], q_rows)
                    if m == KEYS // MS - 1:
                        first = LOWEST * PART - m * MS
                        row_ids = lax.broadcasted_iota(jnp.int32, (KEYS - LOWEST * PART, RB), 0)
                        last = jnp.where(row_ids < live, s[first:], -1e30)
                        s = jnp.concatenate([s[:first], last], axis=0) if first else last
                    sbuf[r, rows, :] = s
                    here = jnp.max(s, axis=0, keepdims=True)
                    top = here if top is None else jnp.maximum(top, here)
                total = jnp.zeros((1, RB), F32)
                for ch in range(4):
                    rows = slice(ch * 256, (ch + 1) * 256)
                    p = jnp.exp2((sbuf[r, rows, :] - top) * (LOG2E * INV_ROOT))
                    total = total + jnp.sum(p, axis=0, keepdims=True)
                    pmat[c, rows, lanes(rb)] = p.astype(BF16)
                stat[c, 0, pl.ds(rb, 1), :] = top
                stat[c, 1, pl.ds(rb, 1), :] = total
            return carry

        lax.fori_loop(0, 6 // UNROLL, block, 0)

    def turn(c):
        for half in range(2):
            for r in range(3):
                rb = half * 3 + r
                dat[c, :, rb * RB : (rb + 1) * RB] = daall[c, half, r * RB : (r + 1) * RB, :].T

    def outs_of(c):
        pick(vall, vc, vt, c)

        def block(i, carry):
            for r in range(UNROLL):
                rb = i * UNROLL + r
                da_t = dat[c, :, lanes(rb)]
                o = nn_dot(vt[c], pmat[c, :, lanes(rb)])
                ot[c, :, lanes(rb)] = o
                cols = pl.ds(pl.multiple_of(lax.rem(rb, 3) * RB, RB), RB)
                xo[0, c, rb // 3, :, cols] = (o / stat[c, 1, pl.ds(rb, 1), :]).astype(BF16)
                stat[c, 2, pl.ds(rb, 1), :] = jnp.sum(da_t.astype(F32) * o, axis=0, keepdims=True)
            return carry

        lax.fori_loop(0, 6 // UNROLL, block, 0)

    def stat_send(c, i):
        for k in range(1, XN):
            send(
                stat.at[c], statin.at[k - 1, c], st_s.at[i, k - 1], st_r.at[i, k - 1],
                dev(z, mod(x + k, XN), h),
            )

    c_right, c_left = x_to
    xg_forward(1)
    turn(x)
    probs_of(x)
    ag_step(1, 3)
    xg_wait(0, 0, 1)
    probs_of(c_left)
    ag_step(1, 4)
    xg_wait(0, 1, 1)
    probs_of(c_right)
    for d in range(2):
        xg_wait(0, d, 2)
    probs_of(x_opp)
    xg_wait(1, 0, 1)
    turn(c_left)
    xg_wait(1, 1, 1)
    turn(c_right)
    for d in range(2):
        xg_wait(1, d, 2)
    turn(x_opp)
    ag_end(1)

    def xr_copy(t, d, i):
        c, half = ((x_opp, d), (x_to[d], 1 - d), (x_to[d], d))[i]
        return pltpu.make_async_remote_copy(
            src_ref=xo.at[t, c, half], dst_ref=xin.at[t, d, i], send_sem=xr_s.at[t, d, i],
            recv_sem=xr_r.at[t, d, i], device_id=dev(z, x_to[d], h), device_id_type=MESH,
        )

    def xr_opp(t):
        for d in range(2):
            xr_copy(t, d, 0).start()

    def xr_near(t, d):
        xr_copy(t, d, 1).start()

    def row_of(ref, c, half):
        return jnp.concatenate([ref[c, pl.ds(half * 3 + r, 1), :] for r in range(3)], axis=1)

    def part_of(t, c, half):
        if t == 1:
            return xo[1, c, half].astype(F32)
        return ot[c, :, half * HALF : (half + 1) * HALF] * row_of(fac, c, half)

    def weighed(t, c, half, d, i):
        got = xin[t, d, i].astype(F32)
        return got * row_of(wgt.at[:, d], c, half) if t == 0 else got

    def xr_add(t):
        for d in range(2):
            arrived(xin.at[t, d, 0], xr_r.at[t, d, 0])
            both = part_of(t, x_to[d], d) + weighed(t, x_to[d], d, d, 0)
            xo[t, x_to[d], d] = both.astype(BF16)
            xr_copy(t, d, 2).start()

    def xr_end(t):
        for d in range(2):
            for i in (1, 2):
                arrived(xin.at[t, d, i], xr_r.at[t, d, i])

    def xr_rows(t, half):
        both = part_of(t, x, half) + xin[t, half, 2].astype(F32) + weighed(t, x, half, 1 - half, 1)
        return both.T

    for c in range(XN):
        outs_of(c)
        stat_send(c, c)
    xr_opp(0)
    xr_near(0, 0)
    xr_near(0, 1)

    def stat_wait(c):
        for k in range(1, XN):
            arrived(statin.at[k - 1, c], st_r.at[c, k - 1])

    def combine(c):
        stat_wait(c)
        tops = [stat[c, 0]] + [statin[k, c, 0] for k in range(XN - 1)]
        totals = [stat[c, 1]] + [statin[k, c, 1] for k in range(XN - 1)]
        dots = [stat[c, 2]] + [statin[k, c, 2] for k in range(XN - 1)]
        top = functools.reduce(jnp.maximum, tops)
        scales = [jnp.exp2((one - top) * (LOG2E * INV_ROOT)) for one in tops]
        total = sum(a * b for a, b in zip(scales, totals))
        delta = sum(a * b for a, b in zip(scales, dots)) / total
        own = scales[0] / total
        wgt[c, 0] = scales[1] * totals[1] / total
        wgt[c, 1] = scales[3] * totals[3] / total
        fac[c] = own
        dlt[c] = delta * own

        def block(rb, carry):
            f = fac[c, pl.ds(rb, 1), :]
            scaled = (dat[c, :, lanes(rb)].astype(F32) * f).astype(BF16)
            dat[c, :, lanes(rb)] = scaled
            dap[c, pl.ds(pl.multiple_of(rb * RB, RB), RB), :] = scaled.T
            return carry

        lax.fori_loop(0, 6, block, 0, unroll=True)

    def value_grads(c):
        for m in range(KEYS // MS):
            part = nn_dot(pmat[c, m * MS : (m + 1) * MS, :], dap[c])
            gv[c, m * MS // PART : (m + 1) * MS // PART] = part.astype(BF16).reshape(MS // PART, PART, HD)

    for c in range(XN):
        combine(c)
        value_grads(c)

    def own_part(t, slot):
        out = None
        for c in range(XN):
            entry = inv_ref[c, slot]
            block = grads[t][c, jnp.maximum(entry, 0)].astype(F32)
            block = jnp.where(entry >= 0, block, 0.0)
            out = block if out is None else out + block
        return out

    def rs_prep(t):
        def one(i, carry):
            for r in range(8):
                slot = i * 8 + r
                sums[t, slot] = own_part(t, slot)
            return carry

        lax.fori_loop(0, SLOTS // 8, one, 0)

    def rs_step(t, i):
        away = 5 - (i + 3) // 2
        for m in range(2):
            for d in range(2):
                zt = mod(z + away, ZN) if d == 0 else mod(z - away, ZN)
                sub = d if i % 2 == 0 else 1 - d
                first = zt * 8 + 4 * sub + 2 * m
                j = 2 * i + m
                if i < 2:
                    for sl in range(2):
                        rout[t, d, j, sl] = own_part(t, first + sl).astype(BF16)
                else:
                    arrived(rin.at[t, d, j - 4], rs_r.at[t, d, j - 4])
                    both = sums[t, pl.ds(first, 2)] + rin[t, d, j - 4].astype(F32)
                    rout[t, d, j] = both.astype(BF16)
                send(rout.at[t, d, j], rin.at[t, d, j], rs_s.at[t, d, j], rs_r.at[t, d, j], dev(z_to[d], x, h))

    def rs_end(t):
        for j in range(10, 14):
            for d in range(2):
                arrived(rin.at[t, d, j], rs_r.at[t, d, j])
        for sub in range(2):
            for m in range(2):
                first = 4 * sub + 2 * m
                part = sums[t, pl.ds(z * 8 + first, 2)]
                for d in range(2):
                    part = part + rin[t, d, (12 if sub == d else 10) + m].astype(F32)
                fin[t, first : first + 2] = part.astype(BF16).reshape(2, 2, 32, HD)

    def fa_copy(t, k, jj):
        target = mod(x + k, XN)
        return pltpu.make_async_remote_copy(
            src_ref=fin.at[t, pl.ds(2 * target, 2), jj], dst_ref=dkvin.at[t, h], send_sem=fa_s.at[t, 2 * k + jj],
            recv_sem=fa_r.at[t, h], device_id=dev(z, target, holder(k, jj)), device_id_type=MESH,
        )

    def fa_start(t):
        for k in range(XN):
            for jj in range(2):
                if k:
                    fa_copy(t, k, jj).start()
                    continue
                own = h == holder(0, jj)

                @pl.when(jnp.logical_not(own))
                def _():
                    fa_copy(t, k, jj).start()

                @pl.when(own)
                def _():
                    pltpu.make_async_copy(fin.at[t, pl.ds(2 * x, 2), jj], dkvin.at[t, h], fa_r.at[t, h]).start()

    def fa_end(t):
        for hh in range(HN):
            arrived(dkvin.at[t, hh], fa_r.at[t, hh])

    def key_grads(c):
        def block(i, carry):
            for r in range(UNROLL):
                rb = i * UNROLL + r
                da_t = dat[c, :, lanes(rb)]
                d_row = dlt[c, pl.ds(rb, 1), :]
                for m in range(KEYS // MS):
                    rows = slice(m * MS, (m + 1) * MS)
                    dp = nn_dot(vc[c, rows, :], da_t) - d_row
                    ds = pmat[c, rows, lanes(rb)].astype(F32) * dp
                    pmat[c, rows, lanes(rb)] = ds.astype(BF16)
            return carry

        lax.fori_loop(0, 6 // UNROLL, block, 0)
        for m in range(KEYS // MS):
            part = nn_dot(pmat[c, m * MS : (m + 1) * MS, :], qall[c].reshape(ROWS, HD)) * INV_ROOT
            gk[c, m * MS // PART : (m + 1) * MS // PART] = part.astype(BF16).reshape(MS // PART, PART, HD)

    def query_grads(c):
        def block(i, carry):
            for r in range(UNROLL):
                rb = i * UNROLL + r
                part = nn_dot(kt[c], pmat[c, :, lanes(rb)]) * INV_ROOT
                cols = pl.ds(pl.multiple_of(lax.rem(rb, 3) * RB, RB), RB)
                xo[1, c, rb // 3, :, cols] = part.astype(BF16)
            return carry

        lax.fori_loop(0, 6 // UNROLL, block, 0)

    rs_step(1, 0)
    rs_step(1, 1)
    rs_prep(1)
    key_grads(x_opp)
    xr_add(0)
    query_grads(x_opp)
    xr_opp(1)
    rs_step(1, 2)
    key_grads(c_right)
    rs_step(1, 3)
    key_grads(c_left)
    key_grads(x)
    rs_step(0, 0)
    rs_step(0, 1)
    rs_step(1, 4)
    rs_prep(0)
    query_grads(c_right)
    xr_near(1, 0)
    query_grads(c_left)
    xr_near(1, 1)
    rs_step(0, 2)
    rs_step(0, 3)
    rs_step(1, 5)
    query_grads(x)
    xr_add(1)
    rs_step(0, 4)
    rs_step(0, 5)
    rs_step(1, 6)
    xr_end(0)
    for half in range(2):
        rows = xr_rows(0, half)
        for gg in range(4):
            g = half * 4 + gg
            gated_ref[:, g * HD : (g + 1) * HD] = (rows[gg * TOK : (gg + 1) * TOK, :] * gate_row(g)).astype(BF16)
    outs[0].start()
    rs_step(0, 6)
    rs_end(1)
    fa_start(1)
    rs_end(0)
    fa_start(0)
    xr_end(1)
    for half in range(2):
        rows = xr_rows(1, half)
        for gg in range(4):
            g = half * 4 + gg
            dq_ref[:, g * HD : (g + 1) * HD] = rows[gg * TOK : (gg + 1) * TOK, :].astype(BF16)
    outs[1].start()
    for t in (1, 0):
        fa_end(t)
        for hh in range(HN):
            dkv_ref[:, :, t, hh * HD : (hh + 1) * HD] = dkvin[t, hh]
    outs[2].start()

    for copy in pending:
        copy.wait_send()
    for copy in outs:
        copy.wait()
    for t in range(2):
        for d in range(2):
            for i in range(3):
                xr_copy(t, d, i).wait_send()
    for t in range(2):
        for k in range(1, HN):
            a2a_copy(t, k).wait_send()

        @pl.when(jnp.logical_not(self_in))
        def _():
            a2a_copy(t, 0).wait_send()

        for k in range(XN):
            for jj in range(2):
                if k:
                    fa_copy(t, k, jj).wait_send()
                    continue

                @pl.when(h != holder(0, jj))
                def _():
                    fa_copy(t, k, jj).wait_send()


def hand_over(a, b, c, a_out, b_out, c_out, a_mid, b_mid, c_mid, in_sem, out_sem):
    ins = [
        pltpu.make_async_copy(src, dst, in_sem.at[i])
        for i, (src, dst) in enumerate(((a, a_mid), (b, b_mid), (c, c_mid)))
    ]
    outs = [
        pltpu.make_async_copy(src, dst, out_sem.at[i])
        for i, (src, dst) in enumerate(((a_mid, a_out), (b_mid, b_out), (c_mid, c_out)))
    ]
    for copy in ins:
        copy.start()
    for one, two in zip(ins, outs):
        one.wait()
        two.start()
    for copy in outs:
        copy.wait()


def on_device(queries, image_kv, gate_logit, d_gated, media_list, media_count, image_slot):
    smem = pl.BlockSpec(memory_space=pltpu.SMEM)
    anywhere = pl.BlockSpec(memory_space=pl.ANY)
    dma = pltpu.SemaphoreType.DMA
    results = pl.pallas_call(
        kernel,
        out_shape=(
            jax.ShapeDtypeStruct((TOK, HN * HD), BF16),
            jax.ShapeDtypeStruct((TOK, HN * HD), BF16),
            jax.ShapeDtypeStruct((2, 32, 2, HN * HD), BF16),
        ),
        in_specs=[smem] * 4 + [anywhere] * 3,
        out_specs=(anywhere,) * 3,
        scratch_shapes=[
            pltpu.VMEM((TOK, HN * HD), BF16),
            pltpu.VMEM((TOK, HN * HD), BF16),
            pltpu.VMEM((2, 32, 2, HN * HD), BF16),
            pltpu.VMEM((TOK, HN * HD), BF16),
            pltpu.VMEM((TOK, HN * HD), BF16),
            pltpu.VMEM((2, 32, 2, HN * HD), BF16),
            pltpu.VMEM((SLOTS, 2, 32, HD), BF16),
            pltpu.VMEM((SLOTS, 2, 32, HD), BF16),
            pltpu.VMEM((XN, 2, HALF, HD), BF16),
            pltpu.VMEM((XN, 2, HALF, HD), BF16),
            pltpu.VMEM((XN, HD, ROWS), BF16),
            pltpu.VMEM((XN, ROWS, HD), BF16),
            pltpu.VMEM((XN, KEYS, ROWS), BF16),
            pltpu.VMEM((XN, KEYS, HD), BF16),
            pltpu.VMEM((XN, HD, KEYS), BF16),
            pltpu.VMEM((XN, KEYS, HD), BF16),
            pltpu.VMEM((XN, HD, KEYS), BF16),
            pltpu.VMEM((UNROLL, KEYS, RB), F32),
            pltpu.VMEM((XN, HD, ROWS), F32),
            pltpu.VMEM((XN, 3, 8, RB), F32),
            pltpu.VMEM((XN - 1, XN, 3, 8, RB), F32),
            pltpu.VMEM((XN, 8, RB), F32),
            pltpu.VMEM((XN, 2, 8, RB), F32),
            pltpu.VMEM((XN, 8, RB), F32),
            pltpu.VMEM((2, XN, 2, HD, HALF), BF16),
            pltpu.VMEM((2, 2, 3, HD, HALF), BF16),
            pltpu.VMEM((XN, MEDIA, PART, HD), BF16),
            pltpu.VMEM((XN, MEDIA, PART, HD), BF16),
            pltpu.VMEM((2, 2, 14, 2, PART, HD), BF16),
            pltpu.VMEM((2, 2, 14, 2, PART, HD), BF16),
            pltpu.VMEM((2, SLOTS, PART, HD), F32),
            pltpu.VMEM((2, 8, 2, 32, HD), BF16),
            pltpu.VMEM((2, HN, 2, 32, HD), BF16),
            pltpu.VMEM((2, 32, 2 * HN * HD), BF16),
            pltpu.VMEM((8, HD), jnp.int32),
            pltpu.SMEM((8, HD), jnp.int32),
            dma,
            dma((2, 8)), dma((2, 8)),
            dma((2, 2, 7)), dma((2, 2, 7)),
            dma((2, 2, 3)), dma((2, 2, 3)),
            dma((4, 3)), dma((4, 3)),
            dma((2, 2, 3)), dma((2, 2, 3)),
            dma((2, 2, 14)), dma((2, 2, 14)),
            dma((2, 8)), dma((2, 8)),
            dma((3,)), dma((3,)),
        ],
        compiler_params=pltpu.CompilerParams(
            collective_id=0, has_side_effects=True, vmem_limit_bytes=60 * 1024 * 1024
        ),
        name="attend",
    )(media_list.T, media_count, image_slot, gate_logit, queries, d_gated, image_kv)
    return pl.pallas_call(
        hand_over,
        out_shape=tuple(jax.ShapeDtypeStruct(one.shape, one.dtype) for one in results),
        in_specs=[anywhere] * 3,
        out_specs=(anywhere,) * 3,
        scratch_shapes=[pltpu.VMEM(one.shape, one.dtype) for one in results] + [dma((3,)), dma((3,))],
        compiler_params=pltpu.CompilerParams(vmem_limit_bytes=60 * 1024 * 1024),
        name="hand_over",
    )(*results)


def solution(mesh):
    return jax.shard_map(
        on_device,
        mesh=mesh,
        in_specs=(
            P("seq", "head"),
            P("seq", "head", None, None),
            P("head"),
            P("seq", "head"),
            P(),
            P(),
            P(),
        ),
        out_specs=(P("seq", "head"), P("seq", "head"), P("seq", "head", None, None)),
        check_vma=False,
    )
```
